32 devices in a mesh: gx: 16 (over z, x, core), gz: 2 (over y).
Axes of the slice: x: 2, y: 2, z: 4, core: 2. Of those that a mesh axis runs over, the one named last changes fastest.
Arguments:
- velocity: float32 [2, 2, 1, 4096, 2048], P(None, None, None, 'gx', 'gz'), may hold values from -6 to 6
- previous: float32 [2, 2, 1, 4096, 2048], P(None, None, None, 'gx', 'gz'), may hold values from -12 to 12
- base_flow: float32 [1], replicated, may hold values from -1 to 1
Outputs:
- velocity_next: float32 [2, 2, 1, 4096, 2048], P(None, None, None, 'gx', 'gz')
- nonlinear: float32 [2, 2, 1, 4096, 2048], P(None, None, None, 'gx', 'gz')
The draws below stay inside these ranges and needn't reach their ends.
All inputs are finite; a program needn't handle non-finite values.
Results may differ from the reference program's by a relative error of at most 0.00014.
Values sent between devices are 32-bit elements; how exact they have to be, the bound alone decides.
A program may use at most 128 MiB of HBM per device.

```python
import math
import jax
import jax.numpy as jnp
from jax import lax

NX = 4096
NZ = 2048
Y_WIN = 1


def block_levels(stream_key, shape, pieces, least, high):
    gain, own = 1.0, jax.random.fold_in(stream_key, 6)
    for axis_at, shards_of in pieces:
        draws = jnp.exp(jax.random.uniform(jax.random.fold_in(own, axis_at), (shards_of,), jnp.float32, least / len(pieces), high / len(pieces)))
        gain = gain * jnp.repeat(draws, shape[axis_at] // shards_of).reshape([-1 if axis == axis_at else 1 for axis in range(len(shape))])
    return gain


def normal_values(key, dims, spread, limit, split=(), kind=jnp.bfloat16):
    loudness = block_levels(key, dims, split, -0.22, 0.18) if split else 1.0
    result = jax.random.normal(key, dims, jnp.float32) * spread * loudness
    return jnp.minimum(jnp.maximum(result, -limit), limit).astype(kind)


def setup_inputs(seed: int = 0) -> dict:
    seeds = jax.random.split(jax.random.key(seed), 4)
    return {
        "velocity": normal_values(seeds[0], (2, 2, Y_WIN, NX, NZ), 1.0, 6.0, ((3, 16), (4, 2)), jnp.float32),
        "previous": normal_values(seeds[1], (2, 2, Y_WIN, NX, NZ), 2.0, 12.0, ((3, 16), (4, 2)), jnp.float32),
        "base_flow": jnp.clip(jax.random.uniform(seeds[2], (Y_WIN,), jnp.float32, -1.0, 1.0), -1.0, 1.0),
    }


VISCOSITY = 0.05
TIME_STEP = 0.2
GAMMA_NEW = 8.0 / 15.0
ZETA_OLD = -17.0 / 60.0


def signed_modes(extent):
    numbers = jnp.arange(extent, dtype=jnp.int32)
    return jnp.where(2 * numbers < extent, numbers, numbers - extent)


def one_plane(arguments):
    plane_velocity, plane_previous, plane_base = arguments
    spectra = lax.complex(plane_velocity[:, 0], plane_velocity[:, 1])
    fields = jnp.real(jnp.fft.ifft2(spectra, axes=(1, 2), norm="ortho"))
    products = jnp.stack([fields[0] * fields[0], fields[0] * fields[1], fields[1] * fields[1]])
    product_spectra = jnp.fft.fft2(products, axes=(1, 2), norm="ortho")
    prod_real = jnp.real(product_spectra)
    prod_imag = jnp.imag(product_spectra)
    modes_along = signed_modes(NX)
    modes_across = signed_modes(NZ)
    wave_along = (modes_along.astype(jnp.float32) * (2.0 * math.pi / NX))[:, None]
    wave_across = (modes_across.astype(jnp.float32) * (2.0 * math.pi / NZ))[None, :]
    keep = jnp.logical_and((3 * jnp.abs(modes_along) < NX)[:, None], (3 * jnp.abs(modes_across) < NZ)[None, :]).astype(jnp.float32)
    shear = plane_base * wave_along
    first_real = keep * (wave_along * prod_imag[0] + wave_across * prod_imag[1]) + shear * plane_velocity[0, 1]
    first_imag = -keep * (wave_along * prod_real[0] + wave_across * prod_real[1]) - shear * plane_velocity[0, 0]
    second_real = keep * (wave_along * prod_imag[1] + wave_across * prod_imag[2]) + shear * plane_velocity[1, 1]
    second_imag = -keep * (wave_along * prod_real[1] + wave_across * prod_real[2]) - shear * plane_velocity[1, 0]
    nonlinear = jnp.stack([jnp.stack([first_real, first_imag]), jnp.stack([second_real, second_imag])])
    damping = jnp.exp(-VISCOSITY * (wave_along * wave_along + wave_across * wave_across))
    advanced = damping * (plane_velocity + TIME_STEP * (GAMMA_NEW * nonlinear + ZETA_OLD * plane_previous))
    return advanced, nonlinear


def reference(velocity, previous, base_flow):
    advanced, nonlinear = lax.map(one_plane, (jnp.moveaxis(velocity, 2, 0), jnp.moveaxis(previous, 2, 0), base_flow))
    return jnp.moveaxis(advanced, 0, 2), jnp.moveaxis(nonlinear, 0, 2)
```

```python
import functools
import math

import jax
import jax.numpy as jnp
import numpy as np
from jax import lax
from jax.experimental import pallas as pl
from jax.experimental.pallas import tpu as pltpu
from jax.sharding import PartitionSpec as P

NX = 4096
NZ = 2048


TWO_PI = 2.0 * math.pi
VISCOSITY = 0.05
TIME_STEP = 0.2
GAMMA_NEW = 8.0 / 15.0
ZETA_OLD = -17.0 / 60.0


def partner_2(x, axis, distance):
    return lax.ppermute(x, axis, [(i, i ^ 1 << distance) for i in range(lax.axis_size(axis))])


def exact_einsum(pattern, left_array, right_array):
    return jnp.einsum(
        pattern,
        left_array,
        right_array,
        precision=lax.Precision.HIGHEST,
        preferred_element_type=jnp.float32,
    )


def phase_table(left_ints, right_ints, period, direction):
    phase_angle = (
        direction * TWO_PI / period * (left_ints * right_ints % period).astype(jnp.float32)
    )
    return (jnp.cos(phase_angle), jnp.sin(phase_angle))


def complex_apply(value_real, value_imag, table_real, table_imag, pattern):
    out_real = exact_einsum(pattern, value_real, table_real) - exact_einsum(
        pattern, value_imag, table_imag
    )
    out_imag = exact_einsum(pattern, value_real, table_imag) + exact_einsum(
        pattern, value_imag, table_real
    )
    return (out_real, out_imag)


def residue_of(position, levels):
    reversed_bits = jnp.zeros((), jnp.int32)
    for level in range(levels):
        reversed_bits = reversed_bits + ((position >> level & 1) << levels - 1 - level)
    return reversed_bits


def section_twiddle(position, half_span):
    phase_angle = TWO_PI / (2 * half_span) * (position % half_span).astype(jnp.float32)
    return (jnp.cos(phase_angle), jnp.sin(phase_angle))


def spread_butterfly(values):
    position = lax.axis_index("gx")
    levels = lax.axis_size("gx").bit_length() - 1
    for level in reversed(range(levels)):
        half_span = 1 << level
        partner = partner_2(values, "gx", level)
        upper_half = position >> level & 1 == 1
        cosine, sine_part = section_twiddle(position, half_span)
        difference = partner - values
        rotated = jnp.stack(
            [
                difference[:, 0] * cosine - difference[:, 1] * sine_part,
                difference[:, 0] * sine_part + difference[:, 1] * cosine,
            ],
            axis=1,
        )
        values = jnp.where(upper_half, rotated, values + partner)
    return (values, residue_of(position, levels))


def gather_butterfly(values):
    position = lax.axis_index("gx")
    levels = lax.axis_size("gx").bit_length() - 1
    for level in range(levels):
        half_span = 1 << level
        partner = partner_2(values, "gx", level)
        upper_half = position >> level & 1 == 1
        cosine, sine_part = section_twiddle(position, half_span)
        upper_item = jnp.where(upper_half, values, partner)
        lower_item = jnp.where(upper_half, partner, values)
        turned = jnp.stack(
            [
                upper_item[:, 0] * cosine + upper_item[:, 1] * sine_part,
                upper_item[:, 1] * cosine - upper_item[:, 0] * sine_part,
            ],
            axis=1,
        )
        values = jnp.where(upper_half, lower_item - turned, lower_item + turned)
    return values


def axial_table(residue, mode_count, device_count):
    numbers = jnp.arange(mode_count, dtype=jnp.int32)
    points = residue + device_count * numbers
    cosine, sine_part = phase_table(points[:, None], numbers[None, :], NX, 1.0)
    norm_scale = 1.0 / math.sqrt(NX)
    return (cosine * norm_scale, sine_part * norm_scale)


def span_table(groups, span_size):
    residues = jnp.arange(groups, dtype=jnp.int32)[:, None, None]
    grid_rows = jnp.arange(span_size, dtype=jnp.int32)[None, :, None]
    mode_cols = jnp.arange(span_size, dtype=jnp.int32)[None, None, :]
    cosine, sine_part = phase_table(mode_cols, residues + groups * grid_rows, NZ, 1.0)
    norm_scale = 1.0 / math.sqrt(NZ)
    return (cosine * norm_scale, sine_part * norm_scale)


def spanwise_work(received):
    fields, pair_size, planes, row_count, extent = received.shape
    groups = lax.axis_size("gz")
    span_size = extent // groups
    blocks = received.reshape(fields, pair_size, planes, row_count, groups, span_size)
    group_ids = jnp.arange(groups, dtype=jnp.int32)
    mix_real, mix_imag = phase_table(group_ids[:, None], group_ids[None, :], groups, 1.0)
    section_real, section_imag = complex_apply(
        blocks[:, 0], blocks[:, 1], mix_real, mix_imag, "fylcj,rc->fylrj"
    )
    table_real, table_imag = span_table(groups, span_size)
    physical = exact_einsum("fylrj,rtj->fylrt", section_real, table_real) - exact_einsum(
        "fylrj,rtj->fylrt", section_imag, table_imag
    )
    products = jnp.stack(
        [physical[0] * physical[0], physical[0] * physical[1], physical[1] * physical[1]]
    )
    back_real = exact_einsum("pylrt,rtj->pylrj", products, table_real)
    back_imag = -exact_einsum("pylrt,rtj->pylrj", products, table_imag)
    out_real, out_imag = complex_apply(back_real, back_imag, mix_real, -mix_imag, "pylrj,cr->pylcj")
    spectra = jnp.stack([out_real, out_imag], axis=1)
    return spectra.reshape(3, pair_size, planes, row_count, extent)


def span_round(values, work):
    span_spectra = work(lax.all_to_all(values, "gz", split_axis=3, concat_axis=4, tiled=True))
    return lax.all_to_all(span_spectra, "gz", split_axis=4, concat_axis=3, tiled=True)


def signed_block(start, mode_count, extent):
    numbers = start + jnp.arange(mode_count, dtype=jnp.int32)
    return jnp.where(2 * numbers < extent, numbers, numbers - extent)


def local(velocity, previous, base_flow):
    mode_count = velocity.shape[3]
    span_size = velocity.shape[4]
    device_count = lax.axis_size("gx")
    spread, residue = spread_butterfly(velocity)
    table_real, table_imag = axial_table(residue, mode_count, device_count)
    along_real, along_imag = complex_apply(
        spread[:, 0], spread[:, 1], table_real, table_imag, "fymq,sm->fysq"
    )
    physical_along = jnp.stack([along_real, along_imag], axis=1)
    returned = span_round(physical_along, spanwise_work)
    local_real, local_imag = complex_apply(
        returned[:, 0], returned[:, 1], table_real.T, -table_imag.T, "fysq,ms->fymq"
    )
    local_spectra = jnp.stack([local_real, local_imag], axis=1)
    product_spectra = gather_butterfly(local_spectra)
    modes_along = signed_block(lax.axis_index("gx") * mode_count, mode_count, NX)
    modes_across = signed_block(lax.axis_index("gz") * span_size, span_size, NZ)
    wave_along = (modes_along.astype(jnp.float32) * (TWO_PI / NX))[:, None]
    wave_across = (modes_across.astype(jnp.float32) * (TWO_PI / NZ))[None, :]
    keep = jnp.logical_and(
        (3 * jnp.abs(modes_along) < NX)[:, None], (3 * jnp.abs(modes_across) < NZ)[None, :]
    ).astype(jnp.float32)
    shear = base_flow[:, None, None] * wave_along[None]
    prod_real = product_spectra[:, 0]
    prod_imag = product_spectra[:, 1]
    first_real = (
        keep * (wave_along * prod_imag[0] + wave_across * prod_imag[1]) + shear * velocity[0, 1]
    )
    first_imag = (
        -keep * (wave_along * prod_real[0] + wave_across * prod_real[1]) - shear * velocity[0, 0]
    )
    second_real = (
        keep * (wave_along * prod_imag[1] + wave_across * prod_imag[2]) + shear * velocity[1, 1]
    )
    second_imag = (
        -keep * (wave_along * prod_real[1] + wave_across * prod_real[2]) - shear * velocity[1, 0]
    )
    nonlinear = jnp.stack(
        [jnp.stack([first_real, first_imag]), jnp.stack([second_real, second_imag])]
    )
    damping = jnp.exp(-VISCOSITY * (wave_along * wave_along + wave_across * wave_across))
    advanced = damping * (velocity + TIME_STEP * (GAMMA_NEW * nonlinear + ZETA_OLD * previous))
    return (advanced, nonlinear)


XR = 16
XS = NX // XR
ZR = 8
ZS = NZ // ZR
LOW = (0, 1, 2)
HIGH = (5, 6, 7)
MIB = 1 << 20
CHUNKS = 4
UNIT = 8
UNITS = 11
SIDE = 16 * UNITS
SKIP = NX // UNIT - 2 * SIDE
SPANS = 4
LARGE = 3


def split_table(table):
    high = table.astype(np.float32).astype(jnp.bfloat16)
    low = (table - high.astype(np.float64)).astype(np.float32).astype(jnp.bfloat16)
    return high, low


def z_table():
    r = np.arange(ZR)[:, None, None]
    b = np.arange(ZS)[None, :, None]
    s = np.arange(ZS)[None, None, :]
    angle = TWO_PI / NZ * ((b * (r + ZR * s)) % NZ)
    cos, sin = np.cos(angle) / math.sqrt(NZ), np.sin(angle) / math.sqrt(NZ)
    return split_table(np.concatenate([cos, sin], axis=2))


def x_table():
    r = np.arange(XR)[:, None, None]
    s = np.arange(XS)[None, :, None]
    m = np.arange(XS)[None, None, :]
    angle = TWO_PI / NX * ((m * (r + XR * s)) % NX)
    cos, sin = np.cos(angle) / math.sqrt(NX), np.sin(angle) / math.sqrt(NX)
    return split_table(np.concatenate([cos, -sin], axis=2))


def turn(value, numerator, size, sign):
    re, im = value
    numerator = numerator % size
    if numerator == 0:
        return re, im
    if 4 * numerator == size:
        return (-im, re) if sign > 0 else (im, -re)
    if 8 * numerator == size:
        h = math.sqrt(0.5)
        return ((re - im) * h, (re + im) * h) if sign > 0 else ((re + im) * h, (im - re) * h)
    if 8 * numerator == 3 * size:
        h = math.sqrt(0.5)
        return ((-re - im) * h, (re - im) * h) if sign > 0 else ((im - re) * h, (-re - im) * h)
    c = math.cos(TWO_PI * numerator / size)
    s = sign * math.sin(TWO_PI * numerator / size)
    return re * c - im * s, re * s + im * c


def small_dft(values, sign):
    size = len(values)
    if size == 1:
        return values
    even = small_dft(values[0::2], sign)
    odd = small_dft(values[1::2], sign)
    half = size // 2
    out = [None] * size
    for i in range(half):
        re, im = turn(odd[i], i, size, sign)
        out[i] = (even[i][0] + re, even[i][1] + im)
        out[i + half] = (even[i][0] - re, even[i][1] - im)
    return out


def parts_of(value):
    high = value.astype(jnp.bfloat16)
    return high, (value - high.astype(jnp.float32)).astype(jnp.bfloat16)


def dot3(a_high, a_low, b_high, b_low, dims):
    def dot(a, b):
        return lax.dot_general(a, b, (dims, ((), ())), preferred_element_type=jnp.float32)

    return dot(a_high, b_high) + (dot(a_high, b_low) + dot(a_low, b_high))


def merge(first, second, low_half):
    return (
        jnp.where(low_half, first, pltpu.roll(second, 64, 1)),
        jnp.where(low_half, pltpu.roll(first, 64, 1), second),
    )


def z_inverse(first, own_ref, other_ref, row, rows, high_ref, low_ref, out_ref, th_ref, tl_ref):
    step = 16
    for c in range(2):
        def body(i, carry):
            at = pl.multiple_of(i * step, step)
            for lane in range(0, ZS, 128):
                values = [None] * ZR
                for a in range(ZR // 2):
                    to = (pl.ds(row + at, step), pl.ds(a * ZS + lane, 128))
                    own = [own_ref[(c, p) + to] for p in range(2)]
                    other = [other_ref[(c, p) + to] for p in range(2)]
                    values[a] = tuple(jnp.where(first, x, y) for x, y in zip(own, other))
                    values[a + ZR // 2] = tuple(jnp.where(first, y, x) for x, y in zip(own, other))
                for r, pair in enumerate(small_dft(values, 1)):
                    for p in range(2):
                        high, low = parts_of(pair[p])
                        line = pl.ds((2 * p + c) * rows + at, step)
                        th_ref[r, line, pl.ds(lane, 128)] = high
                        tl_ref[r, line, pl.ds(lane, 128)] = low
            return carry
        lax.fori_loop(0, rows // step, body, 0)

    def group(r, carry):
        both = dot3(th_ref[r], tl_ref[r], high_ref[r], low_ref[r], ((1,), (0,)))
        real, imag = both[: 2 * rows], both[2 * rows :]
        done = jnp.concatenate(
            [real[:, :ZS] - imag[:, ZS:], real[:, ZS:] + imag[:, :ZS]], axis=1
        )
        low_half = lax.broadcasted_iota(jnp.int32, (rows, 128), 1) < 64
        for p in range(2):
            for t in range(2):
                at = p * ZS + t * 128
                even, odd = merge(done[:rows, at : at + 128], done[rows:, at : at + 128], low_half)
                out_ref[r * 4 + 2 * t, p, pl.ds(row, rows), :] = even
                out_ref[r * 4 + 2 * t + 1, p, pl.ds(row, rows), :] = odd
        return carry
    lax.fori_loop(0, ZR, group, 0)


def x_spread(v_ref, row, rows, th_ref, tl_ref):
    step = 16
    half = XS // 2
    for r in range(2):
        def body(i, carry):
            at = pl.multiple_of(row + i * step, step)
            values = [
                tuple(v_ref[2 * g + r, p, pl.ds(at, step), :] for p in range(2)) for g in range(XR)
            ]
            for res, pair in enumerate(small_dft(values, 1)):
                for p in range(2):
                    high, low = parts_of(pair[p])
                    th_ref[res, pl.ds(p * XS + r * half + at, step), :] = high
                    tl_ref[res, pl.ds(p * XS + r * half + at, step), :] = low
            return carry
        lax.fori_loop(0, rows // step, body, 0)


def x_products(ih_ref, il_ref, fh_ref, fl_ref, th_ref, tl_ref, u_ref):
    def residue(res, carry):
        field = dot3(ih_ref[res], il_ref[res], th_ref[res], tl_ref[res], ((1,), (0,)))
        swapped = pltpu.roll(field, 64, 1)
        products = jnp.concatenate([field * field, field * swapped], axis=1)
        high, low = parts_of(products)
        u_ref[res] = dot3(fh_ref[res], fl_ref[res], high, low, ((1,), (0,)))
        return carry
    lax.fori_loop(0, XR, residue, 0)


def x_gather(u_ref, out_ref):
    low_half = lax.broadcasted_iota(jnp.int32, (UNIT, 128), 1) < 64
    per = XS // UNIT
    split = SIDE % per
    for first, last in ((0, split), (split, per)):
        def back(i, carry):
            at = pl.multiple_of(i * UNIT, UNIT)
            for h in range(2):
                values = [
                    tuple(
                        u_ref[res, pl.ds(p * XS + at, UNIT), pl.ds(h * 128, 128)]
                        for p in range(2)
                    )
                    for res in range(XR)
                ]
                for g, (re, im) in enumerate(small_dft(values, -1)):
                    if g * per + first < SIDE:
                        flat = g * per + i
                    elif g * per + first >= SIDE + SKIP:
                        flat = g * per + i - SKIP
                    else:
                        continue
                    worker = flat // UNITS
                    line = pl.ds(pl.multiple_of((flat - worker * UNITS) * UNIT, UNIT), UNIT)
                    if h == 0:
                        out_ref[worker, 0, line, :] = re
                        out_ref[worker, 1, line, :] = im
                    else:
                        out_ref[worker, 2, line, :] = jnp.where(low_half, re, im)
            return carry
        lax.fori_loop(first, last, back, 0)


def unit_of(flat):
    return jnp.where(flat < SIDE, flat, flat + SKIP)


def z_forward(first_unit, row, rows, v_ref, high_ref, low_ref, out_ref, w_ref):
    low_half = lax.broadcasted_iota(jnp.int32, (rows, 128), 1) < 64

    def group(r, carry):
        real, imag, mixed = (
            [v_ref[r * 4 + j, x, pl.ds(row, rows), :] for j in range(4)] for x in range(3)
        )
        p0r, p2r, p0i, p2i, p1r, p1i = [], [], [], [], [], []
        for source, first, second in ((real, p0r, p2r), (imag, p0i, p2i), (mixed, p1r, p1i)):
            for t in range(2):
                a, b = merge(source[2 * t], source[2 * t + 1], low_half)
                first.append(a)
                second.append(b)
        lines = jnp.concatenate(
            [jnp.concatenate(x, axis=1) for x in (p0r, p1r, p2r, p0i, p1i, p2i)], axis=0
        )
        high, low = parts_of(lines)
        cos, sin = (
            dot3(high, low, high_ref[r, :, at : at + ZS], low_ref[r, :, at : at + ZS], ((1,), (1,)))
            for at in (0, ZS)
        )
        w_ref[r, : 3 * rows, :ZS] = cos[: 3 * rows] + sin[3 * rows :]
        w_ref[r, : 3 * rows, ZS:] = cos[3 * rows :] - sin[: 3 * rows]
        return carry
    lax.fori_loop(0, ZR, group, 0)

    def body(i, carry):
        at = pl.multiple_of(i * UNIT, UNIT)
        along = unit_of(first_unit + i) * UNIT + lax.broadcasted_iota(jnp.int32, (UNIT, 128), 0)
        along = jnp.where(2 * along < NX, along, along - NX)
        wave_along = along.astype(jnp.float32) * (TWO_PI / NX)
        keep_along = 3 * jnp.abs(along) < NX
        for lane in range(0, ZS, 128):
            spectra = []
            for j in range(3):
                values = [
                    tuple(
                        w_ref[r, pl.ds(j * rows + at, UNIT), pl.ds(p * ZS + lane, 128)]
                        for p in range(2)
                    )
                    for r in range(ZR)
                ]
                spectra.append(small_dft(values, -1))
            for half, groups in enumerate((LOW, HIGH)):
                for place, a in enumerate(groups):
                    start = a * ZS + lane - (NZ if half else 0)
                    mode = start + lax.broadcasted_iota(jnp.int32, (UNIT, 128), 1)
                    wave_across = mode.astype(jnp.float32) * (TWO_PI / NZ)
                    keep = jnp.logical_and(3 * jnp.abs(mode) < NZ, keep_along)
                    (ar, ai), (br, bi), (cr, ci) = (x[a] for x in spectra)
                    terms = [
                        jnp.where(keep, wave_along * ai + wave_across * bi, 0.0),
                        jnp.where(keep, -(wave_along * ar + wave_across * br), 0.0),
                        jnp.where(keep, wave_along * bi + wave_across * ci, 0.0),
                        jnp.where(keep, -(wave_along * br + wave_across * cr), 0.0),
                    ]
                    for x in range(4):
                        out_ref[half, x, pl.ds(row + at, UNIT), pl.ds(place * ZS + lane, 128)] = terms[x]
        return carry
    lax.fori_loop(0, rows // UNIT, body, 0)


def substep_kernel(
    velocity_ref, zh_hbm, zl_hbm, ih_hbm, il_hbm, fh_hbm, fl_hbm,
    term_ref,
    own_ref, other_ref, zh_ref, zl_ref, ih_ref, il_ref, fh_ref, fl_ref,
    zth_ref, ztl_ref, out_ref, in_ref, th_ref, tl_ref, u_ref, back_ref, work_ref, w_ref, res_ref,
    table_sems, own_sems, swap_send, swap_recv, out_send, out_recv, back_send, back_recv,
    res_send, res_recv,
):
    gx, gz = lax.axis_index("gx"), lax.axis_index("gz")
    count = 2 * XR
    me = 2 * gx + gz
    half = own_ref.shape[2]
    rows = half // CHUNKS

    def device(t):
        return (t // 2, lax.rem(t, 2))

    tables = [
        pltpu.make_async_copy(src, dst, table_sems.at[n])
        for n, (src, dst) in enumerate(
            (
                (zh_hbm, zh_ref),
                (zl_hbm, zl_ref),
                (ih_hbm, ih_ref),
                (il_hbm, il_ref),
                (fh_hbm, fh_ref),
                (fl_hbm, fl_ref),
            )
        )
    ]

    def load_own(c):
        return pltpu.make_async_copy(
            velocity_ref.at[:, :, pl.ds(pl.multiple_of(gz * half + c * rows, rows), rows), :],
            own_ref.at[:, :, pl.ds(pl.multiple_of(c * rows, rows), rows), :],
            own_sems.at[c],
        )

    def swap(c):
        return pltpu.make_async_remote_copy(
            src_ref=velocity_ref.at[
                :, :, pl.ds(pl.multiple_of((1 - gz) * half + c * rows, rows), rows), :
            ],
            dst_ref=other_ref.at[:, :, pl.ds(pl.multiple_of(c * rows, rows), rows), :],
            send_sem=swap_send.at[c],
            recv_sem=swap_recv.at[c],
            device_id=(gx, 1 - gz),
            device_id_type=pl.DeviceIdType.MESH,
        )

    for c in range(CHUNKS):
        load_own(c).start()
    for table in tables:
        table.start()

    barrier = pltpu.get_barrier_semaphore()

    def greet(i, carry):
        pl.semaphore_signal(
            barrier,
            inc=1,
            device_id=device(lax.rem(me + i, count)),
            device_id_type=pl.DeviceIdType.MESH,
        )
        return carry

    lax.fori_loop(1, count, greet, 0)
    pl.semaphore_wait(barrier, count - 1)
    for c in range(CHUNKS):
        swap(c).start()

    def ship(src_ref, dst_ref, sends, recvs, c, at, length):
        span = pl.ds(at, length)

        def copy(i):
            t = lax.rem(me + i, count)
            return pltpu.make_async_remote_copy(
                src_ref=src_ref.at[t, :, span, :],
                dst_ref=dst_ref.at[me, :, span, :],
                send_sem=sends.at[c, i],
                recv_sem=recvs.at[c, i],
                device_id=device(t),
                device_id_type=pl.DeviceIdType.MESH,
            )

        local = pltpu.make_async_copy(
            src_ref.at[me, :, span, :], dst_ref.at[me, :, span, :], recvs.at[c, 0]
        )
        return copy, local

    def ship_start(*args):
        copy, local = ship(*args)

        def start(i, carry):
            copy(i).start()
            return carry

        lax.fori_loop(1, count, start, 0)
        local.start()

    def ship_arrive(*args):
        copy, local = ship(*args)

        def wait(i, carry):
            copy(i).wait_recv()
            return carry

        lax.fori_loop(1, count, wait, 0)
        local.wait()

    def ship_leave(*args):
        copy, _ = ship(*args)

        def wait(i, carry):
            copy(i).wait_send()
            return carry

        lax.fori_loop(1, count, wait, 0)

    def spread_args(c):
        return out_ref, in_ref, out_send, out_recv, c, pl.multiple_of(c * rows, rows), rows

    tables[0].wait()
    tables[1].wait()

    def inverse(c, carry):
        load_own(c).wait()
        swap(c).wait_recv()
        z_inverse(
            gz == 0, own_ref, other_ref, pl.multiple_of(c * rows, rows), rows,
            zh_ref, zl_ref, out_ref, zth_ref, ztl_ref,
        )
        ship_start(*spread_args(c))
        return carry

    lax.fori_loop(0, CHUNKS, inverse, 0)

    def spread(c, carry):
        ship_arrive(*spread_args(c))
        x_spread(in_ref, pl.multiple_of(c * rows, rows), rows, th_ref, tl_ref)
        return carry

    lax.fori_loop(0, CHUNKS, spread, 0)
    for table in tables[2:]:
        table.wait()
    x_products(ih_ref, il_ref, fh_ref, fl_ref, th_ref, tl_ref, u_ref)
    x_gather(u_ref, back_ref)

    def back_args(c, units):
        at = pl.multiple_of(c * LARGE * UNIT, UNIT)
        return back_ref, work_ref, back_send, back_recv, c, at, units * UNIT

    last = UNITS - LARGE * (SPANS - 1)

    def over_spans(step):
        def one(c, carry):
            step(c, LARGE)
            return carry

        lax.fori_loop(0, SPANS - 1, one, 0)
        step(SPANS - 1, last)

    over_spans(lambda c, units: ship_start(*back_args(c, units)))

    per = XS // UNIT

    def result(u, side):
        unit = unit_of(UNITS * me + u)
        owner = unit // per
        slot = unit - owner * per
        src = res_ref.at[side, :, pl.ds(pl.multiple_of(u * UNIT, UNIT), UNIT), :]
        dst = term_ref.at[:, pl.ds(pl.multiple_of(slot * UNIT, UNIT), UNIT), :]
        here = jnp.logical_and(owner == gx, side == gz)
        remote = pltpu.make_async_remote_copy(
            src_ref=src,
            dst_ref=dst,
            send_sem=res_send.at[side, u],
            recv_sem=res_recv.at[slot],
            device_id=(owner, side),
            device_id_type=pl.DeviceIdType.MESH,
        )
        return here, remote, pltpu.make_async_copy(src, dst, res_recv.at[slot])

    def forward(c, units):
        ship_arrive(*back_args(c, units))
        unit = c * LARGE
        z_forward(
            UNITS * me + unit, pl.multiple_of(unit * UNIT, UNIT), units * UNIT,
            work_ref, zh_ref, zl_ref, res_ref, w_ref,
        )

        def send(n, carry):
            for side in range(2):
                here, remote, local = result(unit + n, side)

                @pl.when(here)
                def _():
                    local.start()

                @pl.when(jnp.logical_not(here))
                def _():
                    remote.start()
            return carry

        lax.fori_loop(0, units, send, 0)

    over_spans(forward)

    def sent(u, carry):
        for side in range(2):
            here, remote, _ = result(u, side)

            @pl.when(jnp.logical_not(here))
            def _():
                remote.wait_send()
        return carry

    def got(s, carry):
        unit = gx * per + s

        @pl.when(jnp.logical_or(unit < SIDE, unit >= SIDE + SKIP))
        def _():
            pltpu.make_async_copy(
                res_ref.at[0, :, pl.ds(0, UNIT), :],
                term_ref.at[:, pl.ds(pl.multiple_of(s * UNIT, UNIT), UNIT), :],
                res_recv.at[s],
            ).wait()
        return carry

    lax.fori_loop(0, per, got, 0)
    lax.fori_loop(0, UNITS, sent, 0)

    def swap_left(c, carry):
        swap(c).wait_send()
        ship_leave(*spread_args(c))
        return carry

    lax.fori_loop(0, CHUNKS, swap_left, 0)
    over_spans(lambda c, units: ship_leave(*back_args(c, units)))


def advance_kernel(place_ref, base_ref, v_ref, old_ref, term_ref, along_ref, across_ref, next_ref, non_ref):
    rows, extent = v_ref.shape[2:]
    unit = place_ref[0] * (XS // UNIT) + pl.program_id(0) * (rows // UNIT)
    lower = place_ref[1] == 0
    active = jnp.logical_or(unit < SIDE, unit >= SIDE + SKIP)
    wave_along = along_ref[:, :1]
    wave_across = across_ref[:1, :]
    damping = jnp.exp(-VISCOSITY * (wave_along * wave_along + wave_across * wave_across))
    shear = base_ref[0] * wave_along
    empty = jnp.zeros((rows, extent - term_ref.shape[2]), jnp.float32)
    for c in range(2):
        for p in range(2):
            term = jnp.where(active, term_ref[2 * c + p], 0.0)
            term = jnp.where(
                lower,
                jnp.concatenate([term, empty], axis=1),
                jnp.concatenate([empty, term], axis=1),
            )
            other = shear * v_ref[c, 1 - p]
            result = term + other if p == 0 else term - other
            non_ref[c, p] = result
            next_ref[c, p] = damping * (
                v_ref[c, p] + TIME_STEP * (GAMMA_NEW * result + ZETA_OLD * old_ref[c, p])
            )


def lines_local(velocity, previous, base_flow):
    velocity, previous = velocity[:, :, 0], previous[:, :, 0]
    mode_count, extent = velocity.shape[2:]
    half = mode_count // 2
    rows = half // CHUNKS
    gx, gz = lax.axis_index("gx"), lax.axis_index("gz")
    f32, bf16 = jnp.float32, jnp.bfloat16
    zh, zl = z_table()
    xh, xl = x_table()
    fh, fl = np.swapaxes(xh, 1, 2), np.swapaxes(xl, 1, 2)
    active = len(LOW) * ZS
    count = 2 * XR
    dma = pltpu.SemaphoreType.DMA

    term = pl.pallas_call(
        substep_kernel,
        out_shape=jax.ShapeDtypeStruct((4, mode_count, active), f32),
        in_specs=[pl.BlockSpec(memory_space=pl.ANY)] * 7,
        out_specs=pl.BlockSpec(memory_space=pl.ANY),
        scratch_shapes=[
            pltpu.VMEM((2, 2, half, extent), f32),
            pltpu.VMEM((2, 2, half, extent), f32),
            pltpu.VMEM(zh.shape, bf16),
            pltpu.VMEM(zl.shape, bf16),
            pltpu.VMEM(xh.shape, bf16),
            pltpu.VMEM(xl.shape, bf16),
            pltpu.VMEM(fh.shape, bf16),
            pltpu.VMEM(fl.shape, bf16),
            pltpu.VMEM((ZR, 4 * rows, ZS), bf16),
            pltpu.VMEM((ZR, 4 * rows, ZS), bf16),
            pltpu.VMEM((count, 2, half, 128), f32),
            pltpu.VMEM((count, 2, half, 128), f32),
            pltpu.VMEM((XR, 2 * XS, 128), bf16),
            pltpu.VMEM((XR, 2 * XS, 128), bf16),
            pltpu.VMEM((XR, 2 * XS, 256), f32),
            pltpu.VMEM((count, 3, UNITS * UNIT, 128), f32),
            pltpu.VMEM((count, 3, UNITS * UNIT, 128), f32),
            pltpu.VMEM((ZR, 3 * LARGE * UNIT, 2 * ZS), f32),
            pltpu.VMEM((2, 4, UNITS * UNIT, active), f32),
            dma((6,)),
            dma((CHUNKS,)),
            dma((CHUNKS,)),
            dma((CHUNKS,)),
            dma((CHUNKS, count)),
            dma((CHUNKS, count)),
            dma((SPANS, count)),
            dma((SPANS, count)),
            dma((2, UNITS)),
            dma((XS // UNIT,)),
        ],
        compiler_params=pltpu.CompilerParams(
            collective_id=1, has_side_effects=True, vmem_limit_bytes=60 * MIB
        ),
        cost_estimate=pl.CostEstimate(
            flops=10**10, bytes_accessed=64 * velocity.size, transcendentals=0
        ),
        name="substep",
    )(velocity, zh, zl, xh, xl, fh, fl)

    def modes(start, count, size):
        numbers = start + jnp.arange(count, dtype=jnp.int32)
        return jnp.where(2 * numbers < size, numbers, numbers - size)

    along = modes(gx * mode_count, mode_count, NX).astype(f32) * (TWO_PI / NX)
    across = modes(gz * extent, extent, NZ).astype(f32) * (TWO_PI / NZ)
    scalar = pl.BlockSpec(memory_space=pltpu.SMEM)
    block = 64
    field = pl.BlockSpec((2, 2, block, extent), lambda i: (0, 0, i, 0))
    advanced, nonlinear = pl.pallas_call(
        advance_kernel,
        grid=(mode_count // block,),
        out_shape=[jax.ShapeDtypeStruct(velocity.shape, f32)] * 2,
        in_specs=[
            scalar,
            scalar,
            field,
            field,
            pl.BlockSpec((4, block, active), lambda i: (0, i, 0)),
            pl.BlockSpec((block, 128), lambda i: (i, 0)),
            pl.BlockSpec((8, extent), lambda i: (0, 0)),
        ],
        out_specs=[field, field],
        compiler_params=pltpu.CompilerParams(vmem_limit_bytes=48 * MIB),
        name="advance",
    )(
        jnp.stack([gx, gz]).astype(jnp.int32),
        base_flow,
        velocity,
        previous,
        term,
        jnp.broadcast_to(along[:, None], (mode_count, 128)),
        jnp.broadcast_to(across[None], (8, extent)),
    )
    return advanced[:, :, None], nonlinear[:, :, None]


def solution(mesh):
    in_specs = (P(None, None, None, "gx", "gz"), P(None, None, None, "gx", "gz"), P())
    out_specs = (P(None, None, None, "gx", "gz"), P(None, None, None, "gx", "gz"))
    fits = mesh.shape["gx"] == XR and mesh.shape["gz"] == 2
    work = lines_local if fits else local
    return jax.shard_map(work, mesh=mesh, in_specs=in_specs, out_specs=out_specs, check_vma=False)
```

```python
import functools
import math

import jax
import jax.numpy as jnp
import numpy as np
from jax import lax
from jax.experimental import pallas as pl
from jax.experimental.pallas import tpu as pltpu
from jax.sharding import PartitionSpec as P

NX = 4096
NZ = 2048


TWO_PI = 2.0 * math.pi
VISCOSITY = 0.05
TIME_STEP = 0.2
GAMMA_NEW = 8.0 / 15.0
ZETA_OLD = -17.0 / 60.0


def partner_2(x, axis, distance):
    return lax.ppermute(x, axis, [(i, i ^ 1 << distance) for i in range(lax.axis_size(axis))])


def exact_einsum(pattern, left_array, right_array):
    return jnp.einsum(
        pattern,
        left_array,
        right_array,
        precision=lax.Precision.HIGHEST,
        preferred_element_type=jnp.float32,
    )


def phase_table(left_ints, right_ints, period, direction):
    phase_angle = (
        direction * TWO_PI / period * (left_ints * right_ints % period).astype(jnp.float32)
    )
    return (jnp.cos(phase_angle), jnp.sin(phase_angle))


def complex_apply(value_real, value_imag, table_real, table_imag, pattern):
    out_real = exact_einsum(pattern, value_real, table_real) - exact_einsum(
        pattern, value_imag, table_imag
    )
    out_imag = exact_einsum(pattern, value_real, table_imag) + exact_einsum(
        pattern, value_imag, table_real
    )
    return (out_real, out_imag)


def residue_of(position, levels):
    reversed_bits = jnp.zeros((), jnp.int32)
    for level in range(levels):
        reversed_bits = reversed_bits + ((position >> level & 1) << levels - 1 - level)
    return reversed_bits


def section_twiddle(position, half_span):
    phase_angle = TWO_PI / (2 * half_span) * (position % half_span).astype(jnp.float32)
    return (jnp.cos(phase_angle), jnp.sin(phase_angle))


def spread_butterfly(values):
    position = lax.axis_index("gx")
    levels = lax.axis_size("gx").bit_length() - 1
    for level in reversed(range(levels)):
        half_span = 1 << level
        partner = partner_2(values, "gx", level)
        upper_half = position >> level & 1 == 1
        cosine, sine_part = section_twiddle(position, half_span)
        difference = partner - values
        rotated = jnp.stack(
            [
                difference[:, 0] * cosine - difference[:, 1] * sine_part,
                difference[:, 0] * sine_part + difference[:, 1] * cosine,
            ],
            axis=1,
        )
        values = jnp.where(upper_half, rotated, values + partner)
    return (values, residue_of(position, levels))


def gather_butterfly(values):
    position = lax.axis_index("gx")
    levels = lax.axis_size("gx").bit_length() - 1
    for level in range(levels):
        half_span = 1 << level
        partner = partner_2(values, "gx", level)
        upper_half = position >> level & 1 == 1
        cosine, sine_part = section_twiddle(position, half_span)
        upper_item = jnp.where(upper_half, values, partner)
        lower_item = jnp.where(upper_half, partner, values)
        turned = jnp.stack(
            [
                upper_item[:, 0] * cosine + upper_item[:, 1] * sine_part,
                upper_item[:, 1] * cosine - upper_item[:, 0] * sine_part,
            ],
            axis=1,
        )
        values = jnp.where(upper_half, lower_item - turned, lower_item + turned)
    return values


def axial_table(residue, mode_count, device_count):
    numbers = jnp.arange(mode_count, dtype=jnp.int32)
    points = residue + device_count * numbers
    cosine, sine_part = phase_table(points[:, None], numbers[None, :], NX, 1.0)
    norm_scale = 1.0 / math.sqrt(NX)
    return (cosine * norm_scale, sine_part * norm_scale)


def span_table(groups, span_size):
    residues = jnp.arange(groups, dtype=jnp.int32)[:, None, None]
    grid_rows = jnp.arange(span_size, dtype=jnp.int32)[None, :, None]
    mode_cols = jnp.arange(span_size, dtype=jnp.int32)[None, None, :]
    cosine, sine_part = phase_table(mode_cols, residues + groups * grid_rows, NZ, 1.0)
    norm_scale = 1.0 / math.sqrt(NZ)
    return (cosine * norm_scale, sine_part * norm_scale)


def spanwise_work(received):
    fields, pair_size, planes, row_count, extent = received.shape
    groups = lax.axis_size("gz")
    span_size = extent // groups
    blocks = received.reshape(fields, pair_size, planes, row_count, groups, span_size)
    group_ids = jnp.arange(groups, dtype=jnp.int32)
    mix_real, mix_imag = phase_table(group_ids[:, None], group_ids[None, :], groups, 1.0)
    section_real, section_imag = complex_apply(
        blocks[:, 0], blocks[:, 1], mix_real, mix_imag, "fylcj,rc->fylrj"
    )
    table_real, table_imag = span_table(groups, span_size)
    physical = exact_einsum("fylrj,rtj->fylrt", section_real, table_real) - exact_einsum(
        "fylrj,rtj->fylrt", section_imag, table_imag
    )
    products = jnp.stack(
        [physical[0] * physical[0], physical[0] * physical[1], physical[1] * physical[1]]
    )
    back_real = exact_einsum("pylrt,rtj->pylrj", products, table_real)
    back_imag = -exact_einsum("pylrt,rtj->pylrj", products, table_imag)
    out_real, out_imag = complex_apply(back_real, back_imag, mix_real, -mix_imag, "pylrj,cr->pylcj")
    spectra = jnp.stack([out_real, out_imag], axis=1)
    return spectra.reshape(3, pair_size, planes, row_count, extent)


def span_round(values, work):
    span_spectra = work(lax.all_to_all(values, "gz", split_axis=3, concat_axis=4, tiled=True))
    return lax.all_to_all(span_spectra, "gz", split_axis=4, concat_axis=3, tiled=True)


def signed_block(start, mode_count, extent):
    numbers = start + jnp.arange(mode_count, dtype=jnp.int32)
    return jnp.where(2 * numbers < extent, numbers, numbers - extent)


def local(velocity, previous, base_flow):
    mode_count = velocity.shape[3]
    span_size = velocity.shape[4]
    device_count = lax.axis_size("gx")
    spread, residue = spread_butterfly(velocity)
    table_real, table_imag = axial_table(residue, mode_count, device_count)
    along_real, along_imag = complex_apply(
        spread[:, 0], spread[:, 1], table_real, table_imag, "fymq,sm->fysq"
    )
    physical_along = jnp.stack([along_real, along_imag], axis=1)
    returned = span_round(physical_along, spanwise_work)
    local_real, local_imag = complex_apply(
        returned[:, 0], returned[:, 1], table_real.T, -table_imag.T, "fysq,ms->fymq"
    )
    local_spectra = jnp.stack([local_real, local_imag], axis=1)
    product_spectra = gather_butterfly(local_spectra)
    modes_along = signed_block(lax.axis_index("gx") * mode_count, mode_count, NX)
    modes_across = signed_block(lax.axis_index("gz") * span_size, span_size, NZ)
    wave_along = (modes_along.astype(jnp.float32) * (TWO_PI / NX))[:, None]
    wave_across = (modes_across.astype(jnp.float32) * (TWO_PI / NZ))[None, :]
    keep = jnp.logical_and(
        (3 * jnp.abs(modes_along) < NX)[:, None], (3 * jnp.abs(modes_across) < NZ)[None, :]
    ).astype(jnp.float32)
    shear = base_flow[:, None, None] * wave_along[None]
    prod_real = product_spectra[:, 0]
    prod_imag = product_spectra[:, 1]
    first_real = (
        keep * (wave_along * prod_imag[0] + wave_across * prod_imag[1]) + shear * velocity[0, 1]
    )
    first_imag = (
        -keep * (wave_along * prod_real[0] + wave_across * prod_real[1]) - shear * velocity[0, 0]
    )
    second_real = (
        keep * (wave_along * prod_imag[1] + wave_across * prod_imag[2]) + shear * velocity[1, 1]
    )
    second_imag = (
        -keep * (wave_along * prod_real[1] + wave_across * prod_real[2]) - shear * velocity[1, 0]
    )
    nonlinear = jnp.stack(
        [jnp.stack([first_real, first_imag]), jnp.stack([second_real, second_imag])]
    )
    damping = jnp.exp(-VISCOSITY * (wave_along * wave_along + wave_across * wave_across))
    advanced = damping * (velocity + TIME_STEP * (GAMMA_NEW * nonlinear + ZETA_OLD * previous))
    return (advanced, nonlinear)


XR = 16
XS = NX // XR
ZR = 8
ZS = NZ // ZR
LOW = (0, 1, 2)
HIGH = (5, 6, 7)
MIB = 1 << 20
CHUNKS = (16, 16, 32, 32, 32)
UNIT = 8
UNITS = 11
SIDE = 16 * UNITS
PER = XS // UNIT
OWN = 2 * UNITS
EXTRA = PER - OWN
SPANS = (2, 2, 2, 2, 2, 1)
BACK_AHEAD = 6
UNROLL = 16


def split_table(table):
    high = table.astype(np.float32).astype(jnp.bfloat16)
    low = (table - high.astype(np.float64)).astype(np.float32).astype(jnp.bfloat16)
    return high, low


def z_table():
    r = np.arange(ZR)[:, None, None]
    b = np.arange(ZS)[None, :, None]
    s = np.arange(ZS)[None, None, :]
    angle = TWO_PI / NZ * ((b * (r + ZR * s)) % NZ)
    cos, sin = np.cos(angle) / math.sqrt(NZ), np.sin(angle) / math.sqrt(NZ)
    return split_table(np.concatenate([cos, sin], axis=2))


def x_table():
    r = np.arange(XR)[:, None, None]
    s = np.arange(XS)[None, :, None]
    m = np.arange(XS)[None, None, :]
    angle = TWO_PI / NX * ((m * (r + XR * s)) % NX)
    cos, sin = np.cos(angle) / math.sqrt(NX), np.sin(angle) / math.sqrt(NX)
    return split_table(np.concatenate([cos, -sin], axis=2))


def turn(value, numerator, size, sign):
    re, im = value
    numerator = numerator % size
    if numerator == 0:
        return re, im
    if 4 * numerator == size:
        return (-im, re) if sign > 0 else (im, -re)
    if 8 * numerator == size:
        h = math.sqrt(0.5)
        return ((re - im) * h, (re + im) * h) if sign > 0 else ((re + im) * h, (im - re) * h)
    if 8 * numerator == 3 * size:
        h = math.sqrt(0.5)
        return ((-re - im) * h, (re - im) * h) if sign > 0 else ((im - re) * h, (-re - im) * h)
    c = math.cos(TWO_PI * numerator / size)
    s = sign * math.sin(TWO_PI * numerator / size)
    return re * c - im * s, re * s + im * c


def small_dft(values, sign):
    size = len(values)
    if size == 1:
        return values
    even = small_dft(values[0::2], sign)
    odd = small_dft(values[1::2], sign)
    half = size // 2
    out = [None] * size
    for i in range(half):
        re, im = turn(odd[i], i, size, sign)
        out[i] = (even[i][0] + re, even[i][1] + im)
        out[i + half] = (even[i][0] - re, even[i][1] - im)
    return out


def parts_of(value):
    high = value.astype(jnp.bfloat16)
    return high, (value - high.astype(jnp.float32)).astype(jnp.bfloat16)


def dot3(a_high, a_low, b_high, b_low, dims):
    def dot(a, b):
        return lax.dot_general(a, b, (dims, ((), ())), preferred_element_type=jnp.float32)

    return dot(a_high, b_high) + (dot(a_high, b_low) + dot(a_low, b_high))


def merge(first, second, low_half):
    return (
        jnp.where(low_half, first, pltpu.roll(second, 64, 1)),
        jnp.where(low_half, pltpu.roll(first, 64, 1), second),
    )


def z_inverse(first, own_ref, other_ref, row, rows, high_ref, low_ref, out_ref, th_ref, tl_ref):
    step = 16
    for c in range(2):
        def body(i, carry):
            at = pl.multiple_of(i * step, step)
            for lane in range(0, ZS, 128):
                values = [None] * ZR
                for a in range(ZR // 2):
                    to = (pl.ds(row + at, step), pl.ds(a * ZS + lane, 128))
                    own = [own_ref[(c, p) + to] for p in range(2)]
                    other = [other_ref[(c, p) + to] for p in range(2)]
                    values[a] = tuple(jnp.where(first, x, y) for x, y in zip(own, other))
                    values[a + ZR // 2] = tuple(jnp.where(first, y, x) for x, y in zip(own, other))
                for r, pair in enumerate(small_dft(values, 1)):
                    for p in range(2):
                        high, low = parts_of(pair[p])
                        line = pl.ds((2 * p + c) * rows + at, step)
                        th_ref[r, line, pl.ds(lane, 128)] = high
                        tl_ref[r, line, pl.ds(lane, 128)] = low
            return carry
        lax.fori_loop(0, rows // step, body, 0)

    def group(r, carry):
        both = dot3(
            th_ref[r, : 4 * rows], tl_ref[r, : 4 * rows], high_ref[r], low_ref[r], ((1,), (0,))
        )
        real, imag = both[: 2 * rows], both[2 * rows :]
        done = jnp.concatenate(
            [real[:, :ZS] - imag[:, ZS:], real[:, ZS:] + imag[:, :ZS]], axis=1
        )
        low_half = lax.broadcasted_iota(jnp.int32, (rows, 128), 1) < 64
        for p in range(2):
            for t in range(2):
                at = p * ZS + t * 128
                even, odd = merge(done[:rows, at : at + 128], done[rows:, at : at + 128], low_half)
                out_ref[r * 4 + 2 * t, p, pl.ds(row, rows), :] = even
                out_ref[r * 4 + 2 * t + 1, p, pl.ds(row, rows), :] = odd
        return carry
    lax.fori_loop(0, ZR, group, 0)


def x_spread(v_ref, row, rows, th_ref, tl_ref):
    step = 16
    half = XS // 2
    for r in range(2):
        def body(i, carry):
            at = pl.multiple_of(row + i * step, step)
            values = [
                tuple(v_ref[2 * g + r, p, pl.ds(at, step), :] for p in range(2)) for g in range(XR)
            ]
            for res, pair in enumerate(small_dft(values, 1)):
                for p in range(2):
                    high, low = parts_of(pair[p])
                    th_ref[res, pl.ds(p * XS + r * half + at, step), :] = high
                    tl_ref[res, pl.ds(p * XS + r * half + at, step), :] = low
            return carry
        lax.fori_loop(0, rows // step, body, 0)


def x_products(ih_ref, il_ref, fh_ref, fl_ref, th_ref, tl_ref, u_ref):
    def residue(res, carry):
        field = dot3(ih_ref[res], il_ref[res], th_ref[res], tl_ref[res], ((1,), (0,)))
        swapped = pltpu.roll(field, 64, 1)
        products = jnp.concatenate([field * field, field * swapped], axis=1)
        high, low = parts_of(products)
        u_ref[res] = dot3(fh_ref[res], fl_ref[res], high, low, ((1,), (0,)))
        return carry
    lax.fori_loop(0, XR, residue, 0, unroll=UNROLL)


def place_of(o, s):
    e = s - OWN
    if o < 2:
        e = e + o * EXTRA
        m = jnp.where(s < OWN, o, jnp.where(e < 14, 4, 5))
        n = jnp.where(s < OWN, s, jnp.where(e < 14, e, e - 14))
    elif o < 4:
        e = e + (o - 2) * EXTRA
        m = jnp.where(s < OWN, o, 6 + lax.rem(e, 2))
        n = jnp.where(s < OWN, s, e // 2)
    elif o == 4:
        e = s + 12
        m = jnp.where(s < 8, 4, 6 + lax.rem(e, 2))
        n = jnp.where(s < 8, s + 14, e // 2)
    else:
        m, n = 5, s + 6
    return m, lax.rem(n, 2), n // 2


def unit_at(gx, gz, u):
    right = gx >= XR // 2
    m = jnp.where(right, XR - 1 - gx, gx)
    n = 2 * u + gz
    e = jnp.where(m == 4, n, jnp.where(m == 5, n + 14, 2 * n + m - 6))
    upper = e >= EXTRA
    helps = jnp.where(m == 4, n < 14, jnp.where(m == 5, n < 6, e < 2 * EXTRA))
    owner = jnp.where(upper, 1, 0) + jnp.where(m >= 6, 2, 0)
    own_slot = jnp.where(m == 4, n - 14, jnp.where(m == 5, n - 6, e - 12))
    o = jnp.where(m < 4, m, jnp.where(helps, owner, jnp.where(m == 5, 5, 4)))
    s = jnp.where(
        m < 4, n, jnp.where(helps, OWN + e - jnp.where(upper, EXTRA, 0), own_slot)
    )
    unit = o * PER + s
    return jnp.where(right, XR * PER - 1 - unit, unit)


def x_gather(u_ref, out_ref):
    low_half = lax.broadcasted_iota(jnp.int32, (UNIT, 128), 1) < 64
    split = SIDE % PER
    for first, last in ((0, split), (split, PER)):
        def back(i, carry):
            at = pl.multiple_of(i * UNIT, UNIT)
            for h in range(2):
                values = [
                    tuple(
                        u_ref[res, pl.ds(p * XS + at, UNIT), pl.ds(h * 128, 128)]
                        for p in range(2)
                    )
                    for res in range(XR)
                ]
                for g, (re, im) in enumerate(small_dft(values, -1)):
                    if g * PER + first < SIDE:
                        m, side, u = place_of(g, i)
                    elif (XR - g) * PER - last < SIDE:
                        m, side, u = place_of(XR - 1 - g, PER - 1 - i)
                        m = XR - 1 - m
                    else:
                        continue
                    worker = 2 * m + side
                    line = pl.ds(pl.multiple_of(u * UNIT, UNIT), UNIT)
                    if h == 0:
                        out_ref[worker, 0, line, :] = re
                        out_ref[worker, 1, line, :] = im
                    else:
                        out_ref[worker, 2, line, :] = jnp.where(low_half, re, im)
            return carry
        lax.fori_loop(first, last, back, 0)


def z_forward(unit_of, row, rows, v_ref, high_ref, low_ref, out_ref, w_ref):
    low_half = lax.broadcasted_iota(jnp.int32, (rows, 128), 1) < 64

    def group(r, carry):
        real, imag, mixed = (
            [v_ref[r * 4 + j, x, pl.ds(row, rows), :] for j in range(4)] for x in range(3)
        )
        p0r, p2r, p0i, p2i, p1r, p1i = [], [], [], [], [], []
        for source, first, second in ((real, p0r, p2r), (imag, p0i, p2i), (mixed, p1r, p1i)):
            for t in range(2):
                a, b = merge(source[2 * t], source[2 * t + 1], low_half)
                first.append(a)
                second.append(b)
        lines = jnp.concatenate(
            [jnp.concatenate(x, axis=1) for x in (p0r, p1r, p2r, p0i, p1i, p2i)], axis=0
        )
        high, low = parts_of(lines)
        cos, sin = (
            dot3(high, low, high_ref[r, :, at : at + ZS], low_ref[r, :, at : at + ZS], ((1,), (1,)))
            for at in (0, ZS)
        )
        w_ref[r, : 3 * rows, :ZS] = cos[: 3 * rows] + sin[3 * rows :]
        w_ref[r, : 3 * rows, ZS:] = cos[3 * rows :] - sin[: 3 * rows]
        return carry
    lax.fori_loop(0, ZR, group, 0)

    def body(i, carry):
        at = pl.multiple_of(i * UNIT, UNIT)
        along = unit_of(row // UNIT + i) * UNIT + lax.broadcasted_iota(jnp.int32, (UNIT, 128), 0)
        along = jnp.where(2 * along < NX, along, along - NX)
        wave_along = along.astype(jnp.float32) * (TWO_PI / NX)
        keep_along = 3 * jnp.abs(along) < NX
        for lane in range(0, ZS, 128):
            spectra = []
            for j in range(3):
                values = [
                    tuple(
                        w_ref[r, pl.ds(j * rows + at, UNIT), pl.ds(p * ZS + lane, 128)]
                        for p in range(2)
                    )
                    for r in range(ZR)
                ]
                spectra.append(small_dft(values, -1))
            for half, groups in enumerate((LOW, HIGH)):
                for place, a in enumerate(groups):
                    start = a * ZS + lane - (NZ if half else 0)
                    mode = start + lax.broadcasted_iota(jnp.int32, (UNIT, 128), 1)
                    wave_across = mode.astype(jnp.float32) * (TWO_PI / NZ)
                    keep = jnp.logical_and(3 * jnp.abs(mode) < NZ, keep_along)
                    (ar, ai), (br, bi), (cr, ci) = (x[a] for x in spectra)
                    terms = [
                        jnp.where(keep, wave_along * ai + wave_across * bi, 0.0),
                        jnp.where(keep, -(wave_along * ar + wave_across * br), 0.0),
                        jnp.where(keep, wave_along * bi + wave_across * ci, 0.0),
                        jnp.where(keep, -(wave_along * br + wave_across * cr), 0.0),
                    ]
                    for x in range(4):
                        out_ref[half, x, pl.ds(row + at, UNIT), pl.ds(place * ZS + lane, 128)] = terms[x]
        return carry
    lax.fori_loop(0, rows // UNIT, body, 0)


def substep_kernel(
    velocity_ref, zh_hbm, zl_hbm, ih_hbm, il_hbm, fh_hbm, fl_hbm,
    term_ref,
    own_ref, other_ref, zh_ref, zl_ref, ih_ref, il_ref, fh_ref, fl_ref,
    zth_ref, ztl_ref, out_ref, in_ref, th_ref, tl_ref, u_ref, back_ref, work_ref, w_ref, res_ref,
    table_sems, own_sems, swap_send, swap_recv, out_send, out_recv, back_send, back_recv,
    res_send, res_recv,
):
    gx, gz = lax.axis_index("gx"), lax.axis_index("gz")
    count = 2 * XR
    me = 2 * gx + gz
    half = own_ref.shape[2]
    offsets = [sum(CHUNKS[:c]) for c in range(len(CHUNKS))]

    def device(t):
        return (t // 2, lax.rem(t, 2))

    tables = [
        pltpu.make_async_copy(src, dst, table_sems.at[n])
        for n, (src, dst) in enumerate(
            (
                (zh_hbm, zh_ref),
                (zl_hbm, zl_ref),
                (ih_hbm, ih_ref),
                (il_hbm, il_ref),
                (fh_hbm, fh_ref),
                (fl_hbm, fl_ref),
            )
        )
    ]

    def load_own(c):
        return pltpu.make_async_copy(
            velocity_ref.at[:, :, pl.ds(pl.multiple_of(gz * half + offsets[c], 16), CHUNKS[c]), :],
            own_ref.at[:, :, pl.ds(offsets[c], CHUNKS[c]), :],
            own_sems.at[c],
        )

    def swap(c):
        return pltpu.make_async_remote_copy(
            src_ref=velocity_ref.at[
                :, :, pl.ds(pl.multiple_of((1 - gz) * half + offsets[c], 16), CHUNKS[c]), :
            ],
            dst_ref=other_ref.at[:, :, pl.ds(offsets[c], CHUNKS[c]), :],
            send_sem=swap_send.at[c],
            recv_sem=swap_recv.at[c],
            device_id=(gx, 1 - gz),
            device_id_type=pl.DeviceIdType.MESH,
        )

    for c in range(len(CHUNKS)):
        load_own(c).start()
    for table in tables[:2]:
        table.start()

    barrier = pltpu.get_barrier_semaphore()

    def greet(i, carry):
        pl.semaphore_signal(
            barrier,
            inc=1,
            device_id=device(lax.rem(me + i, count)),
            device_id_type=pl.DeviceIdType.MESH,
        )
        return carry

    lax.fori_loop(1, count, greet, 0)
    pl.semaphore_wait(barrier, count - 1)
    for c in range(len(CHUNKS)):
        swap(c).start()
    for table in tables[2:]:
        table.start()

    def ship(src_ref, dst_ref, sends, recvs, c, at, length):
        span = pl.ds(at, length)

        def copy(i):
            t = lax.rem(me + i, count)
            return pltpu.make_async_remote_copy(
                src_ref=src_ref.at[t, :, span, :],
                dst_ref=dst_ref.at[me, :, span, :],
                send_sem=sends.at[c, i],
                recv_sem=recvs.at[c, i],
                device_id=device(t),
                device_id_type=pl.DeviceIdType.MESH,
            )

        def local():
            return pltpu.make_async_copy(
                src_ref.at[me, :, span, :], dst_ref.at[me, :, span, :], recvs.at[c, 0]
            )

        return copy, local

    def ship_start(*args):
        copy, local = ship(*args)

        def start(i, carry):
            copy(i).start()
            return carry

        lax.fori_loop(1, count, start, 0)
        local().start()

    def ship_arrive(*args):
        copy, local = ship(*args)

        def wait(i, carry):
            copy(i).wait_recv()
            return carry

        lax.fori_loop(1, count, wait, 0)
        local().wait()

    def ship_leave(*args):
        copy, _ = ship(*args)

        def wait(i, carry):
            copy(i).wait_send()
            return carry

        lax.fori_loop(1, count, wait, 0)

    def spread_args(c):
        return out_ref, in_ref, out_send, out_recv, c, offsets[c], CHUNKS[c]

    tables[0].wait()
    tables[1].wait()
    for c in range(len(CHUNKS)):
        load_own(c).wait()
        swap(c).wait_recv()
        z_inverse(
            gz == 0, own_ref, other_ref, offsets[c], CHUNKS[c],
            zh_ref, zl_ref, out_ref, zth_ref, ztl_ref,
        )
        ship_start(*spread_args(c))

    for c in range(len(CHUNKS)):
        ship_arrive(*spread_args(c))
        x_spread(in_ref, offsets[c], CHUNKS[c], th_ref, tl_ref)
    for table in tables[2:]:
        table.wait()
    x_products(ih_ref, il_ref, fh_ref, fl_ref, th_ref, tl_ref, u_ref)
    x_gather(u_ref, back_ref)

    starts = [sum(SPANS[:c]) for c in range(len(SPANS))]

    def back_args(c):
        return back_ref, work_ref, back_send, back_recv, c, starts[c] * UNIT, SPANS[c] * UNIT

    for c in range(BACK_AHEAD):
        ship_start(*back_args(c))

    def result(u, side):
        unit = unit_at(gx, gz, u)
        owner = unit // PER
        slot = unit - owner * PER
        src = res_ref.at[side, :, pl.ds(pl.multiple_of(u * UNIT, UNIT), UNIT), :]
        dst = term_ref.at[:, pl.ds(pl.multiple_of(slot * UNIT, UNIT), UNIT), :]
        here = jnp.logical_and(owner == gx, side == gz)

        def remote():
            return pltpu.make_async_remote_copy(
                src_ref=src,
                dst_ref=dst,
                send_sem=res_send.at[side, u],
                recv_sem=res_recv.at[slot],
                device_id=(owner, side),
                device_id_type=pl.DeviceIdType.MESH,
            )

        return here, remote, lambda: pltpu.make_async_copy(src, dst, res_recv.at[slot])

    for c in range(len(SPANS)):
        ship_arrive(*back_args(c))
        unit, units = starts[c], SPANS[c]
        z_forward(
            functools.partial(unit_at, gx, gz), unit * UNIT, units * UNIT,
            work_ref, zh_ref, zl_ref, res_ref, w_ref,
        )

        def send(n, carry):
            for side in range(2):
                here, remote, local = result(unit + n, side)

                @pl.when(here)
                def _():
                    local().start()

                @pl.when(jnp.logical_not(here))
                def _():
                    remote().start()
            return carry

        lax.fori_loop(0, units, send, 0)
        if c + BACK_AHEAD < len(SPANS):
            ship_start(*back_args(c + BACK_AHEAD))

    def sent(u, carry):
        for side in range(2):
            here, remote, _ = result(u, side)

            @pl.when(jnp.logical_not(here))
            def _():
                remote().wait_send()
        return carry

    def got(s, carry):
        unit = gx * PER + s

        @pl.when(jnp.logical_or(unit < SIDE, unit >= XR * PER - SIDE))
        def _():
            pltpu.make_async_copy(
                res_ref.at[0, :, pl.ds(0, UNIT), :],
                term_ref.at[:, pl.ds(pl.multiple_of(s * UNIT, UNIT), UNIT), :],
                res_recv.at[s],
            ).wait()
        return carry

    lax.fori_loop(0, PER, got, 0)
    lax.fori_loop(0, UNITS, sent, 0)

    for c in range(len(CHUNKS)):
        swap(c).wait_send()
        ship_leave(*spread_args(c))
    for c in range(len(SPANS)):
        ship_leave(*back_args(c))


def advance_kernel(place_ref, base_ref, v_ref, old_ref, term_ref, along_ref, across_ref, next_ref, non_ref):
    rows, extent = v_ref.shape[2:]
    unit = place_ref[0] * PER + pl.program_id(0) * (rows // UNIT)
    lower = place_ref[1] == 0
    active = jnp.logical_or(unit < SIDE, unit >= XR * PER - SIDE)
    wave_along = along_ref[:, :1]
    wave_across = across_ref[:1, :]
    damping = jnp.exp(-VISCOSITY * (wave_along * wave_along + wave_across * wave_across))
    shear = base_ref[0] * wave_along
    empty = jnp.zeros((rows, extent - term_ref.shape[2]), jnp.float32)
    for c in range(2):
        for p in range(2):
            term = jnp.where(active, term_ref[2 * c + p], 0.0)
            term = jnp.where(
                lower,
                jnp.concatenate([term, empty], axis=1),
                jnp.concatenate([empty, term], axis=1),
            )
            other = shear * v_ref[c, 1 - p]
            result = term + other if p == 0 else term - other
            non_ref[c, p] = result
            next_ref[c, p] = damping * (
                v_ref[c, p] + TIME_STEP * (GAMMA_NEW * result + ZETA_OLD * old_ref[c, p])
            )


def lines_local(velocity, previous, base_flow):
    velocity, previous = velocity[:, :, 0], previous[:, :, 0]
    mode_count, extent = velocity.shape[2:]
    half = mode_count // 2
    rows = max(CHUNKS)
    gx, gz = lax.axis_index("gx"), lax.axis_index("gz")
    f32, bf16 = jnp.float32, jnp.bfloat16
    zh, zl = z_table()
    xh, xl = x_table()
    fh, fl = np.swapaxes(xh, 1, 2), np.swapaxes(xl, 1, 2)
    active = len(LOW) * ZS
    count = 2 * XR
    dma = pltpu.SemaphoreType.DMA

    term = pl.pallas_call(
        substep_kernel,
        out_shape=jax.ShapeDtypeStruct((4, mode_count, active), f32),
        in_specs=[pl.BlockSpec(memory_space=pl.ANY)] * 7,
        out_specs=pl.BlockSpec(memory_space=pl.ANY),
        scratch_shapes=[
            pltpu.VMEM((2, 2, half, extent), f32),
            pltpu.VMEM((2, 2, half, extent), f32),
            pltpu.VMEM(zh.shape, bf16),
            pltpu.VMEM(zl.shape, bf16),
            pltpu.VMEM(xh.shape, bf16),
            pltpu.VMEM(xl.shape, bf16),
            pltpu.VMEM(fh.shape, bf16),
            pltpu.VMEM(fl.shape, bf16),
            pltpu.VMEM((ZR, 4 * rows, ZS), bf16),
            pltpu.VMEM((ZR, 4 * rows, ZS), bf16),
            pltpu.VMEM((count, 2, half, 128), f32),
            pltpu.VMEM((count, 2, half, 128), f32),
            pltpu.VMEM((XR, 2 * XS, 128), bf16),
            pltpu.VMEM((XR, 2 * XS, 128), bf16),
            pltpu.VMEM((XR, 2 * XS, 256), f32),
            pltpu.VMEM((count, 3, UNITS * UNIT, 128), f32),
            pltpu.VMEM((count, 3, UNITS * UNIT, 128), f32),
            pltpu.VMEM((ZR, 3 * max(SPANS) * UNIT, 2 * ZS), f32),
            pltpu.VMEM((2, 4, UNITS * UNIT, active), f32),
            dma((6,)),
            dma((len(CHUNKS),)),
            dma((len(CHUNKS),)),
            dma((len(CHUNKS),)),
            dma((len(CHUNKS), count)),
            dma((len(CHUNKS), count)),
            dma((len(SPANS), count)),
            dma((len(SPANS), count)),
            dma((2, UNITS)),
            dma((PER,)),
        ],
        compiler_params=pltpu.CompilerParams(
            collective_id=1, has_side_effects=True, vmem_limit_bytes=60 * MIB
        ),
        cost_estimate=pl.CostEstimate(
            flops=10**10, bytes_accessed=64 * velocity.size, transcendentals=0
        ),
        name="substep",
    )(velocity, zh, zl, xh, xl, fh, fl)

    def modes(start, count, size):
        numbers = start + jnp.arange(count, dtype=jnp.int32)
        return jnp.where(2 * numbers < size, numbers, numbers - size)

    along = modes(gx * mode_count, mode_count, NX).astype(f32) * (TWO_PI / NX)
    across = modes(gz * extent, extent, NZ).astype(f32) * (TWO_PI / NZ)
    scalar = pl.BlockSpec(memory_space=pltpu.SMEM)
    block = 64
    field = pl.BlockSpec((2, 2, block, extent), lambda i: (0, 0, i, 0))
    advanced, nonlinear = pl.pallas_call(
        advance_kernel,
        grid=(mode_count // block,),
        out_shape=[jax.ShapeDtypeStruct(velocity.shape, f32)] * 2,
        in_specs=[
            scalar,
            scalar,
            field,
            field,
            pl.BlockSpec((4, block, active), lambda i: (0, i, 0)),
            pl.BlockSpec((block, 128), lambda i: (i, 0)),
            pl.BlockSpec((8, extent), lambda i: (0, 0)),
        ],
        out_specs=[field, field],
        compiler_params=pltpu.CompilerParams(vmem_limit_bytes=60 * MIB),
        name="advance",
    )(
        jnp.stack([gx, gz]).astype(jnp.int32),
        base_flow,
        velocity,
        previous,
        term,
        jnp.broadcast_to(along[:, None], (mode_count, 128)),
        jnp.broadcast_to(across[None], (8, extent)),
    )
    return advanced[:, :, None], nonlinear[:, :, None]


def solution(mesh):
    in_specs = (P(None, None, None, "gx", "gz"), P(None, None, None, "gx", "gz"), P())
    out_specs = (P(None, None, None, "gx", "gz"), P(None, None, None, "gx", "gz"))
    fits = mesh.shape["gx"] == XR and mesh.shape["gz"] == 2
    work = lines_local if fits else local
    return jax.shard_map(work, mesh=mesh, in_specs=in_specs, out_specs=out_specs, check_vma=False)
```

```python
import functools
import math

import jax
import jax.numpy as jnp
import numpy as np
from jax import lax
from jax.experimental import pallas as pl
from jax.experimental.pallas import tpu as pltpu
from jax.sharding import PartitionSpec as P

NX = 4096
NZ = 2048


TWO_PI = 2.0 * math.pi
VISCOSITY = 0.05
TIME_STEP = 0.2
GAMMA_NEW = 8.0 / 15.0
ZETA_OLD = -17.0 / 60.0


def partner_2(x, axis, distance):
    return lax.ppermute(x, axis, [(i, i ^ 1 << distance) for i in range(lax.axis_size(axis))])


def exact_einsum(pattern, left_array, right_array):
    return jnp.einsum(
        pattern,
        left_array,
        right_array,
        precision=lax.Precision.HIGHEST,
        preferred_element_type=jnp.float32,
    )


def phase_table(left_ints, right_ints, period, direction):
    phase_angle = (
        direction * TWO_PI / period * (left_ints * right_ints % period).astype(jnp.float32)
    )
    return (jnp.cos(phase_angle), jnp.sin(phase_angle))


def complex_apply(value_real, value_imag, table_real, table_imag, pattern):
    out_real = exact_einsum(pattern, value_real, table_real) - exact_einsum(
        pattern, value_imag, table_imag
    )
    out_imag = exact_einsum(pattern, value_real, table_imag) + exact_einsum(
        pattern, value_imag, table_real
    )
    return (out_real, out_imag)


def residue_of(position, levels):
    reversed_bits = jnp.zeros((), jnp.int32)
    for level in range(levels):
        reversed_bits = reversed_bits + ((position >> level & 1) << levels - 1 - level)
    return reversed_bits


def section_twiddle(position, half_span):
    phase_angle = TWO_PI / (2 * half_span) * (position % half_span).astype(jnp.float32)
    return (jnp.cos(phase_angle), jnp.sin(phase_angle))


def spread_butterfly(values):
    position = lax.axis_index("gx")
    levels = lax.axis_size("gx").bit_length() - 1
    for level in reversed(range(levels)):
        half_span = 1 << level
        partner = partner_2(values, "gx", level)
        upper_half = position >> level & 1 == 1
        cosine, sine_part = section_twiddle(position, half_span)
        difference = partner - values
        rotated = jnp.stack(
            [
                difference[:, 0] * cosine - difference[:, 1] * sine_part,
                difference[:, 0] * sine_part + difference[:, 1] * cosine,
            ],
            axis=1,
        )
        values = jnp.where(upper_half, rotated, values + partner)
    return (values, residue_of(position, levels))


def gather_butterfly(values):
    position = lax.axis_index("gx")
    levels = lax.axis_size("gx").bit_length() - 1
    for level in range(levels):
        half_span = 1 << level
        partner = partner_2(values, "gx", level)
        upper_half = position >> level & 1 == 1
        cosine, sine_part = section_twiddle(position, half_span)
        upper_item = jnp.where(upper_half, values, partner)
        lower_item = jnp.where(upper_half, partner, values)
        turned = jnp.stack(
            [
                upper_item[:, 0] * cosine + upper_item[:, 1] * sine_part,
                upper_item[:, 1] * cosine - upper_item[:, 0] * sine_part,
            ],
            axis=1,
        )
        values = jnp.where(upper_half, lower_item - turned, lower_item + turned)
    return values


def axial_table(residue, mode_count, device_count):
    numbers = jnp.arange(mode_count, dtype=jnp.int32)
    points = residue + device_count * numbers
    cosine, sine_part = phase_table(points[:, None], numbers[None, :], NX, 1.0)
    norm_scale = 1.0 / math.sqrt(NX)
    return (cosine * norm_scale, sine_part * norm_scale)


def span_table(groups, span_size):
    residues = jnp.arange(groups, dtype=jnp.int32)[:, None, None]
    grid_rows = jnp.arange(span_size, dtype=jnp.int32)[None, :, None]
    mode_cols = jnp.arange(span_size, dtype=jnp.int32)[None, None, :]
    cosine, sine_part = phase_table(mode_cols, residues + groups * grid_rows, NZ, 1.0)
    norm_scale = 1.0 / math.sqrt(NZ)
    return (cosine * norm_scale, sine_part * norm_scale)


def spanwise_work(received):
    fields, pair_size, planes, row_count, extent = received.shape
    groups = lax.axis_size("gz")
    span_size = extent // groups
    blocks = received.reshape(fields, pair_size, planes, row_count, groups, span_size)
    group_ids = jnp.arange(groups, dtype=jnp.int32)
    mix_real, mix_imag = phase_table(group_ids[:, None], group_ids[None, :], groups, 1.0)
    section_real, section_imag = complex_apply(
        blocks[:, 0], blocks[:, 1], mix_real, mix_imag, "fylcj,rc->fylrj"
    )
    table_real, table_imag = span_table(groups, span_size)
    physical = exact_einsum("fylrj,rtj->fylrt", section_real, table_real) - exact_einsum(
        "fylrj,rtj->fylrt", section_imag, table_imag
    )
    products = jnp.stack(
        [physical[0] * physical[0], physical[0] * physical[1], physical[1] * physical[1]]
    )
    back_real = exact_einsum("pylrt,rtj->pylrj", products, table_real)
    back_imag = -exact_einsum("pylrt,rtj->pylrj", products, table_imag)
    out_real, out_imag = complex_apply(back_real, back_imag, mix_real, -mix_imag, "pylrj,cr->pylcj")
    spectra = jnp.stack([out_real, out_imag], axis=1)
    return spectra.reshape(3, pair_size, planes, row_count, extent)


def span_round(values, work):
    span_spectra = work(lax.all_to_all(values, "gz", split_axis=3, concat_axis=4, tiled=True))
    return lax.all_to_all(span_spectra, "gz", split_axis=4, concat_axis=3, tiled=True)


def signed_block(start, mode_count, extent):
    numbers = start + jnp.arange(mode_count, dtype=jnp.int32)
    return jnp.where(2 * numbers < extent, numbers, numbers - extent)


def local(velocity, previous, base_flow):
    mode_count = velocity.shape[3]
    span_size = velocity.shape[4]
    device_count = lax.axis_size("gx")
    spread, residue = spread_butterfly(velocity)
    table_real, table_imag = axial_table(residue, mode_count, device_count)
    along_real, along_imag = complex_apply(
        spread[:, 0], spread[:, 1], table_real, table_imag, "fymq,sm->fysq"
    )
    physical_along = jnp.stack([along_real, along_imag], axis=1)
    returned = span_round(physical_along, spanwise_work)
    local_real, local_imag = complex_apply(
        returned[:, 0], returned[:, 1], table_real.T, -table_imag.T, "fysq,ms->fymq"
    )
    local_spectra = jnp.stack([local_real, local_imag], axis=1)
    product_spectra = gather_butterfly(local_spectra)
    modes_along = signed_block(lax.axis_index("gx") * mode_count, mode_count, NX)
    modes_across = signed_block(lax.axis_index("gz") * span_size, span_size, NZ)
    wave_along = (modes_along.astype(jnp.float32) * (TWO_PI / NX))[:, None]
    wave_across = (modes_across.astype(jnp.float32) * (TWO_PI / NZ))[None, :]
    keep = jnp.logical_and(
        (3 * jnp.abs(modes_along) < NX)[:, None], (3 * jnp.abs(modes_across) < NZ)[None, :]
    ).astype(jnp.float32)
    shear = base_flow[:, None, None] * wave_along[None]
    prod_real = product_spectra[:, 0]
    prod_imag = product_spectra[:, 1]
    first_real = (
        keep * (wave_along * prod_imag[0] + wave_across * prod_imag[1]) + shear * velocity[0, 1]
    )
    first_imag = (
        -keep * (wave_along * prod_real[0] + wave_across * prod_real[1]) - shear * velocity[0, 0]
    )
    second_real = (
        keep * (wave_along * prod_imag[1] + wave_across * prod_imag[2]) + shear * velocity[1, 1]
    )
    second_imag = (
        -keep * (wave_along * prod_real[1] + wave_across * prod_real[2]) - shear * velocity[1, 0]
    )
    nonlinear = jnp.stack(
        [jnp.stack([first_real, first_imag]), jnp.stack([second_real, second_imag])]
    )
    damping = jnp.exp(-VISCOSITY * (wave_along * wave_along + wave_across * wave_across))
    advanced = damping * (velocity + TIME_STEP * (GAMMA_NEW * nonlinear + ZETA_OLD * previous))
    return (advanced, nonlinear)


XR = 16
XS = NX // XR
ZR = 8
ZS = NZ // ZR
LOW = (0, 1, 2)
HIGH = (5, 6, 7)
MIB = 1 << 20
CHUNKS = (16,) * 8
UNIT = 8
UNITS = 11
SIDE = 16 * UNITS
PER = XS // UNIT
OWN = 2 * UNITS
EXTRA = PER - OWN
SPANS = (3, 3, 3, 1, 1)
BACK_AHEAD = 3
UNROLL = 16
UNROLL_INV = 8
UNROLL_FWD = 8
UNROLL_EARLY = 4
BLOCK = 32
SUB_VMEM = 49
ADV_VMEM = 40
SHORT = 9
NEEDED = SIDE - 4


def split_table(table):
    high = table.astype(np.float32).astype(jnp.bfloat16)
    low = (table - high.astype(np.float64)).astype(np.float32).astype(jnp.bfloat16)
    return high, low


def z_table():
    r = np.arange(ZR)[:, None, None]
    b = np.arange(ZS)[None, :, None]
    s = np.arange(ZS)[None, None, :]
    angle = TWO_PI / NZ * ((b * (r + ZR * s)) % NZ)
    cos, sin = np.cos(angle) / math.sqrt(NZ), np.sin(angle) / math.sqrt(NZ)
    return split_table(np.concatenate([cos, sin], axis=2))


def x_table():
    r = np.arange(XR)[:, None, None]
    s = np.arange(XS)[None, :, None]
    m = np.arange(XS)[None, None, :]
    angle = TWO_PI / NX * ((m * (r + XR * s)) % NX)
    cos, sin = np.cos(angle) / math.sqrt(NX), np.sin(angle) / math.sqrt(NX)
    return np.stack([cos, -sin], axis=2)


def x_inverse_table():
    table = x_table().reshape(XR, XS, 4, XS // 2)
    parts = []
    for c, length in enumerate(CHUNKS):
        start = sum(CHUNKS[:c])
        parts.append(table[..., start : start + length].reshape(XR, XS, 4 * length))
    return split_table(np.concatenate(parts, axis=2))


def x_forward_table():
    return split_table(np.swapaxes(x_table().reshape(XR, XS, 2 * XS), 1, 2))


def turn(value, numerator, size, sign):
    re, im = value
    numerator = numerator % size
    if numerator == 0:
        return re, im
    if 4 * numerator == size:
        return (-im, re) if sign > 0 else (im, -re)
    if 8 * numerator == size:
        h = math.sqrt(0.5)
        return ((re - im) * h, (re + im) * h) if sign > 0 else ((re + im) * h, (im - re) * h)
    if 8 * numerator == 3 * size:
        h = math.sqrt(0.5)
        return ((-re - im) * h, (re - im) * h) if sign > 0 else ((im - re) * h, (-re - im) * h)
    c = math.cos(TWO_PI * numerator / size)
    s = sign * math.sin(TWO_PI * numerator / size)
    return re * c - im * s, re * s + im * c


def small_dft(values, sign):
    size = len(values)
    if size == 1:
        return values
    even = small_dft(values[0::2], sign)
    odd = small_dft(values[1::2], sign)
    half = size // 2
    out = [None] * size
    for i in range(half):
        re, im = turn(odd[i], i, size, sign)
        out[i] = (even[i][0] + re, even[i][1] + im)
        out[i + half] = (even[i][0] - re, even[i][1] - im)
    return out


def parts_of(value):
    high = value.astype(jnp.bfloat16)
    return high, (value - high.astype(jnp.float32)).astype(jnp.bfloat16)


def dot3(a_high, a_low, b_high, b_low, dims):
    def dot(a, b):
        return lax.dot_general(a, b, (dims, ((), ())), preferred_element_type=jnp.float32)

    return dot(a_high, b_high) + (dot(a_high, b_low) + dot(a_low, b_high))


def merge(first, second, low_half):
    return (
        jnp.where(low_half, first, pltpu.roll(second, 64, 1)),
        jnp.where(low_half, pltpu.roll(first, 64, 1), second),
    )


def z_inverse(first, rows_ref, row, rows, high_ref, low_ref, out_ref, th_ref, tl_ref):
    step = 16
    for c in range(2):
        def body(i, carry):
            at = pl.multiple_of(i * step, step)
            for lane in range(0, ZS, 128):
                values = [None] * ZR
                for a in range(ZR // 2):
                    to = (pl.ds(row + at, step), pl.ds(a * ZS + lane, 128))
                    own = [rows_ref[(0, 2 * c + p) + to] for p in range(2)]
                    other = [rows_ref[(1, 2 * c + p) + to] for p in range(2)]
                    values[a] = tuple(jnp.where(first, x, y) for x, y in zip(own, other))
                    values[a + ZR // 2] = tuple(jnp.where(first, y, x) for x, y in zip(own, other))
                for r, pair in enumerate(small_dft(values, 1)):
                    for p in range(2):
                        high, low = parts_of(pair[p])
                        line = pl.ds((2 * p + c) * rows + at, step)
                        th_ref[r, line, pl.ds(lane, 128)] = high
                        tl_ref[r, line, pl.ds(lane, 128)] = low
            return carry
        lax.fori_loop(0, rows // step, body, 0)

    def group(r, carry):
        both = dot3(
            th_ref[r, : 4 * rows], tl_ref[r, : 4 * rows], high_ref[r], low_ref[r], ((1,), (0,))
        )
        real, imag = both[: 2 * rows], both[2 * rows :]
        done = jnp.concatenate(
            [real[:, :ZS] - imag[:, ZS:], real[:, ZS:] + imag[:, :ZS]], axis=1
        )
        low_half = lax.broadcasted_iota(jnp.int32, (rows, 128), 1) < 64
        for p in range(2):
            for t in range(2):
                at = p * ZS + t * 128
                even, odd = merge(done[:rows, at : at + 128], done[rows:, at : at + 128], low_half)
                out_ref[r * 4 + 2 * t, p, pl.ds(row, rows), :] = even
                out_ref[r * 4 + 2 * t + 1, p, pl.ds(row, rows), :] = odd
        return carry
    lax.fori_loop(0, ZR, group, 0, unroll=UNROLL_INV)


def x_spread(v_ref, row, rows, th_ref, tl_ref):
    step = 16
    for r in range(2):
        def body(i, carry):
            at = pl.multiple_of(i * step, step)
            values = [
                tuple(v_ref[2 * g + r, p, pl.ds(row + at, step), :] for p in range(2))
                for g in range(XR)
            ]
            for res, pair in enumerate(small_dft(values, 1)):
                for p in range(2):
                    high, low = parts_of(pair[p])
                    line = pl.ds(4 * row + (2 * p + r) * rows + at, step)
                    th_ref[res, line, :] = high
                    tl_ref[res, line, :] = low
            return carry
        lax.fori_loop(0, rows // step, body, 0)


def x_early(lines, ih_ref, il_ref, th_ref, tl_ref, f_ref):
    def residue(res, carry):
        f_ref[res] = dot3(
            ih_ref[res, :, :lines], il_ref[res, :, :lines],
            th_ref[res, :lines], tl_ref[res, :lines], ((1,), (0,)),
        )
        return carry
    lax.fori_loop(0, XR, residue, 0, unroll=UNROLL_EARLY)


def x_products(lines, ih_ref, il_ref, fh_ref, fl_ref, th_ref, tl_ref, f_ref, u_refs):
    def residue(res, carry):
        field = f_ref[res] + dot3(
            ih_ref[res, :, lines:], il_ref[res, :, lines:],
            th_ref[res, lines:], tl_ref[res, lines:], ((1,), (0,)),
        )
        swapped = pltpu.roll(field, 64, 1)
        products = jnp.concatenate([field * field, field * swapped], axis=1)
        high, low = parts_of(products)
        both = dot3(fh_ref[res], fl_ref[res], high, low, ((1,), (0,)))
        half = XS // 2
        for h, u_ref in enumerate(u_refs):
            for p in range(2):
                for r in range(2):
                    at = p * XS + r * half
                    u_ref[2 * res + p, r] = both[at : at + half, h * 128 : h * 128 + 128]
        return carry
    lax.fori_loop(0, XR, residue, 0, unroll=UNROLL)


def place_of(o, s):
    e = s - OWN
    if o < 2:
        e = e + o * EXTRA
        m = jnp.where(s < OWN, o, jnp.where(e < 14, 4, 5))
        n = jnp.where(s < OWN, s, jnp.where(e < 14, e, e - 14))
    elif o < 4:
        e = e + (o - 2) * EXTRA
        m = jnp.where(s < OWN, o, 6 + lax.rem(e, 2))
        n = jnp.where(s < OWN, s, e // 2)
    elif o == 4:
        e = s + 12
        m = jnp.where(s < 8, 4, 6 + lax.rem(e, 2))
        n = jnp.where(s < 8, s + 14, e // 2)
    else:
        m, n = 5, s + 6
    return m, lax.rem(n, 2), n // 2


def unit_at(gx, gz, u):
    right = gx >= XR // 2
    m = jnp.where(right, XR - 1 - gx, gx)
    n = 2 * u + gz
    e = jnp.where(m == 4, n, jnp.where(m == 5, n + 14, 2 * n + m - 6))
    upper = e >= EXTRA
    helps = jnp.where(m == 4, n < 14, jnp.where(m == 5, n < 6, e < 2 * EXTRA))
    owner = jnp.where(upper, 1, 0) + jnp.where(m >= 6, 2, 0)
    own_slot = jnp.where(m == 4, n - 14, jnp.where(m == 5, n - 6, e - 12))
    o = jnp.where(m < 4, m, jnp.where(helps, owner, jnp.where(m == 5, 5, 4)))
    s = jnp.where(
        m < 4, n, jnp.where(helps, OWN + e - jnp.where(upper, EXTRA, 0), own_slot)
    )
    unit = o * PER + s
    return jnp.where(right, XR * PER - 1 - unit, unit)


def x_gather(u_refs, out_ref):
    low_half = lax.broadcasted_iota(jnp.int32, (UNIT, 128), 1) < 64
    split = SIDE % PER
    for first, last in ((0, split), (split, PER)):
        def back(i, carry):
            part = i * UNIT // (XS // 2)
            at = pl.multiple_of(i * UNIT - part * (XS // 2), UNIT)
            for h in range(2):
                values = [
                    tuple(
                        u_refs[h][2 * res + p, part, pl.ds(at, UNIT), :]
                        for p in range(2)
                    )
                    for res in range(XR)
                ]
                for g, (re, im) in enumerate(small_dft(values, -1)):
                    if g * PER + first < SIDE:
                        m, side, u = place_of(g, i)
                    elif (XR - g) * PER - last < SIDE:
                        m, side, u = place_of(XR - 1 - g, PER - 1 - i)
                        m = XR - 1 - m
                    else:
                        continue
                    worker = 2 * m + side
                    line = pl.ds(pl.multiple_of(u * UNIT, UNIT), UNIT)
                    if h == 0:
                        out_ref[worker, 0, line, :] = re
                        out_ref[worker, 1, line, :] = im
                    else:
                        out_ref[worker, 2, line, :] = jnp.where(low_half, re, im)
            return carry
        lax.fori_loop(first, last, back, 0)


def z_forward(unit_of, row, rows, v_ref, high_ref, low_ref, out_ref, w_ref):
    low_half = lax.broadcasted_iota(jnp.int32, (rows, 128), 1) < 64

    def group(r, carry):
        real, imag, mixed = (
            [v_ref[r * 4 + j, x, pl.ds(row, rows), :] for j in range(4)] for x in range(3)
        )
        p0r, p2r, p0i, p2i, p1r, p1i = [], [], [], [], [], []
        for source, first, second in ((real, p0r, p2r), (imag, p0i, p2i), (mixed, p1r, p1i)):
            for t in range(2):
                a, b = merge(source[2 * t], source[2 * t + 1], low_half)
                first.append(a)
                second.append(b)
        lines = jnp.concatenate(
            [jnp.concatenate(x, axis=1) for x in (p0r, p1r, p2r, p0i, p1i, p2i)], axis=0
        )
        high, low = parts_of(lines)
        cos, sin = (
            dot3(high, low, high_ref[r, :, at : at + ZS], low_ref[r, :, at : at + ZS], ((1,), (1,)))
            for at in (0, ZS)
        )
        w_ref[r, : 3 * rows, :ZS] = cos[: 3 * rows] + sin[3 * rows :]
        w_ref[r, : 3 * rows, ZS:] = cos[3 * rows :] - sin[: 3 * rows]
        return carry
    lax.fori_loop(0, ZR, group, 0, unroll=UNROLL_FWD)

    def body(i, carry):
        at = pl.multiple_of(i * UNIT, UNIT)
        along = unit_of(row // UNIT + i) * UNIT + lax.broadcasted_iota(jnp.int32, (UNIT, 128), 0)
        along = jnp.where(2 * along < NX, along, along - NX)
        wave_along = along.astype(jnp.float32) * (TWO_PI / NX)
        keep_along = 3 * jnp.abs(along) < NX
        for lane in range(0, ZS, 128):
            spectra = []
            for j in range(3):
                values = [
                    tuple(
                        w_ref[r, pl.ds(j * rows + at, UNIT), pl.ds(p * ZS + lane, 128)]
                        for p in range(2)
                    )
                    for r in range(ZR)
                ]
                spectra.append(small_dft(values, -1))
            for half, groups in enumerate((LOW, HIGH)):
                for place, a in enumerate(groups):
                    start = a * ZS + lane - (NZ if half else 0)
                    mode = start + lax.broadcasted_iota(jnp.int32, (UNIT, 128), 1)
                    wave_across = mode.astype(jnp.float32) * (TWO_PI / NZ)
                    keep = jnp.logical_and(3 * jnp.abs(mode) < NZ, keep_along)
                    (ar, ai), (br, bi), (cr, ci) = (x[a] for x in spectra)
                    terms = [
                        jnp.where(keep, wave_along * ai + wave_across * bi, 0.0),
                        jnp.where(keep, -(wave_along * ar + wave_across * br), 0.0),
                        jnp.where(keep, wave_along * bi + wave_across * ci, 0.0),
                        jnp.where(keep, -(wave_along * br + wave_across * cr), 0.0),
                    ]
                    for x in range(4):
                        out_ref[half, x, pl.ds(row + at, UNIT), pl.ds(place * ZS + lane, 128)] = terms[x]
        return carry
    lax.fori_loop(0, rows // UNIT, body, 0)


def substep_kernel(
    velocity_ref, tables_hbm, fh_hbm, fl_hbm,
    term_ref,
    rows_ref, zh_ref, zl_ref, ih_ref, il_ref, fh_ref, fl_ref,
    zth_ref, ztl_ref, out_ref, in_ref, th_ref, tl_ref, f_ref, back_ref, work_ref, w_ref,
    table_sems, own_sems, swap_send, swap_recv, out_send, out_recv, back_send, back_recv,
    res_send, res_recv,
):
    gx, gz = lax.axis_index("gx"), lax.axis_index("gz")
    count = 2 * XR
    me = 2 * gx + gz
    half = rows_ref.shape[2]
    offsets = [sum(CHUNKS[:c]) for c in range(len(CHUNKS))]

    def device(t):
        return (t // 2, lax.rem(t, 2))

    tables = [
        pltpu.make_async_copy(src, dst, table_sems.at[n])
        for n, (src, dst) in enumerate(
            (
                (tables_hbm.at[pl.ds(0, ZR)], zh_ref),
                (tables_hbm.at[pl.ds(ZR, ZR)], zl_ref),
                (tables_hbm.at[pl.ds(2 * ZR, XR)], ih_ref),
                (tables_hbm.at[pl.ds(2 * ZR + XR, XR)], il_ref),
                (fh_hbm, fh_ref),
                (fl_hbm, fl_ref),
            )
        )
    ]

    def load_own(c):
        return pltpu.make_async_copy(
            velocity_ref.at[:, pl.ds(pl.multiple_of(gz * half + offsets[c], 16), CHUNKS[c]), :],
            rows_ref.at[0, :, pl.ds(offsets[c], CHUNKS[c]), :],
            own_sems.at[c],
        )

    def swap(c):
        return pltpu.make_async_remote_copy(
            src_ref=velocity_ref.at[
                :, pl.ds(pl.multiple_of((1 - gz) * half + offsets[c], 16), CHUNKS[c]), :
            ],
            dst_ref=rows_ref.at[1, :, pl.ds(offsets[c], CHUNKS[c]), :],
            send_sem=swap_send.at[c],
            recv_sem=swap_recv.at[c],
            device_id=(gx, 1 - gz),
            device_id_type=pl.DeviceIdType.MESH,
        )

    for c in range(len(CHUNKS)):
        load_own(c).start()
    for table in tables[:2]:
        table.start()

    barrier = pltpu.get_barrier_semaphore()

    def greet(i, carry):
        pl.semaphore_signal(
            barrier,
            inc=1,
            device_id=device(lax.rem(me + i, count)),
            device_id_type=pl.DeviceIdType.MESH,
        )
        return carry

    lax.fori_loop(1, count, greet, 0)
    pl.semaphore_wait(barrier, count - 1)
    for c in range(len(CHUNKS)):
        swap(c).start()
    for table in tables[2:]:
        table.start()

    def ship(src_ref, dst_ref, sends, recvs, c, at, length):
        span = pl.ds(at, length)

        def copy(i):
            t = lax.rem(me + i, count)
            return pltpu.make_async_remote_copy(
                src_ref=src_ref.at[t, :, span, :],
                dst_ref=dst_ref.at[me, :, span, :],
                send_sem=sends.at[c, i],
                recv_sem=recvs.at[c, i],
                device_id=device(t),
                device_id_type=pl.DeviceIdType.MESH,
            )

        def local():
            return pltpu.make_async_copy(
                src_ref.at[me, :, span, :], dst_ref.at[me, :, span, :], recvs.at[c, 0]
            )

        return copy, local

    def takes(t, src_ref, dst_ref, sends, recvs, c, at, length):
        if dst_ref is not work_ref or at < SHORT * UNIT:
            return t >= 0
        g = t // 2
        return jnp.logical_and(g != 5, g != XR - 6)

    def ship_start(*args):
        copy, local = ship(*args)

        def start(i, carry):
            @pl.when(takes(lax.rem(me + i, count), *args))
            def _():
                copy(i).start()
            return carry

        lax.fori_loop(1, count, start, 0)

        @pl.when(takes(me, *args))
        def _():
            local().start()

    def ship_arrive(*args):
        copy, local = ship(*args)

        def wait(i, carry):
            copy(i).wait_recv()
            return carry

        lax.fori_loop(1, count, wait, 0)
        local().wait()

    def ship_leave(*args):
        copy, _ = ship(*args)

        def wait(i, carry):
            @pl.when(takes(lax.rem(me + i, count), *args))
            def _():
                copy(i).wait_send()
            return carry

        lax.fori_loop(1, count, wait, 0)

    def spread_args(c):
        return out_ref, in_ref, out_send, out_recv, c, offsets[c], CHUNKS[c]

    tables[0].wait()
    tables[1].wait()
    for c in range(len(CHUNKS)):
        load_own(c).wait()
        swap(c).wait_recv()
        z_inverse(
            gz == 0, rows_ref, offsets[c], CHUNKS[c],
            zh_ref, zl_ref, out_ref, zth_ref, ztl_ref,
        )
        ship_start(*spread_args(c))

    for c in range(len(CHUNKS)):
        ship_arrive(*spread_args(c))
        x_spread(in_ref, offsets[c], CHUNKS[c], th_ref, tl_ref)
        if c == len(CHUNKS) - 2:
            for table in tables[2:]:
                table.wait()
            x_early(4 * offsets[-1], ih_ref, il_ref, th_ref, tl_ref, f_ref)
    for c in range(len(CHUNKS)):
        ship_leave(*spread_args(c))
    x_products(
        4 * offsets[-1], ih_ref, il_ref, fh_ref, fl_ref, th_ref, tl_ref, f_ref, (out_ref, in_ref)
    )
    x_gather((out_ref, in_ref), back_ref)

    starts = [sum(SPANS[:c]) for c in range(len(SPANS))]

    def back_args(c):
        return back_ref, work_ref, back_send, back_recv, c, starts[c] * UNIT, SPANS[c] * UNIT

    for c in range(BACK_AHEAD):
        ship_start(*back_args(c))

    def result(u, side):
        unit = unit_at(gx, gz, u)
        owner = unit // PER
        slot = unit - owner * PER
        src = rows_ref.at[
            side, :, pl.ds(pl.multiple_of(u * UNIT, UNIT), UNIT), pl.ds(0, term_ref.shape[2])
        ]
        dst = term_ref.at[:, pl.ds(pl.multiple_of(slot * UNIT, UNIT), UNIT), :]
        here = jnp.logical_and(owner == gx, side == gz)

        def remote():
            return pltpu.make_async_remote_copy(
                src_ref=src,
                dst_ref=dst,
                send_sem=res_send.at[side, u],
                recv_sem=res_recv.at[slot],
                device_id=(owner, side),
                device_id_type=pl.DeviceIdType.MESH,
            )

        return here, remote, lambda: pltpu.make_async_copy(src, dst, res_recv.at[slot])

    def forward(c):
        ship_arrive(*back_args(c))
        unit, units = starts[c], SPANS[c]
        z_forward(
            functools.partial(unit_at, gx, gz), unit * UNIT, units * UNIT,
            work_ref, zh_ref, zl_ref, rows_ref, w_ref,
        )

        def send(n, carry):
            for side in range(2):
                here, remote, local = result(unit + n, side)

                @pl.when(here)
                def _():
                    local().start()

                @pl.when(jnp.logical_not(here))
                def _():
                    remote().start()
            return carry

        lax.fori_loop(0, units, send, 0)

    for c in range(len(SPANS)):
        @pl.when(takes(me, *back_args(c)))
        def _():
            forward(c)

        if c + BACK_AHEAD < len(SPANS):
            ship_start(*back_args(c + BACK_AHEAD))

    def sent(u, carry):
        for side in range(2):
            here, remote, _ = result(u, side)

            @pl.when(jnp.logical_not(here))
            def _():
                remote().wait_send()
        return carry

    def got(s, carry):
        unit = gx * PER + s

        @pl.when(jnp.logical_or(unit < NEEDED, unit >= XR * PER - NEEDED))
        def _():
            pltpu.make_async_copy(
                rows_ref.at[0, :, pl.ds(0, UNIT), pl.ds(0, term_ref.shape[2])],
                term_ref.at[:, pl.ds(pl.multiple_of(s * UNIT, UNIT), UNIT), :],
                res_recv.at[s],
            ).wait()
        return carry

    lax.fori_loop(0, PER, got, 0)
    short = jnp.logical_or(gx == 5, gx == XR - 6)
    lax.fori_loop(0, jnp.where(short, SHORT, UNITS), sent, 0)

    for c in range(len(CHUNKS)):
        swap(c).wait_send()
    for c in range(len(SPANS)):
        ship_leave(*back_args(c))


def advance_kernel(
    base_ref, v_ref, old_ref, term_ref, next_hbm, non_hbm, next_ref, non_ref, store_sems
):
    mode_count, extent = v_ref.shape[2:]
    lower = lax.axis_index("gz") == 0
    across = lax.axis_index("gz") * extent + lax.broadcasted_iota(jnp.int32, (1, extent), 1)
    wave_across = jnp.where(2 * across < NZ, across, across - NZ).astype(jnp.float32) * (TWO_PI / NZ)
    empty = jnp.zeros((UNIT, extent - term_ref.shape[2]), jnp.float32)

    def at(c):
        return pl.ds(pl.multiple_of(c * BLOCK, BLOCK), BLOCK)

    def stores(c):
        return (
            pltpu.make_async_copy(
                next_ref.at[:, :, at(c), :], next_hbm.at[:, :, at(c), :], store_sems.at[0, c]
            ),
            pltpu.make_async_copy(
                non_ref.at[:, :, at(c), :], non_hbm.at[:, :, at(c), :], store_sems.at[1, c]
            ),
        )

    def work(c, carry):
        def lines(i, carry):
            row = pl.multiple_of(c * BLOCK + i * UNIT, UNIT)
            start = lax.axis_index("gx") * XS + row
            active = jnp.logical_or(start < NEEDED * UNIT, start >= NX - NEEDED * UNIT)
            along = start + lax.broadcasted_iota(jnp.int32, (UNIT, 1), 0)
            wave_along = jnp.where(2 * along < NX, along, along - NX).astype(jnp.float32) * (TWO_PI / NX)
            damping = jnp.exp(-VISCOSITY * (wave_along * wave_along + wave_across * wave_across))
            shear = base_ref[0] * wave_along
            to = pl.ds(row, UNIT)
            for f in range(2):
                for p in range(2):
                    term = jnp.where(active, term_ref[2 * f + p, to, :], 0.0)
                    term = jnp.where(
                        lower,
                        jnp.concatenate([term, empty], axis=1),
                        jnp.concatenate([empty, term], axis=1),
                    )
                    other = shear * v_ref[f, 1 - p, to, :]
                    result = term + other if p == 0 else term - other
                    non_ref[f, p, to, :] = result
                    next_ref[f, p, to, :] = damping * (
                        v_ref[f, p, to, :]
                        + TIME_STEP * (GAMMA_NEW * result + ZETA_OLD * old_ref[f, p, to, :])
                    )
            return carry

        lax.fori_loop(0, BLOCK // UNIT, lines, 0)
        for store in stores(c):
            store.start()
        return carry

    lax.fori_loop(0, mode_count // BLOCK, work, 0)

    def end(c, carry):
        for store in stores(c):
            store.wait()
        return carry

    lax.fori_loop(0, mode_count // BLOCK, end, 0)


def lines_local(velocity, previous, base_flow):
    velocity, previous = velocity[:, :, 0], previous[:, :, 0]
    mode_count, extent = velocity.shape[2:]
    half = mode_count // 2
    rows = max(CHUNKS)
    f32, bf16 = jnp.float32, jnp.bfloat16
    zh, zl = z_table()
    xh, xl = x_inverse_table()
    fh, fl = x_forward_table()
    active = len(LOW) * ZS
    count = 2 * XR
    dma = pltpu.SemaphoreType.DMA

    term = pl.pallas_call(
        substep_kernel,
        out_shape=jax.ShapeDtypeStruct((4, mode_count, active), f32),
        in_specs=[pl.BlockSpec(memory_space=pl.ANY)] * 4,
        out_specs=pl.BlockSpec(memory_space=pl.ANY),
        scratch_shapes=[
            pltpu.VMEM((2, 4, half, extent), f32),
            pltpu.VMEM(zh.shape, bf16),
            pltpu.VMEM(zl.shape, bf16),
            pltpu.VMEM(xh.shape, bf16),
            pltpu.VMEM(xl.shape, bf16),
            pltpu.VMEM(fh.shape, bf16),
            pltpu.VMEM(fl.shape, bf16),
            pltpu.VMEM((ZR, 4 * rows, ZS), bf16),
            pltpu.VMEM((ZR, 4 * rows, ZS), bf16),
            pltpu.VMEM((count, 2, half, 128), f32),
            pltpu.VMEM((count, 2, half, 128), f32),
            pltpu.VMEM((XR, 2 * XS, 128), bf16),
            pltpu.VMEM((XR, 2 * XS, 128), bf16),
            pltpu.VMEM((XR, XS, 128), f32),
            pltpu.VMEM((count, 3, UNITS * UNIT, 128), f32),
            pltpu.VMEM((count, 3, UNITS * UNIT, 128), f32),
            pltpu.VMEM((ZR, 3 * max(SPANS) * UNIT, 2 * ZS), f32),
            dma((6,)),
            dma((len(CHUNKS),)),
            dma((len(CHUNKS),)),
            dma((len(CHUNKS),)),
            dma((len(CHUNKS), count)),
            dma((len(CHUNKS), count)),
            dma((len(SPANS), count)),
            dma((len(SPANS), count)),
            dma((2, UNITS)),
            dma((PER,)),
        ],
        compiler_params=pltpu.CompilerParams(
            collective_id=1, has_side_effects=True, vmem_limit_bytes=int(SUB_VMEM * MIB)
        ),
        cost_estimate=pl.CostEstimate(
            flops=10**10, bytes_accessed=64 * velocity.size, transcendentals=0
        ),
        name="substep",
    )(velocity.reshape(4, mode_count, extent), np.concatenate([zh, zl, xh, xl]), fh, fl)

    field = pltpu.VMEM(velocity.shape, f32)
    blocks = mode_count // BLOCK
    advanced, nonlinear = pl.pallas_call(
        advance_kernel,
        out_shape=[jax.ShapeDtypeStruct(velocity.shape, f32)] * 2,
        in_specs=[pl.BlockSpec(memory_space=pltpu.SMEM)] + [pl.BlockSpec(memory_space=pltpu.VMEM)] * 3,
        out_specs=[pl.BlockSpec(memory_space=pl.ANY)] * 2,
        scratch_shapes=[
            field,
            field,
            dma((2, blocks)),
        ],
        compiler_params=pltpu.CompilerParams(vmem_limit_bytes=ADV_VMEM * MIB),
        name="advance",
    )(
        base_flow,
        velocity,
        previous,
        term,
    )
    return advanced[:, :, None], nonlinear[:, :, None]


def solution(mesh):
    in_specs = (P(None, None, None, "gx", "gz"), P(None, None, None, "gx", "gz"), P())
    out_specs = (P(None, None, None, "gx", "gz"), P(None, None, None, "gx", "gz"))
    fits = mesh.shape["gx"] == XR and mesh.shape["gz"] == 2
    work = lines_local if fits else local
    return jax.shard_map(work, mesh=mesh, in_specs=in_specs, out_specs=out_specs, check_vma=False)
```

```python
import functools
import math

import jax
import jax.numpy as jnp
import numpy as np
from jax import lax
from jax.experimental import pallas as pl
from jax.experimental.pallas import tpu as pltpu
from jax.sharding import PartitionSpec as P

NX = 4096
NZ = 2048


TWO_PI = 2.0 * math.pi
VISCOSITY = 0.05
TIME_STEP = 0.2
GAMMA_NEW = 8.0 / 15.0
ZETA_OLD = -17.0 / 60.0


def partner_2(x, axis, distance):
    return lax.ppermute(x, axis, [(i, i ^ 1 << distance) for i in range(lax.axis_size(axis))])


def exact_einsum(pattern, left_array, right_array):
    return jnp.einsum(
        pattern,
        left_array,
        right_array,
        precision=lax.Precision.HIGHEST,
        preferred_element_type=jnp.float32,
    )


def phase_table(left_ints, right_ints, period, direction):
    phase_angle = (
        direction * TWO_PI / period * (left_ints * right_ints % period).astype(jnp.float32)
    )
    return (jnp.cos(phase_angle), jnp.sin(phase_angle))


def complex_apply(value_real, value_imag, table_real, table_imag, pattern):
    out_real = exact_einsum(pattern, value_real, table_real) - exact_einsum(
        pattern, value_imag, table_imag
    )
    out_imag = exact_einsum(pattern, value_real, table_imag) + exact_einsum(
        pattern, value_imag, table_real
    )
    return (out_real, out_imag)


def residue_of(position, levels):
    reversed_bits = jnp.zeros((), jnp.int32)
    for level in range(levels):
        reversed_bits = reversed_bits + ((position >> level & 1) << levels - 1 - level)
    return reversed_bits


def section_twiddle(position, half_span):
    phase_angle = TWO_PI / (2 * half_span) * (position % half_span).astype(jnp.float32)
    return (jnp.cos(phase_angle), jnp.sin(phase_angle))


def spread_butterfly(values):
    position = lax.axis_index("gx")
    levels = lax.axis_size("gx").bit_length() - 1
    for level in reversed(range(levels)):
        half_span = 1 << level
        partner = partner_2(values, "gx", level)
        upper_half = position >> level & 1 == 1
        cosine, sine_part = section_twiddle(position, half_span)
        difference = partner - values
        rotated = jnp.stack(
            [
                difference[:, 0] * cosine - difference[:, 1] * sine_part,
                difference[:, 0] * sine_part + difference[:, 1] * cosine,
            ],
            axis=1,
        )
        values = jnp.where(upper_half, rotated, values + partner)
    return (values, residue_of(position, levels))


def gather_butterfly(values):
    position = lax.axis_index("gx")
    levels = lax.axis_size("gx").bit_length() - 1
    for level in range(levels):
        half_span = 1 << level
        partner = partner_2(values, "gx", level)
        upper_half = position >> level & 1 == 1
        cosine, sine_part = section_twiddle(position, half_span)
        upper_item = jnp.where(upper_half, values, partner)
        lower_item = jnp.where(upper_half, partner, values)
        turned = jnp.stack(
            [
                upper_item[:, 0] * cosine + upper_item[:, 1] * sine_part,
                upper_item[:, 1] * cosine - upper_item[:, 0] * sine_part,
            ],
            axis=1,
        )
        values = jnp.where(upper_half, lower_item - turned, lower_item + turned)
    return values


def axial_table(residue, mode_count, device_count):
    numbers = jnp.arange(mode_count, dtype=jnp.int32)
    points = residue + device_count * numbers
    cosine, sine_part = phase_table(points[:, None], numbers[None, :], NX, 1.0)
    norm_scale = 1.0 / math.sqrt(NX)
    return (cosine * norm_scale, sine_part * norm_scale)


def span_table(groups, span_size):
    residues = jnp.arange(groups, dtype=jnp.int32)[:, None, None]
    grid_rows = jnp.arange(span_size, dtype=jnp.int32)[None, :, None]
    mode_cols = jnp.arange(span_size, dtype=jnp.int32)[None, None, :]
    cosine, sine_part = phase_table(mode_cols, residues + groups * grid_rows, NZ, 1.0)
    norm_scale = 1.0 / math.sqrt(NZ)
    return (cosine * norm_scale, sine_part * norm_scale)


def spanwise_work(received):
    fields, pair_size, planes, row_count, extent = received.shape
    groups = lax.axis_size("gz")
    span_size = extent // groups
    blocks = received.reshape(fields, pair_size, planes, row_count, groups, span_size)
    group_ids = jnp.arange(groups, dtype=jnp.int32)
    mix_real, mix_imag = phase_table(group_ids[:, None], group_ids[None, :], groups, 1.0)
    section_real, section_imag = complex_apply(
        blocks[:, 0], blocks[:, 1], mix_real, mix_imag, "fylcj,rc->fylrj"
    )
    table_real, table_imag = span_table(groups, span_size)
    physical = exact_einsum("fylrj,rtj->fylrt", section_real, table_real) - exact_einsum(
        "fylrj,rtj->fylrt", section_imag, table_imag
    )
    products = jnp.stack(
        [physical[0] * physical[0], physical[0] * physical[1], physical[1] * physical[1]]
    )
    back_real = exact_einsum("pylrt,rtj->pylrj", products, table_real)
    back_imag = -exact_einsum("pylrt,rtj->pylrj", products, table_imag)
    out_real, out_imag = complex_apply(back_real, back_imag, mix_real, -mix_imag, "pylrj,cr->pylcj")
    spectra = jnp.stack([out_real, out_imag], axis=1)
    return spectra.reshape(3, pair_size, planes, row_count, extent)


def span_round(values, work):
    span_spectra = work(lax.all_to_all(values, "gz", split_axis=3, concat_axis=4, tiled=True))
    return lax.all_to_all(span_spectra, "gz", split_axis=4, concat_axis=3, tiled=True)


def signed_block(start, mode_count, extent):
    numbers = start + jnp.arange(mode_count, dtype=jnp.int32)
    return jnp.where(2 * numbers < extent, numbers, numbers - extent)


def local(velocity, previous, base_flow):
    mode_count = velocity.shape[3]
    span_size = velocity.shape[4]
    device_count = lax.axis_size("gx")
    spread, residue = spread_butterfly(velocity)
    table_real, table_imag = axial_table(residue, mode_count, device_count)
    along_real, along_imag = complex_apply(
        spread[:, 0], spread[:, 1], table_real, table_imag, "fymq,sm->fysq"
    )
    physical_along = jnp.stack([along_real, along_imag], axis=1)
    returned = span_round(physical_along, spanwise_work)
    local_real, local_imag = complex_apply(
        returned[:, 0], returned[:, 1], table_real.T, -table_imag.T, "fysq,ms->fymq"
    )
    local_spectra = jnp.stack([local_real, local_imag], axis=1)
    product_spectra = gather_butterfly(local_spectra)
    modes_along = signed_block(lax.axis_index("gx") * mode_count, mode_count, NX)
    modes_across = signed_block(lax.axis_index("gz") * span_size, span_size, NZ)
    wave_along = (modes_along.astype(jnp.float32) * (TWO_PI / NX))[:, None]
    wave_across = (modes_across.astype(jnp.float32) * (TWO_PI / NZ))[None, :]
    keep = jnp.logical_and(
        (3 * jnp.abs(modes_along) < NX)[:, None], (3 * jnp.abs(modes_across) < NZ)[None, :]
    ).astype(jnp.float32)
    shear = base_flow[:, None, None] * wave_along[None]
    prod_real = product_spectra[:, 0]
    prod_imag = product_spectra[:, 1]
    first_real = (
        keep * (wave_along * prod_imag[0] + wave_across * prod_imag[1]) + shear * velocity[0, 1]
    )
    first_imag = (
        -keep * (wave_along * prod_real[0] + wave_across * prod_real[1]) - shear * velocity[0, 0]
    )
    second_real = (
        keep * (wave_along * prod_imag[1] + wave_across * prod_imag[2]) + shear * velocity[1, 1]
    )
    second_imag = (
        -keep * (wave_along * prod_real[1] + wave_across * prod_real[2]) - shear * velocity[1, 0]
    )
    nonlinear = jnp.stack(
        [jnp.stack([first_real, first_imag]), jnp.stack([second_real, second_imag])]
    )
    damping = jnp.exp(-VISCOSITY * (wave_along * wave_along + wave_across * wave_across))
    advanced = damping * (velocity + TIME_STEP * (GAMMA_NEW * nonlinear + ZETA_OLD * previous))
    return (advanced, nonlinear)


XR = 16
XS = NX // XR
ZR = 8
ZS = NZ // ZR
LOW = (0, 1, 2)
HIGH = (5, 6, 7)
MIB = 1 << 20
CHUNKS = (16,) * 8
UNIT = 8
UNITS = 11
SIDE = 16 * UNITS
PER = XS // UNIT
OWN = 2 * UNITS
EXTRA = PER - OWN
SPANS = (3, 3, 3, 1, 1)
BACK_AHEAD = 3
UNROLL = 16
UNROLL_INV = 8
UNROLL_FWD = 8
UNROLL_EARLY = 4
BLOCK = 32
SUB_VMEM = 49
ADV_VMEM = 40
SHORT = 9
NEEDED = SIDE - 4


def split_table(table):
    high = table.astype(np.float32).astype(jnp.bfloat16)
    low = (table - high.astype(np.float64)).astype(np.float32).astype(jnp.bfloat16)
    return high, low


def z_table():
    r = np.arange(ZR)[:, None, None]
    b = np.arange(ZS)[None, :, None]
    s = np.arange(ZS)[None, None, :]
    angle = TWO_PI / NZ * ((b * (r + ZR * s)) % NZ)
    cos, sin = np.cos(angle) / math.sqrt(NZ), np.sin(angle) / math.sqrt(NZ)
    return split_table(np.concatenate([cos, sin], axis=2))


def x_table():
    r = np.arange(XR)[:, None, None]
    s = np.arange(XS)[None, :, None]
    m = np.arange(XS)[None, None, :]
    angle = TWO_PI / NX * ((m * (r + XR * s)) % NX)
    cos, sin = np.cos(angle) / math.sqrt(NX), np.sin(angle) / math.sqrt(NX)
    return np.stack([cos, -sin], axis=2)


def x_inverse_table():
    table = x_table().reshape(XR, XS, 4, XS // 2)
    parts = []
    for c, length in enumerate(CHUNKS):
        start = sum(CHUNKS[:c])
        parts.append(table[..., start : start + length].reshape(XR, XS, 4 * length))
    return split_table(np.concatenate(parts, axis=2))


def x_forward_table():
    return split_table(np.swapaxes(x_table().reshape(XR, XS, 2 * XS), 1, 2))


def turn(value, numerator, size, sign):
    re, im = value
    numerator = numerator % size
    if numerator == 0:
        return re, im
    if 4 * numerator == size:
        return (-im, re) if sign > 0 else (im, -re)
    if 8 * numerator == size:
        h = math.sqrt(0.5)
        return ((re - im) * h, (re + im) * h) if sign > 0 else ((re + im) * h, (im - re) * h)
    if 8 * numerator == 3 * size:
        h = math.sqrt(0.5)
        return ((-re - im) * h, (re - im) * h) if sign > 0 else ((im - re) * h, (-re - im) * h)
    c = math.cos(TWO_PI * numerator / size)
    s = sign * math.sin(TWO_PI * numerator / size)
    return re * c - im * s, re * s + im * c


def small_dft(values, sign):
    size = len(values)
    if size == 1:
        return values
    even = small_dft(values[0::2], sign)
    odd = small_dft(values[1::2], sign)
    half = size // 2
    out = [None] * size
    for i in range(half):
        re, im = turn(odd[i], i, size, sign)
        out[i] = (even[i][0] + re, even[i][1] + im)
        out[i + half] = (even[i][0] - re, even[i][1] - im)
    return out


def parts_of(value):
    high = value.astype(jnp.bfloat16)
    return high, (value - high.astype(jnp.float32)).astype(jnp.bfloat16)


def dot3(a_high, a_low, b_high, b_low, dims):
    def dot(a, b):
        return lax.dot_general(a, b, (dims, ((), ())), preferred_element_type=jnp.float32)

    return dot(a_high, b_high) + (dot(a_high, b_low) + dot(a_low, b_high))


def merge(first, second, low_half):
    return (
        jnp.where(low_half, first, pltpu.roll(second, 64, 1)),
        jnp.where(low_half, pltpu.roll(first, 64, 1), second),
    )


def z_inverse(first, rows_ref, row, rows, high_ref, low_ref, out_ref, th_ref, tl_ref):
    step = 16
    for c in range(2):
        def body(i, carry):
            at = pl.multiple_of(i * step, step)
            for lane in range(0, ZS, 128):
                values = [None] * ZR
                for a in range(ZR // 2):
                    to = (pl.ds(row + at, step), pl.ds(a * ZS + lane, 128))
                    own = [rows_ref[(0, 2 * c + p) + to] for p in range(2)]
                    other = [rows_ref[(1, 2 * c + p) + to] for p in range(2)]
                    values[a] = tuple(jnp.where(first, x, y) for x, y in zip(own, other))
                    values[a + ZR // 2] = tuple(jnp.where(first, y, x) for x, y in zip(own, other))
                for r, pair in enumerate(small_dft(values, 1)):
                    for p in range(2):
                        high, low = parts_of(pair[p])
                        line = pl.ds((2 * p + c) * rows + at, step)
                        th_ref[r, line, pl.ds(lane, 128)] = high
                        tl_ref[r, line, pl.ds(lane, 128)] = low
            return carry
        lax.fori_loop(0, rows // step, body, 0)

    def group(r, carry):
        both = dot3(
            th_ref[r, : 4 * rows], tl_ref[r, : 4 * rows], high_ref[r], low_ref[r], ((1,), (0,))
        )
        real, imag = both[: 2 * rows], both[2 * rows :]
        done = jnp.concatenate(
            [real[:, :ZS] - imag[:, ZS:], real[:, ZS:] + imag[:, :ZS]], axis=1
        )
        low_half = lax.broadcasted_iota(jnp.int32, (rows, 128), 1) < 64
        for p in range(2):
            for t in range(2):
                at = p * ZS + t * 128
                even, odd = merge(done[:rows, at : at + 128], done[rows:, at : at + 128], low_half)
                out_ref[r * 4 + 2 * t, p, pl.ds(row, rows), :] = even
                out_ref[r * 4 + 2 * t + 1, p, pl.ds(row, rows), :] = odd
        return carry
    lax.fori_loop(0, ZR, group, 0, unroll=UNROLL_INV)


def x_spread(v_ref, row, rows, th_ref, tl_ref):
    step = 16
    for r in range(2):
        def body(i, carry):
            at = pl.multiple_of(i * step, step)
            values = [
                tuple(v_ref[2 * g + r, p, pl.ds(row + at, step), :] for p in range(2))
                for g in range(XR)
            ]
            for res, pair in enumerate(small_dft(values, 1)):
                for p in range(2):
                    high, low = parts_of(pair[p])
                    line = pl.ds(4 * row + (2 * p + r) * rows + at, step)
                    th_ref[res, line, :] = high
                    tl_ref[res, line, :] = low
            return carry
        lax.fori_loop(0, rows // step, body, 0)


def x_early(lines, ih_ref, il_ref, th_ref, tl_ref, f_ref):
    def residue(res, carry):
        f_ref[res] = dot3(
            ih_ref[res, :, :lines], il_ref[res, :, :lines],
            th_ref[res, :lines], tl_ref[res, :lines], ((1,), (0,)),
        )
        return carry
    lax.fori_loop(0, XR, residue, 0, unroll=UNROLL_EARLY)


def x_products(lines, ih_ref, il_ref, fh_ref, fl_ref, th_ref, tl_ref, f_ref, u_refs):
    def residue(res, carry):
        field = f_ref[res] + dot3(
            ih_ref[res, :, lines:], il_ref[res, :, lines:],
            th_ref[res, lines:], tl_ref[res, lines:], ((1,), (0,)),
        )
        swapped = pltpu.roll(field, 64, 1)
        products = jnp.concatenate([field * field, field * swapped], axis=1)
        high, low = parts_of(products)
        both = dot3(fh_ref[res], fl_ref[res], high, low, ((1,), (0,)))
        half = XS // 2
        for h, u_ref in enumerate(u_refs):
            for p in range(2):
                for r in range(2):
                    at = p * XS + r * half
                    u_ref[2 * res + p, r] = both[at : at + half, h * 128 : h * 128 + 128]
        return carry
    lax.fori_loop(0, XR, residue, 0, unroll=UNROLL)


def place_of(o, s):
    e = s - OWN
    if o < 2:
        e = e + o * EXTRA
        m = jnp.where(s < OWN, o, jnp.where(e < 14, 4, 5))
        n = jnp.where(s < OWN, s, jnp.where(e < 14, e, e - 14))
    elif o < 4:
        e = e + (o - 2) * EXTRA
        m = jnp.where(s < OWN, o, 6 + lax.rem(e, 2))
        n = jnp.where(s < OWN, s, e // 2)
    elif o == 4:
        e = s + 12
        m = jnp.where(s < 8, 4, 6 + lax.rem(e, 2))
        n = jnp.where(s < 8, s + 14, e // 2)
    else:
        m, n = 5, s + 6
    return m, lax.rem(n, 2), n // 2


def unit_at(gx, gz, u):
    right = gx >= XR // 2
    m = jnp.where(right, XR - 1 - gx, gx)
    n = 2 * u + gz
    e = jnp.where(m == 4, n, jnp.where(m == 5, n + 14, 2 * n + m - 6))
    upper = e >= EXTRA
    helps = jnp.where(m == 4, n < 14, jnp.where(m == 5, n < 6, e < 2 * EXTRA))
    owner = jnp.where(upper, 1, 0) + jnp.where(m >= 6, 2, 0)
    own_slot = jnp.where(m == 4, n - 14, jnp.where(m == 5, n - 6, e - 12))
    o = jnp.where(m < 4, m, jnp.where(helps, owner, jnp.where(m == 5, 5, 4)))
    s = jnp.where(
        m < 4, n, jnp.where(helps, OWN + e - jnp.where(upper, EXTRA, 0), own_slot)
    )
    unit = o * PER + s
    return jnp.where(right, XR * PER - 1 - unit, unit)


def x_gather(u_refs, out_ref):
    low_half = lax.broadcasted_iota(jnp.int32, (UNIT, 128), 1) < 64
    split = SIDE % PER
    for first, last in ((0, split), (split, PER)):
        def back(i, carry):
            part = i * UNIT // (XS // 2)
            at = pl.multiple_of(i * UNIT - part * (XS // 2), UNIT)
            for h in range(2):
                values = [
                    tuple(
                        u_refs[h][2 * res + p, part, pl.ds(at, UNIT), :]
                        for p in range(2)
                    )
                    for res in range(XR)
                ]
                for g, (re, im) in enumerate(small_dft(values, -1)):
                    if g * PER + first < SIDE:
                        m, side, u = place_of(g, i)
                    elif (XR - g) * PER - last < SIDE:
                        m, side, u = place_of(XR - 1 - g, PER - 1 - i)
                        m = XR - 1 - m
                    else:
                        continue
                    worker = 2 * m + side
                    line = pl.ds(pl.multiple_of(u * UNIT, UNIT), UNIT)
                    if h == 0:
                        out_ref[worker, 0, line, :] = re
                        out_ref[worker, 1, line, :] = im
                    else:
                        out_ref[worker, 2, line, :] = jnp.where(low_half, re, im)
            return carry
        lax.fori_loop(first, last, back, 0)


def z_forward(unit_of, row, rows, v_ref, high_ref, low_ref, out_ref, w_ref):
    low_half = lax.broadcasted_iota(jnp.int32, (rows, 128), 1) < 64

    def group(r, carry):
        real, imag, mixed = (
            [v_ref[r * 4 + j, x, pl.ds(row, rows), :] for j in range(4)] for x in range(3)
        )
        p0r, p2r, p0i, p2i, p1r, p1i = [], [], [], [], [], []
        for source, first, second in ((real, p0r, p2r), (imag, p0i, p2i), (mixed, p1r, p1i)):
            for t in range(2):
                a, b = merge(source[2 * t], source[2 * t + 1], low_half)
                first.append(a)
                second.append(b)
        lines = jnp.concatenate(
            [jnp.concatenate(x, axis=1) for x in (p0r, p1r, p2r, p0i, p1i, p2i)], axis=0
        )
        high, low = parts_of(lines)
        cos, sin = (
            dot3(high, low, high_ref[r, :, at : at + ZS], low_ref[r, :, at : at + ZS], ((1,), (1,)))
            for at in (0, ZS)
        )
        w_ref[r, : 3 * rows, :ZS] = cos[: 3 * rows] + sin[3 * rows :]
        w_ref[r, : 3 * rows, ZS:] = cos[3 * rows :] - sin[: 3 * rows]
        return carry
    lax.fori_loop(0, ZR, group, 0, unroll=UNROLL_FWD)

    def body(i, carry):
        at = pl.multiple_of(i * UNIT, UNIT)
        along = unit_of(row // UNIT + i) * UNIT + lax.broadcasted_iota(jnp.int32, (UNIT, 128), 0)
        along = jnp.where(2 * along < NX, along, along - NX)
        wave_along = along.astype(jnp.float32) * (TWO_PI / NX)
        keep_along = 3 * jnp.abs(along) < NX
        for lane in range(0, ZS, 128):
            spectra = []
            for j in range(3):
                values = [
                    tuple(
                        w_ref[r, pl.ds(j * rows + at, UNIT), pl.ds(p * ZS + lane, 128)]
                        for p in range(2)
                    )
                    for r in range(ZR)
                ]
                spectra.append(small_dft(values, -1))
            for half, groups in enumerate((LOW, HIGH)):
                for place, a in enumerate(groups):
                    start = a * ZS + lane - (NZ if half else 0)
                    mode = start + lax.broadcasted_iota(jnp.int32, (UNIT, 128), 1)
                    wave_across = mode.astype(jnp.float32) * (TWO_PI / NZ)
                    keep = jnp.logical_and(3 * jnp.abs(mode) < NZ, keep_along)
                    (ar, ai), (br, bi), (cr, ci) = (x[a] for x in spectra)
                    terms = [
                        jnp.where(keep, wave_along * ai + wave_across * bi, 0.0),
                        jnp.where(keep, -(wave_along * ar + wave_across * br), 0.0),
                        jnp.where(keep, wave_along * bi + wave_across * ci, 0.0),
                        jnp.where(keep, -(wave_along * br + wave_across * cr), 0.0),
                    ]
                    for x in range(4):
                        out_ref[half, x, pl.ds(row + at, UNIT), pl.ds(place * ZS + lane, 128)] = terms[x]
        return carry
    lax.fori_loop(0, rows // UNIT, body, 0)


def substep_kernel(
    velocity_ref, tables_hbm, fh_hbm, fl_hbm,
    term_ref,
    rows_ref, zh_ref, zl_ref, ih_ref, il_ref, fh_ref, fl_ref,
    zth_ref, ztl_ref, out_ref, in_ref, th_ref, tl_ref, f_ref, back_ref, work_ref, w_ref,
    table_sems, own_sems, swap_send, swap_recv, out_send, out_recv, back_send, back_recv,
    res_send, res_recv,
):
    gx, gz = lax.axis_index("gx"), lax.axis_index("gz")
    count = 2 * XR
    me = 2 * gx + gz
    half = rows_ref.shape[2]
    offsets = [sum(CHUNKS[:c]) for c in range(len(CHUNKS))]

    def device(t):
        return (t // 2, lax.rem(t, 2))

    tables = [
        pltpu.make_async_copy(src, dst, table_sems.at[n])
        for n, (src, dst) in enumerate(
            (
                (tables_hbm.at[pl.ds(0, ZR)], zh_ref),
                (tables_hbm.at[pl.ds(ZR, ZR)], zl_ref),
                (tables_hbm.at[pl.ds(2 * ZR, XR)], ih_ref),
                (tables_hbm.at[pl.ds(2 * ZR + XR, XR)], il_ref),
                (fh_hbm, fh_ref),
                (fl_hbm, fl_ref),
            )
        )
    ]

    def load_own(c):
        return pltpu.make_async_copy(
            velocity_ref.at[:, pl.ds(pl.multiple_of(gz * half + offsets[c], 16), CHUNKS[c]), :],
            rows_ref.at[0, :, pl.ds(offsets[c], CHUNKS[c]), :],
            own_sems.at[c],
        )

    def swap(c):
        return pltpu.make_async_remote_copy(
            src_ref=velocity_ref.at[
                :, pl.ds(pl.multiple_of((1 - gz) * half + offsets[c], 16), CHUNKS[c]), :
            ],
            dst_ref=rows_ref.at[1, :, pl.ds(offsets[c], CHUNKS[c]), :],
            send_sem=swap_send.at[c],
            recv_sem=swap_recv.at[c],
            device_id=(gx, 1 - gz),
            device_id_type=pl.DeviceIdType.MESH,
        )

    for c in range(len(CHUNKS)):
        load_own(c).start()
    for table in tables[:2]:
        table.start()

    barrier = pltpu.get_barrier_semaphore()

    def greet(i, carry):
        pl.semaphore_signal(
            barrier,
            inc=1,
            device_id=device(lax.rem(me + i, count)),
            device_id_type=pl.DeviceIdType.MESH,
        )
        return carry

    lax.fori_loop(1, count, greet, 0)
    pl.semaphore_wait(barrier, count - 1)
    for c in range(len(CHUNKS)):
        swap(c).start()
    for table in tables[2:]:
        table.start()

    def target(i, c):
        return lax.rem(me + jnp.where(me < XR, i, 2 * XR - i), count)

    def ship(src_ref, dst_ref, sends, recvs, c, at, length):
        span = pl.ds(at, length)

        def copy(i):
            t = target(i, c)
            return pltpu.make_async_remote_copy(
                src_ref=src_ref.at[t, :, span, :],
                dst_ref=dst_ref.at[me, :, span, :],
                send_sem=sends.at[c, i],
                recv_sem=recvs.at[c, me],
                device_id=device(t),
                device_id_type=pl.DeviceIdType.MESH,
            )

        def local():
            return pltpu.make_async_copy(
                src_ref.at[me, :, span, :], dst_ref.at[me, :, span, :], recvs.at[c, me]
            )

        return copy, local

    def takes(t, src_ref, dst_ref, sends, recvs, c, at, length):
        if dst_ref is not work_ref or at < SHORT * UNIT:
            return t >= 0
        g = t // 2
        return jnp.logical_and(g != 5, g != XR - 6)

    def goes(t, *args):
        return jnp.logical_and(t != me, takes(t, *args))

    def ship_start(*args):
        copy, local = ship(*args)

        def start(i, carry):
            @pl.when(goes(target(i, args[4]), *args))
            def _():
                copy(i).start()
            return carry

        lax.fori_loop(0, count, start, 0)

        @pl.when(takes(me, *args))
        def _():
            local().start()

    def ship_arrive(src_ref, dst_ref, sends, recvs, c, at, length):
        span = pl.ds(at, length)
        _, local = ship(src_ref, dst_ref, sends, recvs, c, at, length)

        def wait(i, carry):
            t = lax.rem(me + i, count)
            pltpu.make_async_copy(
                src_ref.at[t, :, span, :], dst_ref.at[t, :, span, :], recvs.at[c, t]
            ).wait()
            return carry

        lax.fori_loop(1, count, wait, 0)
        local().wait()

    def ship_leave(*args):
        copy, _ = ship(*args)

        def wait(i, carry):
            @pl.when(goes(target(i, args[4]), *args))
            def _():
                copy(i).wait_send()
            return carry

        lax.fori_loop(0, count, wait, 0)

    def spread_args(c):
        return out_ref, in_ref, out_send, out_recv, c, offsets[c], CHUNKS[c]

    tables[0].wait()
    tables[1].wait()
    for c in range(len(CHUNKS)):
        load_own(c).wait()
        swap(c).wait_recv()
        z_inverse(
            gz == 0, rows_ref, offsets[c], CHUNKS[c],
            zh_ref, zl_ref, out_ref, zth_ref, ztl_ref,
        )
        ship_start(*spread_args(c))

    for c in range(len(CHUNKS)):
        ship_arrive(*spread_args(c))
        x_spread(in_ref, offsets[c], CHUNKS[c], th_ref, tl_ref)
        if c == len(CHUNKS) - 2:
            for table in tables[2:]:
                table.wait()
            x_early(4 * offsets[-1], ih_ref, il_ref, th_ref, tl_ref, f_ref)
    for c in range(len(CHUNKS)):
        ship_leave(*spread_args(c))
    x_products(
        4 * offsets[-1], ih_ref, il_ref, fh_ref, fl_ref, th_ref, tl_ref, f_ref, (out_ref, in_ref)
    )
    x_gather((out_ref, in_ref), back_ref)

    starts = [sum(SPANS[:c]) for c in range(len(SPANS))]

    def back_args(c):
        return back_ref, work_ref, back_send, back_recv, c, starts[c] * UNIT, SPANS[c] * UNIT

    for c in range(BACK_AHEAD):
        ship_start(*back_args(c))

    def result(u, side):
        unit = unit_at(gx, gz, u)
        owner = unit // PER
        slot = unit - owner * PER
        src = rows_ref.at[
            side, :, pl.ds(pl.multiple_of(u * UNIT, UNIT), UNIT), pl.ds(0, term_ref.shape[2])
        ]
        dst = term_ref.at[:, pl.ds(pl.multiple_of(slot * UNIT, UNIT), UNIT), :]
        here = jnp.logical_and(owner == gx, side == gz)

        def remote():
            return pltpu.make_async_remote_copy(
                src_ref=src,
                dst_ref=dst,
                send_sem=res_send.at[side, u],
                recv_sem=res_recv.at[slot],
                device_id=(owner, side),
                device_id_type=pl.DeviceIdType.MESH,
            )

        return here, remote, lambda: pltpu.make_async_copy(src, dst, res_recv.at[slot])

    def forward(c):
        ship_arrive(*back_args(c))
        unit, units = starts[c], SPANS[c]
        z_forward(
            functools.partial(unit_at, gx, gz), unit * UNIT, units * UNIT,
            work_ref, zh_ref, zl_ref, rows_ref, w_ref,
        )

        def send(n, carry):
            for side in range(2):
                here, remote, local = result(unit + n, side)

                @pl.when(here)
                def _():
                    local().start()

                @pl.when(jnp.logical_not(here))
                def _():
                    remote().start()
            return carry

        lax.fori_loop(0, units, send, 0)

    for c in range(len(SPANS)):
        @pl.when(takes(me, *back_args(c)))
        def _():
            forward(c)

        if c + BACK_AHEAD < len(SPANS):
            ship_start(*back_args(c + BACK_AHEAD))

    def sent(u, carry):
        for side in range(2):
            here, remote, _ = result(u, side)

            @pl.when(jnp.logical_not(here))
            def _():
                remote().wait_send()
        return carry

    def got(s, carry):
        unit = gx * PER + s

        @pl.when(jnp.logical_or(unit < NEEDED, unit >= XR * PER - NEEDED))
        def _():
            pltpu.make_async_copy(
                rows_ref.at[0, :, pl.ds(0, UNIT), pl.ds(0, term_ref.shape[2])],
                term_ref.at[:, pl.ds(pl.multiple_of(s * UNIT, UNIT), UNIT), :],
                res_recv.at[s],
            ).wait()
        return carry

    lax.fori_loop(0, PER, got, 0)
    short = jnp.logical_or(gx == 5, gx == XR - 6)
    lax.fori_loop(0, jnp.where(short, SHORT, UNITS), sent, 0)

    for c in range(len(CHUNKS)):
        swap(c).wait_send()
    for c in range(len(SPANS)):
        ship_leave(*back_args(c))


def advance_kernel(
    base_ref, v_ref, old_ref, term_ref, next_hbm, non_hbm, next_ref, non_ref, store_sems
):
    mode_count, extent = v_ref.shape[2:]
    lower = lax.axis_index("gz") == 0
    across = lax.axis_index("gz") * extent + lax.broadcasted_iota(jnp.int32, (1, extent), 1)
    wave_across = jnp.where(2 * across < NZ, across, across - NZ).astype(jnp.float32) * (TWO_PI / NZ)
    empty = jnp.zeros((UNIT, extent - term_ref.shape[2]), jnp.float32)

    def at(c):
        return pl.ds(pl.multiple_of(c * BLOCK, BLOCK), BLOCK)

    def stores(c):
        return (
            pltpu.make_async_copy(
                next_ref.at[:, :, at(c), :], next_hbm.at[:, :, at(c), :], store_sems.at[0, c]
            ),
            pltpu.make_async_copy(
                non_ref.at[:, :, at(c), :], non_hbm.at[:, :, at(c), :], store_sems.at[1, c]
            ),
        )

    def work(c, carry):
        def lines(i, carry):
            row = pl.multiple_of(c * BLOCK + i * UNIT, UNIT)
            start = lax.axis_index("gx") * XS + row
            active = jnp.logical_or(start < NEEDED * UNIT, start >= NX - NEEDED * UNIT)
            along = start + lax.broadcasted_iota(jnp.int32, (UNIT, 1), 0)
            wave_along = jnp.where(2 * along < NX, along, along - NX).astype(jnp.float32) * (TWO_PI / NX)
            damping = jnp.exp(-VISCOSITY * (wave_along * wave_along + wave_across * wave_across))
            shear = base_ref[0] * wave_along
            to = pl.ds(row, UNIT)
            for f in range(2):
                for p in range(2):
                    term = jnp.where(active, term_ref[2 * f + p, to, :], 0.0)
                    term = jnp.where(
                        lower,
                        jnp.concatenate([term, empty], axis=1),
                        jnp.concatenate([empty, term], axis=1),
                    )
                    other = shear * v_ref[f, 1 - p, to, :]
                    result = term + other if p == 0 else term - other
                    non_ref[f, p, to, :] = result
                    next_ref[f, p, to, :] = damping * (
                        v_ref[f, p, to, :]
                        + TIME_STEP * (GAMMA_NEW * result + ZETA_OLD * old_ref[f, p, to, :])
                    )
            return carry

        lax.fori_loop(0, BLOCK // UNIT, lines, 0)
        for store in stores(c):
            store.start()
        return carry

    lax.fori_loop(0, mode_count // BLOCK, work, 0)

    def end(c, carry):
        for store in stores(c):
            store.wait()
        return carry

    lax.fori_loop(0, mode_count // BLOCK, end, 0)


def lines_local(velocity, previous, base_flow):
    velocity, previous = velocity[:, :, 0], previous[:, :, 0]
    mode_count, extent = velocity.shape[2:]
    half = mode_count // 2
    rows = max(CHUNKS)
    f32, bf16 = jnp.float32, jnp.bfloat16
    zh, zl = z_table()
    xh, xl = x_inverse_table()
    fh, fl = x_forward_table()
    active = len(LOW) * ZS
    count = 2 * XR
    dma = pltpu.SemaphoreType.DMA

    term = pl.pallas_call(
        substep_kernel,
        out_shape=jax.ShapeDtypeStruct((4, mode_count, active), f32),
        in_specs=[pl.BlockSpec(memory_space=pl.ANY)] * 4,
        out_specs=pl.BlockSpec(memory_space=pl.ANY),
        scratch_shapes=[
            pltpu.VMEM((2, 4, half, extent), f32),
            pltpu.VMEM(zh.shape, bf16),
            pltpu.VMEM(zl.shape, bf16),
            pltpu.VMEM(xh.shape, bf16),
            pltpu.VMEM(xl.shape, bf16),
            pltpu.VMEM(fh.shape, bf16),
            pltpu.VMEM(fl.shape, bf16),
            pltpu.VMEM((ZR, 4 * rows, ZS), bf16),
            pltpu.VMEM((ZR, 4 * rows, ZS), bf16),
            pltpu.VMEM((count, 2, half, 128), f32),
            pltpu.VMEM((count, 2, half, 128), f32),
            pltpu.VMEM((XR, 2 * XS, 128), bf16),
            pltpu.VMEM((XR, 2 * XS, 128), bf16),
            pltpu.VMEM((XR, XS, 128), f32),
            pltpu.VMEM((count, 3, UNITS * UNIT, 128), f32),
            pltpu.VMEM((count, 3, UNITS * UNIT, 128), f32),
            pltpu.VMEM((ZR, 3 * max(SPANS) * UNIT, 2 * ZS), f32),
            dma((6,)),
            dma((len(CHUNKS),)),
            dma((len(CHUNKS),)),
            dma((len(CHUNKS),)),
            dma((len(CHUNKS), count)),
            dma((len(CHUNKS), count)),
            dma((len(SPANS), count)),
            dma((len(SPANS), count)),
            dma((2, UNITS)),
            dma((PER,)),
        ],
        compiler_params=pltpu.CompilerParams(
            collective_id=1, has_side_effects=True, vmem_limit_bytes=int(SUB_VMEM * MIB)
        ),
        cost_estimate=pl.CostEstimate(
            flops=10**10, bytes_accessed=64 * velocity.size, transcendentals=0
        ),
        name="substep",
    )(velocity.reshape(4, mode_count, extent), np.concatenate([zh, zl, xh, xl]), fh, fl)

    field = pltpu.VMEM(velocity.shape, f32)
    blocks = mode_count // BLOCK
    advanced, nonlinear = pl.pallas_call(
        advance_kernel,
        out_shape=[jax.ShapeDtypeStruct(velocity.shape, f32)] * 2,
        in_specs=[pl.BlockSpec(memory_space=pltpu.SMEM)] + [pl.BlockSpec(memory_space=pltpu.VMEM)] * 3,
        out_specs=[pl.BlockSpec(memory_space=pl.ANY)] * 2,
        scratch_shapes=[
            field,
            field,
            dma((2, blocks)),
        ],
        compiler_params=pltpu.CompilerParams(vmem_limit_bytes=ADV_VMEM * MIB),
        name="advance",
    )(
        base_flow,
        velocity,
        previous,
        term,
    )
    return advanced[:, :, None], nonlinear[:, :, None]


def solution(mesh):
    in_specs = (P(None, None, None, "gx", "gz"), P(None, None, None, "gx", "gz"), P())
    out_specs = (P(None, None, None, "gx", "gz"), P(None, None, None, "gx", "gz"))
    fits = mesh.shape["gx"] == XR and mesh.shape["gz"] == 2
    work = lines_local if fits else local
    return jax.shard_map(work, mesh=mesh, in_specs=in_specs, out_specs=out_specs, check_vma=False)
```

```python
import functools
import math

import jax
import jax.numpy as jnp
import numpy as np
from jax import lax
from jax.experimental import pallas as pl
from jax.experimental.pallas import tpu as pltpu
from jax.sharding import PartitionSpec as P

NX = 4096
NZ = 2048


TWO_PI = 2.0 * math.pi
VISCOSITY = 0.05
TIME_STEP = 0.2
GAMMA_NEW = 8.0 / 15.0
ZETA_OLD = -17.0 / 60.0


def partner_2(x, axis, distance):
    return lax.ppermute(x, axis, [(i, i ^ 1 << distance) for i in range(lax.axis_size(axis))])


def exact_einsum(pattern, left_array, right_array):
    return jnp.einsum(
        pattern,
        left_array,
        right_array,
        precision=lax.Precision.HIGHEST,
        preferred_element_type=jnp.float32,
    )


def phase_table(left_ints, right_ints, period, direction):
    phase_angle = (
        direction * TWO_PI / period * (left_ints * right_ints % period).astype(jnp.float32)
    )
    return (jnp.cos(phase_angle), jnp.sin(phase_angle))


def complex_apply(value_real, value_imag, table_real, table_imag, pattern):
    out_real = exact_einsum(pattern, value_real, table_real) - exact_einsum(
        pattern, value_imag, table_imag
    )
    out_imag = exact_einsum(pattern, value_real, table_imag) + exact_einsum(
        pattern, value_imag, table_real
    )
    return (out_real, out_imag)


def residue_of(position, levels):
    reversed_bits = jnp.zeros((), jnp.int32)
    for level in range(levels):
        reversed_bits = reversed_bits + ((position >> level & 1) << levels - 1 - level)
    return reversed_bits


def section_twiddle(position, half_span):
    phase_angle = TWO_PI / (2 * half_span) * (position % half_span).astype(jnp.float32)
    return (jnp.cos(phase_angle), jnp.sin(phase_angle))


def spread_butterfly(values):
    position = lax.axis_index("gx")
    levels = lax.axis_size("gx").bit_length() - 1
    for level in reversed(range(levels)):
        half_span = 1 << level
        partner = partner_2(values, "gx", level)
        upper_half = position >> level & 1 == 1
        cosine, sine_part = section_twiddle(position, half_span)
        difference = partner - values
        rotated = jnp.stack(
            [
                difference[:, 0] * cosine - difference[:, 1] * sine_part,
                difference[:, 0] * sine_part + difference[:, 1] * cosine,
            ],
            axis=1,
        )
        values = jnp.where(upper_half, rotated, values + partner)
    return (values, residue_of(position, levels))


def gather_butterfly(values):
    position = lax.axis_index("gx")
    levels = lax.axis_size("gx").bit_length() - 1
    for level in range(levels):
        half_span = 1 << level
        partner = partner_2(values, "gx", level)
        upper_half = position >> level & 1 == 1
        cosine, sine_part = section_twiddle(position, half_span)
        upper_item = jnp.where(upper_half, values, partner)
        lower_item = jnp.where(upper_half, partner, values)
        turned = jnp.stack(
            [
                upper_item[:, 0] * cosine + upper_item[:, 1] * sine_part,
                upper_item[:, 1] * cosine - upper_item[:, 0] * sine_part,
            ],
            axis=1,
        )
        values = jnp.where(upper_half, lower_item - turned, lower_item + turned)
    return values


def axial_table(residue, mode_count, device_count):
    numbers = jnp.arange(mode_count, dtype=jnp.int32)
    points = residue + device_count * numbers
    cosine, sine_part = phase_table(points[:, None], numbers[None, :], NX, 1.0)
    norm_scale = 1.0 / math.sqrt(NX)
    return (cosine * norm_scale, sine_part * norm_scale)


def span_table(groups, span_size):
    residues = jnp.arange(groups, dtype=jnp.int32)[:, None, None]
    grid_rows = jnp.arange(span_size, dtype=jnp.int32)[None, :, None]
    mode_cols = jnp.arange(span_size, dtype=jnp.int32)[None, None, :]
    cosine, sine_part = phase_table(mode_cols, residues + groups * grid_rows, NZ, 1.0)
    norm_scale = 1.0 / math.sqrt(NZ)
    return (cosine * norm_scale, sine_part * norm_scale)


def spanwise_work(received):
    fields, pair_size, planes, row_count, extent = received.shape
    groups = lax.axis_size("gz")
    span_size = extent // groups
    blocks = received.reshape(fields, pair_size, planes, row_count, groups, span_size)
    group_ids = jnp.arange(groups, dtype=jnp.int32)
    mix_real, mix_imag = phase_table(group_ids[:, None], group_ids[None, :], groups, 1.0)
    section_real, section_imag = complex_apply(
        blocks[:, 0], blocks[:, 1], mix_real, mix_imag, "fylcj,rc->fylrj"
    )
    table_real, table_imag = span_table(groups, span_size)
    physical = exact_einsum("fylrj,rtj->fylrt", section_real, table_real) - exact_einsum(
        "fylrj,rtj->fylrt", section_imag, table_imag
    )
    products = jnp.stack(
        [physical[0] * physical[0], physical[0] * physical[1], physical[1] * physical[1]]
    )
    back_real = exact_einsum("pylrt,rtj->pylrj", products, table_real)
    back_imag = -exact_einsum("pylrt,rtj->pylrj", products, table_imag)
    out_real, out_imag = complex_apply(back_real, back_imag, mix_real, -mix_imag, "pylrj,cr->pylcj")
    spectra = jnp.stack([out_real, out_imag], axis=1)
    return spectra.reshape(3, pair_size, planes, row_count, extent)


def span_round(values, work):
    span_spectra = work(lax.all_to_all(values, "gz", split_axis=3, concat_axis=4, tiled=True))
    return lax.all_to_all(span_spectra, "gz", split_axis=4, concat_axis=3, tiled=True)


def signed_block(start, mode_count, extent):
    numbers = start + jnp.arange(mode_count, dtype=jnp.int32)
    return jnp.where(2 * numbers < extent, numbers, numbers - extent)


def local(velocity, previous, base_flow):
    mode_count = velocity.shape[3]
    span_size = velocity.shape[4]
    device_count = lax.axis_size("gx")
    spread, residue = spread_butterfly(velocity)
    table_real, table_imag = axial_table(residue, mode_count, device_count)
    along_real, along_imag = complex_apply(
        spread[:, 0], spread[:, 1], table_real, table_imag, "fymq,sm->fysq"
    )
    physical_along = jnp.stack([along_real, along_imag], axis=1)
    returned = span_round(physical_along, spanwise_work)
    local_real, local_imag = complex_apply(
        returned[:, 0], returned[:, 1], table_real.T, -table_imag.T, "fysq,ms->fymq"
    )
    local_spectra = jnp.stack([local_real, local_imag], axis=1)
    product_spectra = gather_butterfly(local_spectra)
    modes_along = signed_block(lax.axis_index("gx") * mode_count, mode_count, NX)
    modes_across = signed_block(lax.axis_index("gz") * span_size, span_size, NZ)
    wave_along = (modes_along.astype(jnp.float32) * (TWO_PI / NX))[:, None]
    wave_across = (modes_across.astype(jnp.float32) * (TWO_PI / NZ))[None, :]
    keep = jnp.logical_and(
        (3 * jnp.abs(modes_along) < NX)[:, None], (3 * jnp.abs(modes_across) < NZ)[None, :]
    ).astype(jnp.float32)
    shear = base_flow[:, None, None] * wave_along[None]
    prod_real = product_spectra[:, 0]
    prod_imag = product_spectra[:, 1]
    first_real = (
        keep * (wave_along * prod_imag[0] + wave_across * prod_imag[1]) + shear * velocity[0, 1]
    )
    first_imag = (
        -keep * (wave_along * prod_real[0] + wave_across * prod_real[1]) - shear * velocity[0, 0]
    )
    second_real = (
        keep * (wave_along * prod_imag[1] + wave_across * prod_imag[2]) + shear * velocity[1, 1]
    )
    second_imag = (
        -keep * (wave_along * prod_real[1] + wave_across * prod_real[2]) - shear * velocity[1, 0]
    )
    nonlinear = jnp.stack(
        [jnp.stack([first_real, first_imag]), jnp.stack([second_real, second_imag])]
    )
    damping = jnp.exp(-VISCOSITY * (wave_along * wave_along + wave_across * wave_across))
    advanced = damping * (velocity + TIME_STEP * (GAMMA_NEW * nonlinear + ZETA_OLD * previous))
    return (advanced, nonlinear)


XR = 16
XS = NX // XR
ZR = 8
ZS = NZ // ZR
LOW = (0, 1, 2)
HIGH = (5, 6, 7)
MIB = 1 << 20
CHUNKS = (16, 16, 32, 32, 32)
UNIT = 8
UNITS = 11
SIDE = 16 * UNITS
PER = XS // UNIT
OWN = 2 * UNITS
EXTRA = PER - OWN
SPANS = (3, 3, 3, 1, 1)
BACK_AHEAD = 3
UNROLL = 16
UNROLL_INV = 8
UNROLL_FWD = 8
UNROLL_EARLY = 4
BLOCK = 32
SUB_VMEM = 49.5
ADV_VMEM = 40
SHORT = 9
NEEDED = SIDE - 4


def split_table(table):
    high = table.astype(np.float32).astype(jnp.bfloat16)
    low = (table - high.astype(np.float64)).astype(np.float32).astype(jnp.bfloat16)
    return high, low


def z_table():
    r = np.arange(ZR)[:, None, None]
    b = np.arange(ZS)[None, :, None]
    s = np.arange(ZS)[None, None, :]
    angle = TWO_PI / NZ * ((b * (r + ZR * s)) % NZ)
    cos, sin = np.cos(angle) / math.sqrt(NZ), np.sin(angle) / math.sqrt(NZ)
    return split_table(np.concatenate([cos, sin], axis=2))


def x_table():
    r = np.arange(XR)[:, None, None]
    s = np.arange(XS)[None, :, None]
    m = np.arange(XS)[None, None, :]
    angle = TWO_PI / NX * ((m * (r + XR * s)) % NX)
    cos, sin = np.cos(angle) / math.sqrt(NX), np.sin(angle) / math.sqrt(NX)
    return np.stack([cos, -sin], axis=2)


def x_inverse_table():
    table = x_table().reshape(XR, XS, 4, XS // 2)
    parts = []
    for c, length in enumerate(CHUNKS):
        start = sum(CHUNKS[:c])
        parts.append(table[..., start : start + length].reshape(XR, XS, 4 * length))
    return split_table(np.concatenate(parts, axis=2))


def x_forward_table():
    return split_table(np.swapaxes(x_table().reshape(XR, XS, 2 * XS), 1, 2))


def turn(value, numerator, size, sign):
    re, im = value
    numerator = numerator % size
    if numerator == 0:
        return re, im
    if 4 * numerator == size:
        return (-im, re) if sign > 0 else (im, -re)
    if 8 * numerator == size:
        h = math.sqrt(0.5)
        return ((re - im) * h, (re + im) * h) if sign > 0 else ((re + im) * h, (im - re) * h)
    if 8 * numerator == 3 * size:
        h = math.sqrt(0.5)
        return ((-re - im) * h, (re - im) * h) if sign > 0 else ((im - re) * h, (-re - im) * h)
    c = math.cos(TWO_PI * numerator / size)
    s = sign * math.sin(TWO_PI * numerator / size)
    return re * c - im * s, re * s + im * c


def small_dft(values, sign):
    size = len(values)
    if size == 1:
        return values
    even = small_dft(values[0::2], sign)
    odd = small_dft(values[1::2], sign)
    half = size // 2
    out = [None] * size
    for i in range(half):
        re, im = turn(odd[i], i, size, sign)
        out[i] = (even[i][0] + re, even[i][1] + im)
        out[i + half] = (even[i][0] - re, even[i][1] - im)
    return out


def parts_of(value):
    high = value.astype(jnp.bfloat16)
    return high, (value - high.astype(jnp.float32)).astype(jnp.bfloat16)


def dot3(a_high, a_low, b_high, b_low, dims):
    def dot(a, b):
        return lax.dot_general(a, b, (dims, ((), ())), preferred_element_type=jnp.float32)

    return dot(a_high, b_high) + (dot(a_high, b_low) + dot(a_low, b_high))


def merge(first, second, low_half):
    return (
        jnp.where(low_half, first, pltpu.roll(second, 64, 1)),
        jnp.where(low_half, pltpu.roll(first, 64, 1), second),
    )


def z_inverse(first, rows_ref, row, rows, high_ref, low_ref, out_ref, th_ref, tl_ref):
    step = 16
    for c in range(2):
        def body(i, carry):
            at = pl.multiple_of(i * step, step)
            for lane in range(0, ZS, 128):
                values = [None] * ZR
                for a in range(ZR // 2):
                    to = (pl.ds(row + at, step), pl.ds(a * ZS + lane, 128))
                    own = [rows_ref[(0, 2 * c + p) + to] for p in range(2)]
                    other = [rows_ref[(1, 2 * c + p) + to] for p in range(2)]
                    values[a] = tuple(jnp.where(first, x, y) for x, y in zip(own, other))
                    values[a + ZR // 2] = tuple(jnp.where(first, y, x) for x, y in zip(own, other))
                for r, pair in enumerate(small_dft(values, 1)):
                    for p in range(2):
                        high, low = parts_of(pair[p])
                        line = pl.ds((2 * p + c) * rows + at, step)
                        th_ref[r, line, pl.ds(lane, 128)] = high
                        tl_ref[r, line, pl.ds(lane, 128)] = low
            return carry
        lax.fori_loop(0, rows // step, body, 0)

    def group(r, carry):
        both = dot3(
            th_ref[r, : 4 * rows], tl_ref[r, : 4 * rows], high_ref[r], low_ref[r], ((1,), (0,))
        )
        real, imag = both[: 2 * rows], both[2 * rows :]
        done = jnp.concatenate(
            [real[:, :ZS] - imag[:, ZS:], real[:, ZS:] + imag[:, :ZS]], axis=1
        )
        low_half = lax.broadcasted_iota(jnp.int32, (rows, 128), 1) < 64
        for p in range(2):
            for t in range(2):
                at = p * ZS + t * 128
                even, odd = merge(done[:rows, at : at + 128], done[rows:, at : at + 128], low_half)
                out_ref[r * 4 + 2 * t, p, pl.ds(row, rows), :] = even
                out_ref[r * 4 + 2 * t + 1, p, pl.ds(row, rows), :] = odd
        return carry
    lax.fori_loop(0, ZR, group, 0, unroll=UNROLL_INV)


def x_spread(v_ref, row, rows, th_ref, tl_ref):
    step = 16
    for r in range(2):
        def body(i, carry):
            at = pl.multiple_of(i * step, step)
            values = [
                tuple(v_ref[2 * g + r, p, pl.ds(row + at, step), :] for p in range(2))
                for g in range(XR)
            ]
            for res, pair in enumerate(small_dft(values, 1)):
                for p in range(2):
                    high, low = parts_of(pair[p])
                    line = pl.ds(4 * row + (2 * p + r) * rows + at, step)
                    th_ref[res, line, :] = high
                    tl_ref[res, line, :] = low
            return carry
        lax.fori_loop(0, rows // step, body, 0)


def x_early(lines, ih_ref, il_ref, th_ref, tl_ref, f_ref):
    def residue(res, carry):
        f_ref[res] = dot3(
            ih_ref[res, :, :lines], il_ref[res, :, :lines],
            th_ref[res, :lines], tl_ref[res, :lines], ((1,), (0,)),
        )
        return carry
    lax.fori_loop(0, XR, residue, 0, unroll=UNROLL_EARLY)


def x_products(lines, ih_ref, il_ref, fh_ref, fl_ref, th_ref, tl_ref, f_ref, u_refs):
    def residue(res, carry):
        field = f_ref[res] + dot3(
            ih_ref[res, :, lines:], il_ref[res, :, lines:],
            th_ref[res, lines:], tl_ref[res, lines:], ((1,), (0,)),
        )
        swapped = pltpu.roll(field, 64, 1)
        products = jnp.concatenate([field * field, field * swapped], axis=1)
        high, low = parts_of(products)
        both = dot3(fh_ref[res], fl_ref[res], high, low, ((1,), (0,)))
        half = XS // 2
        for h, u_ref in enumerate(u_refs):
            for p in range(2):
                for r in range(2):
                    at = p * XS + r * half
                    u_ref[2 * res + p, r] = both[at : at + half, h * 128 : h * 128 + 128]
        return carry
    lax.fori_loop(0, XR, residue, 0, unroll=UNROLL)


def place_of(o, s):
    e = s - OWN
    if o < 2:
        e = e + o * EXTRA
        m = jnp.where(s < OWN, o, jnp.where(e < 14, 4, 5))
        n = jnp.where(s < OWN, s, jnp.where(e < 14, e, e - 14))
    elif o < 4:
        e = e + (o - 2) * EXTRA
        m = jnp.where(s < OWN, o, 6 + lax.rem(e, 2))
        n = jnp.where(s < OWN, s, e // 2)
    elif o == 4:
        e = s + 12
        m = jnp.where(s < 8, 4, 6 + lax.rem(e, 2))
        n = jnp.where(s < 8, s + 14, e // 2)
    else:
        m, n = 5, s + 6
    return m, lax.rem(n, 2), n // 2


def unit_at(gx, gz, u):
    right = gx >= XR // 2
    m = jnp.where(right, XR - 1 - gx, gx)
    n = 2 * u + gz
    e = jnp.where(m == 4, n, jnp.where(m == 5, n + 14, 2 * n + m - 6))
    upper = e >= EXTRA
    helps = jnp.where(m == 4, n < 14, jnp.where(m == 5, n < 6, e < 2 * EXTRA))
    owner = jnp.where(upper, 1, 0) + jnp.where(m >= 6, 2, 0)
    own_slot = jnp.where(m == 4, n - 14, jnp.where(m == 5, n - 6, e - 12))
    o = jnp.where(m < 4, m, jnp.where(helps, owner, jnp.where(m == 5, 5, 4)))
    s = jnp.where(
        m < 4, n, jnp.where(helps, OWN + e - jnp.where(upper, EXTRA, 0), own_slot)
    )
    unit = o * PER + s
    return jnp.where(right, XR * PER - 1 - unit, unit)


def x_gather(u_refs, out_ref):
    low_half = lax.broadcasted_iota(jnp.int32, (UNIT, 128), 1) < 64
    split = SIDE % PER
    for first, last in ((0, split), (split, PER)):
        def back(i, carry):
            part = i * UNIT // (XS // 2)
            at = pl.multiple_of(i * UNIT - part * (XS // 2), UNIT)
            for h in range(2):
                values = [
                    tuple(
                        u_refs[h][2 * res + p, part, pl.ds(at, UNIT), :]
                        for p in range(2)
                    )
                    for res in range(XR)
                ]
                for g, (re, im) in enumerate(small_dft(values, -1)):
                    if g * PER + first < SIDE:
                        m, side, u = place_of(g, i)
                    elif (XR - g) * PER - last < SIDE:
                        m, side, u = place_of(XR - 1 - g, PER - 1 - i)
                        m = XR - 1 - m
                    else:
                        continue
                    worker = 2 * m + side
                    line = pl.ds(pl.multiple_of(u * UNIT, UNIT), UNIT)
                    if h == 0:
                        out_ref[worker, 0, line, :] = re
                        out_ref[worker, 1, line, :] = im
                    else:
                        out_ref[worker, 2, line, :] = jnp.where(low_half, re, im)
            return carry
        lax.fori_loop(first, last, back, 0)


def z_forward(unit_of, row, rows, v_ref, high_ref, low_ref, out_ref, w_ref):
    low_half = lax.broadcasted_iota(jnp.int32, (rows, 128), 1) < 64

    def group(r, carry):
        real, imag, mixed = (
            [v_ref[r * 4 + j, x, pl.ds(row, rows), :] for j in range(4)] for x in range(3)
        )
        p0r, p2r, p0i, p2i, p1r, p1i = [], [], [], [], [], []
        for source, first, second in ((real, p0r, p2r), (imag, p0i, p2i), (mixed, p1r, p1i)):
            for t in range(2):
                a, b = merge(source[2 * t], source[2 * t + 1], low_half)
                first.append(a)
                second.append(b)
        lines = jnp.concatenate(
            [jnp.concatenate(x, axis=1) for x in (p0r, p1r, p2r, p0i, p1i, p2i)], axis=0
        )
        high, low = parts_of(lines)
        cos, sin = (
            dot3(high, low, high_ref[r, :, at : at + ZS], low_ref[r, :, at : at + ZS], ((1,), (1,)))
            for at in (0, ZS)
        )
        w_ref[r, : 3 * rows, :ZS] = cos[: 3 * rows] + sin[3 * rows :]
        w_ref[r, : 3 * rows, ZS:] = cos[3 * rows :] - sin[: 3 * rows]
        return carry
    lax.fori_loop(0, ZR, group, 0, unroll=UNROLL_FWD)

    def body(i, carry):
        at = pl.multiple_of(i * UNIT, UNIT)
        along = unit_of(row // UNIT + i) * UNIT + lax.broadcasted_iota(jnp.int32, (UNIT, 128), 0)
        along = jnp.where(2 * along < NX, along, along - NX)
        wave_along = along.astype(jnp.float32) * (TWO_PI / NX)
        keep_along = 3 * jnp.abs(along) < NX
        for lane in range(0, ZS, 128):
            spectra = []
            for j in range(3):
                values = [
                    tuple(
                        w_ref[r, pl.ds(j * rows + at, UNIT), pl.ds(p * ZS + lane, 128)]
                        for p in range(2)
                    )
                    for r in range(ZR)
                ]
                spectra.append(small_dft(values, -1))
            for half, groups in enumerate((LOW, HIGH)):
                for place, a in enumerate(groups):
                    start = a * ZS + lane - (NZ if half else 0)
                    mode = start + lax.broadcasted_iota(jnp.int32, (UNIT, 128), 1)
                    wave_across = mode.astype(jnp.float32) * (TWO_PI / NZ)
                    keep = jnp.logical_and(3 * jnp.abs(mode) < NZ, keep_along)
                    (ar, ai), (br, bi), (cr, ci) = (x[a] for x in spectra)
                    terms = [
                        jnp.where(keep, wave_along * ai + wave_across * bi, 0.0),
                        jnp.where(keep, -(wave_along * ar + wave_across * br), 0.0),
                        jnp.where(keep, wave_along * bi + wave_across * ci, 0.0),
                        jnp.where(keep, -(wave_along * br + wave_across * cr), 0.0),
                    ]
                    for x in range(4):
                        out_ref[half, x, pl.ds(row + at, UNIT), pl.ds(place * ZS + lane, 128)] = terms[x]
        return carry
    lax.fori_loop(0, rows // UNIT, body, 0)


def substep_kernel(
    velocity_ref, tables_hbm, fh_hbm, fl_hbm,
    term_ref,
    rows_ref, zh_ref, zl_ref, ih_ref, il_ref, fh_ref, fl_ref,
    zth_ref, ztl_ref, out_ref, in_ref, th_ref, tl_ref, f_ref, back_ref, work_ref, w_ref,
    table_sems, own_sems, swap_send, swap_recv, out_send, out_recv, back_send, back_recv,
    res_send, res_recv,
):
    gx, gz = lax.axis_index("gx"), lax.axis_index("gz")
    count = 2 * XR
    me = 2 * gx + gz
    half = rows_ref.shape[2]
    offsets = [sum(CHUNKS[:c]) for c in range(len(CHUNKS))]

    def device(t):
        return (t // 2, lax.rem(t, 2))

    tables = [
        pltpu.make_async_copy(src, dst, table_sems.at[n])
        for n, (src, dst) in enumerate(
            (
                (tables_hbm.at[pl.ds(0, ZR)], zh_ref),
                (tables_hbm.at[pl.ds(ZR, ZR)], zl_ref),
                (tables_hbm.at[pl.ds(2 * ZR, XR)], ih_ref),
                (tables_hbm.at[pl.ds(2 * ZR + XR, XR)], il_ref),
                (fh_hbm, fh_ref),
                (fl_hbm, fl_ref),
            )
        )
    ]

    def load_own(c):
        return pltpu.make_async_copy(
            velocity_ref.at[:, pl.ds(pl.multiple_of(gz * half + offsets[c], 16), CHUNKS[c]), :],
            rows_ref.at[0, :, pl.ds(offsets[c], CHUNKS[c]), :],
            own_sems.at[c],
        )

    def swap(c):
        return pltpu.make_async_remote_copy(
            src_ref=velocity_ref.at[
                :, pl.ds(pl.multiple_of((1 - gz) * half + offsets[c], 16), CHUNKS[c]), :
            ],
            dst_ref=rows_ref.at[1, :, pl.ds(offsets[c], CHUNKS[c]), :],
            send_sem=swap_send.at[c],
            recv_sem=swap_recv.at[c],
            device_id=(gx, 1 - gz),
            device_id_type=pl.DeviceIdType.MESH,
        )

    for c in range(len(CHUNKS)):
        load_own(c).start()
    for table in tables[:2]:
        table.start()

    barrier = pltpu.get_barrier_semaphore()

    def greet(i, carry):
        pl.semaphore_signal(
            barrier,
            inc=1,
            device_id=device(lax.rem(me + i, count)),
            device_id_type=pl.DeviceIdType.MESH,
        )
        return carry

    lax.fori_loop(1, count, greet, 0)
    pl.semaphore_wait(barrier, count - 1)
    for c in range(len(CHUNKS)):
        swap(c).start()
    for table in tables[2:]:
        table.start()

    def target(i, c):
        return lax.rem(me + jnp.where(me < XR, i, 2 * XR - i), count)

    def ship(src_ref, dst_ref, sends, recvs, c, at, length):
        span = pl.ds(at, length)

        def copy(i):
            t = target(i, c)
            return pltpu.make_async_remote_copy(
                src_ref=src_ref.at[t, :, span, :],
                dst_ref=dst_ref.at[me, :, span, :],
                send_sem=sends.at[c, i],
                recv_sem=recvs.at[c, me],
                device_id=device(t),
                device_id_type=pl.DeviceIdType.MESH,
            )

        def local():
            return pltpu.make_async_copy(
                src_ref.at[me, :, span, :], dst_ref.at[me, :, span, :], recvs.at[c, me]
            )

        return copy, local

    def takes(t, src_ref, dst_ref, sends, recvs, c, at, length):
        if dst_ref is not work_ref or at < SHORT * UNIT:
            return t >= 0
        g = t // 2
        return jnp.logical_and(g != 5, g != XR - 6)

    def goes(t, *args):
        return jnp.logical_and(t != me, takes(t, *args))

    def ship_start(*args):
        copy, local = ship(*args)

        def start(i, carry):
            @pl.when(goes(target(i, args[4]), *args))
            def _():
                copy(i).start()
            return carry

        lax.fori_loop(0, count, start, 0)

        @pl.when(takes(me, *args))
        def _():
            local().start()

    def ship_arrive(src_ref, dst_ref, sends, recvs, c, at, length):
        span = pl.ds(at, length)
        _, local = ship(src_ref, dst_ref, sends, recvs, c, at, length)

        def wait(i, carry):
            t = lax.rem(me + i, count)
            pltpu.make_async_copy(
                src_ref.at[t, :, span, :], dst_ref.at[t, :, span, :], recvs.at[c, t]
            ).wait()
            return carry

        lax.fori_loop(1, count, wait, 0)
        local().wait()

    def ship_leave(*args):
        copy, _ = ship(*args)

        def wait(i, carry):
            @pl.when(goes(target(i, args[4]), *args))
            def _():
                copy(i).wait_send()
            return carry

        lax.fori_loop(0, count, wait, 0)

    def spread_args(c):
        return out_ref, in_ref, out_send, out_recv, c, offsets[c], CHUNKS[c]

    tables[0].wait()
    tables[1].wait()
    for c in range(len(CHUNKS)):
        load_own(c).wait()
        swap(c).wait_recv()
        z_inverse(
            gz == 0, rows_ref, offsets[c], CHUNKS[c],
            zh_ref, zl_ref, out_ref, zth_ref, ztl_ref,
        )
        ship_start(*spread_args(c))

    for c in range(len(CHUNKS)):
        ship_arrive(*spread_args(c))
        x_spread(in_ref, offsets[c], CHUNKS[c], th_ref, tl_ref)
        if c == len(CHUNKS) - 2:
            for table in tables[2:]:
                table.wait()
            x_early(4 * offsets[-1], ih_ref, il_ref, th_ref, tl_ref, f_ref)
    for c in range(len(CHUNKS)):
        ship_leave(*spread_args(c))
    x_products(
        4 * offsets[-1], ih_ref, il_ref, fh_ref, fl_ref, th_ref, tl_ref, f_ref, (out_ref, in_ref)
    )
    x_gather((out_ref, in_ref), back_ref)

    starts = [sum(SPANS[:c]) for c in range(len(SPANS))]

    def back_args(c):
        return back_ref, work_ref, back_send, back_recv, c, starts[c] * UNIT, SPANS[c] * UNIT

    for c in range(BACK_AHEAD):
        ship_start(*back_args(c))

    def result(u, side):
        unit = unit_at(gx, gz, u)
        owner = unit // PER
        slot = unit - owner * PER
        src = rows_ref.at[
            side, :, pl.ds(pl.multiple_of(u * UNIT, UNIT), UNIT), pl.ds(0, term_ref.shape[2])
        ]
        dst = term_ref.at[:, pl.ds(pl.multiple_of(slot * UNIT, UNIT), UNIT), :]
        here = jnp.logical_and(owner == gx, side == gz)

        def remote():
            return pltpu.make_async_remote_copy(
                src_ref=src,
                dst_ref=dst,
                send_sem=res_send.at[side, u],
                recv_sem=res_recv.at[slot],
                device_id=(owner, side),
                device_id_type=pl.DeviceIdType.MESH,
            )

        return here, remote, lambda: pltpu.make_async_copy(src, dst, res_recv.at[slot])

    def forward(c):
        ship_arrive(*back_args(c))
        unit, units = starts[c], SPANS[c]
        z_forward(
            functools.partial(unit_at, gx, gz), unit * UNIT, units * UNIT,
            work_ref, zh_ref, zl_ref, rows_ref, w_ref,
        )

        def send(n, carry):
            for side in range(2):
                here, remote, local = result(unit + n, side)

                @pl.when(here)
                def _():
                    local().start()

                @pl.when(jnp.logical_not(here))
                def _():
                    remote().start()
            return carry

        lax.fori_loop(0, units, send, 0)

    for c in range(len(SPANS)):
        @pl.when(takes(me, *back_args(c)))
        def _():
            forward(c)

        if c + BACK_AHEAD < len(SPANS):
            ship_start(*back_args(c + BACK_AHEAD))

    def sent(u, carry):
        for side in range(2):
            here, remote, _ = result(u, side)

            @pl.when(jnp.logical_not(here))
            def _():
                remote().wait_send()
        return carry

    def got(s, carry):
        unit = gx * PER + s

        @pl.when(jnp.logical_or(unit < NEEDED, unit >= XR * PER - NEEDED))
        def _():
            pltpu.make_async_copy(
                rows_ref.at[0, :, pl.ds(0, UNIT), pl.ds(0, term_ref.shape[2])],
                term_ref.at[:, pl.ds(pl.multiple_of(s * UNIT, UNIT), UNIT), :],
                res_recv.at[s],
            ).wait()
        return carry

    lax.fori_loop(0, PER, got, 0)
    short = jnp.logical_or(gx == 5, gx == XR - 6)
    lax.fori_loop(0, jnp.where(short, SHORT, UNITS), sent, 0)

    for c in range(len(CHUNKS)):
        swap(c).wait_send()
    for c in range(len(SPANS)):
        ship_leave(*back_args(c))


def advance_kernel(
    base_ref, v_ref, old_ref, term_ref, next_hbm, non_hbm, next_ref, non_ref, store_sems
):
    mode_count, extent = v_ref.shape[2:]
    lower = lax.axis_index("gz") == 0
    across = lax.axis_index("gz") * extent + lax.broadcasted_iota(jnp.int32, (1, extent), 1)
    wave_across = jnp.where(2 * across < NZ, across, across - NZ).astype(jnp.float32) * (TWO_PI / NZ)
    empty = jnp.zeros((UNIT, extent - term_ref.shape[2]), jnp.float32)

    def at(c):
        return pl.ds(pl.multiple_of(c * BLOCK, BLOCK), BLOCK)

    def stores(c):
        return (
            pltpu.make_async_copy(
                next_ref.at[:, :, at(c), :], next_hbm.at[:, :, at(c), :], store_sems.at[0, c]
            ),
            pltpu.make_async_copy(
                non_ref.at[:, :, at(c), :], non_hbm.at[:, :, at(c), :], store_sems.at[1, c]
            ),
        )

    def work(c, carry):
        def lines(i, carry):
            row = pl.multiple_of(c * BLOCK + i * UNIT, UNIT)
            start = lax.axis_index("gx") * XS + row
            active = jnp.logical_or(start < NEEDED * UNIT, start >= NX - NEEDED * UNIT)
            along = start + lax.broadcasted_iota(jnp.int32, (UNIT, 1), 0)
            wave_along = jnp.where(2 * along < NX, along, along - NX).astype(jnp.float32) * (TWO_PI / NX)
            damping = jnp.exp(-VISCOSITY * (wave_along * wave_along + wave_across * wave_across))
            shear = base_ref[0] * wave_along
            to = pl.ds(row, UNIT)
            for f in range(2):
                for p in range(2):
                    term = jnp.where(active, term_ref[2 * f + p, to, :], 0.0)
                    term = jnp.where(
                        lower,
                        jnp.concatenate([term, empty], axis=1),
                        jnp.concatenate([empty, term], axis=1),
                    )
                    other = shear * v_ref[f, 1 - p, to, :]
                    result = term + other if p == 0 else term - other
                    non_ref[f, p, to, :] = result
                    next_ref[f, p, to, :] = damping * (
                        v_ref[f, p, to, :]
                        + TIME_STEP * (GAMMA_NEW * result + ZETA_OLD * old_ref[f, p, to, :])
                    )
            return carry

        lax.fori_loop(0, BLOCK // UNIT, lines, 0)
        for store in stores(c):
            store.start()
        return carry

    lax.fori_loop(0, mode_count // BLOCK, work, 0)

    def end(c, carry):
        for store in stores(c):
            store.wait()
        return carry

    lax.fori_loop(0, mode_count // BLOCK, end, 0)


def lines_local(velocity, previous, base_flow):
    velocity, previous = velocity[:, :, 0], previous[:, :, 0]
    mode_count, extent = velocity.shape[2:]
    half = mode_count // 2
    rows = max(CHUNKS)
    f32, bf16 = jnp.float32, jnp.bfloat16
    zh, zl = z_table()
    xh, xl = x_inverse_table()
    fh, fl = x_forward_table()
    active = len(LOW) * ZS
    count = 2 * XR
    dma = pltpu.SemaphoreType.DMA

    term = pl.pallas_call(
        substep_kernel,
        out_shape=jax.ShapeDtypeStruct((4, mode_count, active), f32),
        in_specs=[pl.BlockSpec(memory_space=pl.ANY)] * 4,
        out_specs=pl.BlockSpec(memory_space=pl.ANY),
        scratch_shapes=[
            pltpu.VMEM((2, 4, half, extent), f32),
            pltpu.VMEM(zh.shape, bf16),
            pltpu.VMEM(zl.shape, bf16),
            pltpu.VMEM(xh.shape, bf16),
            pltpu.VMEM(xl.shape, bf16),
            pltpu.VMEM(fh.shape, bf16),
            pltpu.VMEM(fl.shape, bf16),
            pltpu.VMEM((ZR, 4 * rows, ZS), bf16),
            pltpu.VMEM((ZR, 4 * rows, ZS), bf16),
            pltpu.VMEM((count, 2, half, 128), f32),
            pltpu.VMEM((count, 2, half, 128), f32),
            pltpu.VMEM((XR, 2 * XS, 128), bf16),
            pltpu.VMEM((XR, 2 * XS, 128), bf16),
            pltpu.VMEM((XR, XS, 128), f32),
            pltpu.VMEM((count, 3, UNITS * UNIT, 128), f32),
            pltpu.VMEM((count, 3, UNITS * UNIT, 128), f32),
            pltpu.VMEM((ZR, 3 * max(SPANS) * UNIT, 2 * ZS), f32),
            dma((6,)),
            dma((len(CHUNKS),)),
            dma((len(CHUNKS),)),
            dma((len(CHUNKS),)),
            dma((len(CHUNKS), count)),
            dma((len(CHUNKS), count)),
            dma((len(SPANS), count)),
            dma((len(SPANS), count)),
            dma((2, UNITS)),
            dma((PER,)),
        ],
        compiler_params=pltpu.CompilerParams(
            collective_id=1, has_side_effects=True, vmem_limit_bytes=int(SUB_VMEM * MIB)
        ),
        cost_estimate=pl.CostEstimate(
            flops=10**10, bytes_accessed=64 * velocity.size, transcendentals=0
        ),
        name="substep",
    )(velocity.reshape(4, mode_count, extent), np.concatenate([zh, zl, xh, xl]), fh, fl)

    field = pltpu.VMEM(velocity.shape, f32)
    blocks = mode_count // BLOCK
    advanced, nonlinear = pl.pallas_call(
        advance_kernel,
        out_shape=[jax.ShapeDtypeStruct(velocity.shape, f32)] * 2,
        in_specs=[pl.BlockSpec(memory_space=pltpu.SMEM)] + [pl.BlockSpec(memory_space=pltpu.VMEM)] * 3,
        out_specs=[pl.BlockSpec(memory_space=pl.ANY)] * 2,
        scratch_shapes=[
            field,
            field,
            dma((2, blocks)),
        ],
        compiler_params=pltpu.CompilerParams(vmem_limit_bytes=ADV_VMEM * MIB),
        name="advance",
    )(
        base_flow,
        velocity,
        previous,
        term,
    )
    return advanced[:, :, None], nonlinear[:, :, None]


def solution(mesh):
    in_specs = (P(None, None, None, "gx", "gz"), P(None, None, None, "gx", "gz"), P())
    out_specs = (P(None, None, None, "gx", "gz"), P(None, None, None, "gx", "gz"))
    fits = mesh.shape["gx"] == XR and mesh.shape["gz"] == 2
    work = lines_local if fits else local
    return jax.shard_map(work, mesh=mesh, in_specs=in_specs, out_specs=out_specs, check_vma=False)
```

```python
import functools
import math

import jax
import jax.numpy as jnp
import numpy as np
from jax import lax
from jax.experimental import pallas as pl
from jax.experimental.pallas import tpu as pltpu
from jax.sharding import PartitionSpec as P

NX = 4096
NZ = 2048


TWO_PI = 2.0 * math.pi
VISCOSITY = 0.05
TIME_STEP = 0.2
GAMMA_NEW = 8.0 / 15.0
ZETA_OLD = -17.0 / 60.0


def partner_2(x, axis, distance):
    return lax.ppermute(x, axis, [(i, i ^ 1 << distance) for i in range(lax.axis_size(axis))])


def exact_einsum(pattern, left_array, right_array):
    return jnp.einsum(
        pattern,
        left_array,
        right_array,
        precision=lax.Precision.HIGHEST,
        preferred_element_type=jnp.float32,
    )


def phase_table(left_ints, right_ints, period, direction):
    phase_angle = (
        direction * TWO_PI / period * (left_ints * right_ints % period).astype(jnp.float32)
    )
    return (jnp.cos(phase_angle), jnp.sin(phase_angle))


def complex_apply(value_real, value_imag, table_real, table_imag, pattern):
    out_real = exact_einsum(pattern, value_real, table_real) - exact_einsum(
        pattern, value_imag, table_imag
    )
    out_imag = exact_einsum(pattern, value_real, table_imag) + exact_einsum(
        pattern, value_imag, table_real
    )
    return (out_real, out_imag)


def residue_of(position, levels):
    reversed_bits = jnp.zeros((), jnp.int32)
    for level in range(levels):
        reversed_bits = reversed_bits + ((position >> level & 1) << levels - 1 - level)
    return reversed_bits


def section_twiddle(position, half_span):
    phase_angle = TWO_PI / (2 * half_span) * (position % half_span).astype(jnp.float32)
    return (jnp.cos(phase_angle), jnp.sin(phase_angle))


def spread_butterfly(values):
    position = lax.axis_index("gx")
    levels = lax.axis_size("gx").bit_length() - 1
    for level in reversed(range(levels)):
        half_span = 1 << level
        partner = partner_2(values, "gx", level)
        upper_half = position >> level & 1 == 1
        cosine, sine_part = section_twiddle(position, half_span)
        difference = partner - values
        rotated = jnp.stack(
            [
                difference[:, 0] * cosine - difference[:, 1] * sine_part,
                difference[:, 0] * sine_part + difference[:, 1] * cosine,
            ],
            axis=1,
        )
        values = jnp.where(upper_half, rotated, values + partner)
    return (values, residue_of(position, levels))


def gather_butterfly(values):
    position = lax.axis_index("gx")
    levels = lax.axis_size("gx").bit_length() - 1
    for level in range(levels):
        half_span = 1 << level
        partner = partner_2(values, "gx", level)
        upper_half = position >> level & 1 == 1
        cosine, sine_part = section_twiddle(position, half_span)
        upper_item = jnp.where(upper_half, values, partner)
        lower_item = jnp.where(upper_half, partner, values)
        turned = jnp.stack(
            [
                upper_item[:, 0] * cosine + upper_item[:, 1] * sine_part,
                upper_item[:, 1] * cosine - upper_item[:, 0] * sine_part,
            ],
            axis=1,
        )
        values = jnp.where(upper_half, lower_item - turned, lower_item + turned)
    return values


def axial_table(residue, mode_count, device_count):
    numbers = jnp.arange(mode_count, dtype=jnp.int32)
    points = residue + device_count * numbers
    cosine, sine_part = phase_table(points[:, None], numbers[None, :], NX, 1.0)
    norm_scale = 1.0 / math.sqrt(NX)
    return (cosine * norm_scale, sine_part * norm_scale)


def span_table(groups, span_size):
    residues = jnp.arange(groups, dtype=jnp.int32)[:, None, None]
    grid_rows = jnp.arange(span_size, dtype=jnp.int32)[None, :, None]
    mode_cols = jnp.arange(span_size, dtype=jnp.int32)[None, None, :]
    cosine, sine_part = phase_table(mode_cols, residues + groups * grid_rows, NZ, 1.0)
    norm_scale = 1.0 / math.sqrt(NZ)
    return (cosine * norm_scale, sine_part * norm_scale)


def spanwise_work(received):
    fields, pair_size, planes, row_count, extent = received.shape
    groups = lax.axis_size("gz")
    span_size = extent // groups
    blocks = received.reshape(fields, pair_size, planes, row_count, groups, span_size)
    group_ids = jnp.arange(groups, dtype=jnp.int32)
    mix_real, mix_imag = phase_table(group_ids[:, None], group_ids[None, :], groups, 1.0)
    section_real, section_imag = complex_apply(
        blocks[:, 0], blocks[:, 1], mix_real, mix_imag, "fylcj,rc->fylrj"
    )
    table_real, table_imag = span_table(groups, span_size)
    physical = exact_einsum("fylrj,rtj->fylrt", section_real, table_real) - exact_einsum(
        "fylrj,rtj->fylrt", section_imag, table_imag
    )
    products = jnp.stack(
        [physical[0] * physical[0], physical[0] * physical[1], physical[1] * physical[1]]
    )
    back_real = exact_einsum("pylrt,rtj->pylrj", products, table_real)
    back_imag = -exact_einsum("pylrt,rtj->pylrj", products, table_imag)
    out_real, out_imag = complex_apply(back_real, back_imag, mix_real, -mix_imag, "pylrj,cr->pylcj")
    spectra = jnp.stack([out_real, out_imag], axis=1)
    return spectra.reshape(3, pair_size, planes, row_count, extent)


def span_round(values, work):
    span_spectra = work(lax.all_to_all(values, "gz", split_axis=3, concat_axis=4, tiled=True))
    return lax.all_to_all(span_spectra, "gz", split_axis=4, concat_axis=3, tiled=True)


def signed_block(start, mode_count, extent):
    numbers = start + jnp.arange(mode_count, dtype=jnp.int32)
    return jnp.where(2 * numbers < extent, numbers, numbers - extent)


def local(velocity, previous, base_flow):
    mode_count = velocity.shape[3]
    span_size = velocity.shape[4]
    device_count = lax.axis_size("gx")
    spread, residue = spread_butterfly(velocity)
    table_real, table_imag = axial_table(residue, mode_count, device_count)
    along_real, along_imag = complex_apply(
        spread[:, 0], spread[:, 1], table_real, table_imag, "fymq,sm->fysq"
    )
    physical_along = jnp.stack([along_real, along_imag], axis=1)
    returned = span_round(physical_along, spanwise_work)
    local_real, local_imag = complex_apply(
        returned[:, 0], returned[:, 1], table_real.T, -table_imag.T, "fysq,ms->fymq"
    )
    local_spectra = jnp.stack([local_real, local_imag], axis=1)
    product_spectra = gather_butterfly(local_spectra)
    modes_along = signed_block(lax.axis_index("gx") * mode_count, mode_count, NX)
    modes_across = signed_block(lax.axis_index("gz") * span_size, span_size, NZ)
    wave_along = (modes_along.astype(jnp.float32) * (TWO_PI / NX))[:, None]
    wave_across = (modes_across.astype(jnp.float32) * (TWO_PI / NZ))[None, :]
    keep = jnp.logical_and(
        (3 * jnp.abs(modes_along) < NX)[:, None], (3 * jnp.abs(modes_across) < NZ)[None, :]
    ).astype(jnp.float32)
    shear = base_flow[:, None, None] * wave_along[None]
    prod_real = product_spectra[:, 0]
    prod_imag = product_spectra[:, 1]
    first_real = (
        keep * (wave_along * prod_imag[0] + wave_across * prod_imag[1]) + shear * velocity[0, 1]
    )
    first_imag = (
        -keep * (wave_along * prod_real[0] + wave_across * prod_real[1]) - shear * velocity[0, 0]
    )
    second_real = (
        keep * (wave_along * prod_imag[1] + wave_across * prod_imag[2]) + shear * velocity[1, 1]
    )
    second_imag = (
        -keep * (wave_along * prod_real[1] + wave_across * prod_real[2]) - shear * velocity[1, 0]
    )
    nonlinear = jnp.stack(
        [jnp.stack([first_real, first_imag]), jnp.stack([second_real, second_imag])]
    )
    damping = jnp.exp(-VISCOSITY * (wave_along * wave_along + wave_across * wave_across))
    advanced = damping * (velocity + TIME_STEP * (GAMMA_NEW * nonlinear + ZETA_OLD * previous))
    return (advanced, nonlinear)


XR = 16
XS = NX // XR
ZR = 8
ZS = NZ // ZR
LOW = (0, 1, 2)
HIGH = (5, 6, 7)
MIB = 1 << 20
CHUNKS = (16, 16, 32, 32, 32)
UNIT = 8
UNITS = 11
SIDE = 16 * UNITS
PER = XS // UNIT
OWN = 2 * UNITS
EXTRA = PER - OWN
SPANS = (3, 3, 3, 1, 1)
BACK_AHEAD = 4
UNROLL = 16
UNROLL_INV = 8
UNROLL_FWD = 8
UNROLL_EARLY = 4
BLOCK = 32
SUB_VMEM = 49.5
ADV_VMEM = 40
SHORT = 9
NEEDED = SIDE - 4


def split_table(table):
    high = table.astype(np.float32).astype(jnp.bfloat16)
    low = (table - high.astype(np.float64)).astype(np.float32).astype(jnp.bfloat16)
    return high, low


def z_table():
    r = np.arange(ZR)[:, None, None]
    b = np.arange(ZS)[None, :, None]
    s = np.arange(ZS)[None, None, :]
    angle = TWO_PI / NZ * ((b * (r + ZR * s)) % NZ)
    cos, sin = np.cos(angle) / math.sqrt(NZ), np.sin(angle) / math.sqrt(NZ)
    return split_table(np.concatenate([cos, sin], axis=2))


def x_table():
    r = np.arange(XR)[:, None, None]
    s = np.arange(XS)[None, :, None]
    m = np.arange(XS)[None, None, :]
    angle = TWO_PI / NX * ((m * (r + XR * s)) % NX)
    cos, sin = np.cos(angle) / math.sqrt(NX), np.sin(angle) / math.sqrt(NX)
    return np.stack([cos, -sin], axis=2)


def x_inverse_table():
    table = x_table().reshape(XR, XS, 4, XS // 2)
    parts = []
    for c, length in enumerate(CHUNKS):
        start = sum(CHUNKS[:c])
        parts.append(table[..., start : start + length].reshape(XR, XS, 4 * length))
    return split_table(np.concatenate(parts, axis=2))


def x_forward_table():
    return split_table(np.swapaxes(x_table().reshape(XR, XS, 2 * XS), 1, 2))


def turn(value, numerator, size, sign):
    re, im = value
    numerator = numerator % size
    if numerator == 0:
        return re, im
    if 4 * numerator == size:
        return (-im, re) if sign > 0 else (im, -re)
    if 8 * numerator == size:
        h = math.sqrt(0.5)
        return ((re - im) * h, (re + im) * h) if sign > 0 else ((re + im) * h, (im - re) * h)
    if 8 * numerator == 3 * size:
        h = math.sqrt(0.5)
        return ((-re - im) * h, (re - im) * h) if sign > 0 else ((im - re) * h, (-re - im) * h)
    c = math.cos(TWO_PI * numerator / size)
    s = sign * math.sin(TWO_PI * numerator / size)
    return re * c - im * s, re * s + im * c


def small_dft(values, sign):
    size = len(values)
    if size == 1:
        return values
    even = small_dft(values[0::2], sign)
    odd = small_dft(values[1::2], sign)
    half = size // 2
    out = [None] * size
    for i in range(half):
        re, im = turn(odd[i], i, size, sign)
        out[i] = (even[i][0] + re, even[i][1] + im)
        out[i + half] = (even[i][0] - re, even[i][1] - im)
    return out


def parts_of(value):
    high = value.astype(jnp.bfloat16)
    return high, (value - high.astype(jnp.float32)).astype(jnp.bfloat16)


def dot3(a_high, a_low, b_high, b_low, dims):
    def dot(a, b):
        return lax.dot_general(a, b, (dims, ((), ())), preferred_element_type=jnp.float32)

    return dot(a_high, b_high) + (dot(a_high, b_low) + dot(a_low, b_high))


def merge(first, second, low_half):
    return (
        jnp.where(low_half, first, pltpu.roll(second, 64, 1)),
        jnp.where(low_half, pltpu.roll(first, 64, 1), second),
    )


def z_inverse(first, rows_ref, row, rows, high_ref, low_ref, out_ref, th_ref, tl_ref):
    step = 16
    for c in range(2):
        def body(i, carry):
            at = pl.multiple_of(i * step, step)
            for lane in range(0, ZS, 128):
                values = [None] * ZR
                for a in range(ZR // 2):
                    to = (pl.ds(row + at, step), pl.ds(a * ZS + lane, 128))
                    own = [rows_ref[(0, 2 * c + p) + to] for p in range(2)]
                    other = [rows_ref[(1, 2 * c + p) + to] for p in range(2)]
                    values[a] = tuple(jnp.where(first, x, y) for x, y in zip(own, other))
                    values[a + ZR // 2] = tuple(jnp.where(first, y, x) for x, y in zip(own, other))
                for r, pair in enumerate(small_dft(values, 1)):
                    for p in range(2):
                        high, low = parts_of(pair[p])
                        line = pl.ds((2 * p + c) * rows + at, step)
                        th_ref[r, line, pl.ds(lane, 128)] = high
                        tl_ref[r, line, pl.ds(lane, 128)] = low
            return carry
        lax.fori_loop(0, rows // step, body, 0)

    def group(r, carry):
        both = dot3(
            th_ref[r, : 4 * rows], tl_ref[r, : 4 * rows], high_ref[r], low_ref[r], ((1,), (0,))
        )
        real, imag = both[: 2 * rows], both[2 * rows :]
        done = jnp.concatenate(
            [real[:, :ZS] - imag[:, ZS:], real[:, ZS:] + imag[:, :ZS]], axis=1
        )
        low_half = lax.broadcasted_iota(jnp.int32, (rows, 128), 1) < 64
        for p in range(2):
            for t in range(2):
                at = p * ZS + t * 128
                even, odd = merge(done[:rows, at : at + 128], done[rows:, at : at + 128], low_half)
                out_ref[r * 4 + 2 * t, p, pl.ds(row, rows), :] = even
                out_ref[r * 4 + 2 * t + 1, p, pl.ds(row, rows), :] = odd
        return carry
    lax.fori_loop(0, ZR, group, 0, unroll=UNROLL_INV)


def x_spread(v_ref, row, rows, th_ref, tl_ref):
    step = 16
    for r in range(2):
        def body(i, carry):
            at = pl.multiple_of(i * step, step)
            values = [
                tuple(v_ref[2 * g + r, p, pl.ds(row + at, step), :] for p in range(2))
                for g in range(XR)
            ]
            for res, pair in enumerate(small_dft(values, 1)):
                for p in range(2):
                    high, low = parts_of(pair[p])
                    line = pl.ds(4 * row + (2 * p + r) * rows + at, step)
                    th_ref[res, line, :] = high
                    tl_ref[res, line, :] = low
            return carry
        lax.fori_loop(0, rows // step, body, 0)


def x_early(lines, ih_ref, il_ref, th_ref, tl_ref, f_ref):
    def residue(res, carry):
        f_ref[res] = dot3(
            ih_ref[res, :, :lines], il_ref[res, :, :lines],
            th_ref[res, :lines], tl_ref[res, :lines], ((1,), (0,)),
        )
        return carry
    lax.fori_loop(0, XR, residue, 0, unroll=UNROLL_EARLY)


def x_products(lines, ih_ref, il_ref, fh_ref, fl_ref, th_ref, tl_ref, f_ref, u_refs):
    def residue(res, carry):
        field = f_ref[res] + dot3(
            ih_ref[res, :, lines:], il_ref[res, :, lines:],
            th_ref[res, lines:], tl_ref[res, lines:], ((1,), (0,)),
        )
        swapped = pltpu.roll(field, 64, 1)
        products = jnp.concatenate([field * field, field * swapped], axis=1)
        high, low = parts_of(products)
        both = dot3(fh_ref[res], fl_ref[res], high, low, ((1,), (0,)))
        half = XS // 2
        for h, u_ref in enumerate(u_refs):
            for p in range(2):
                for r in range(2):
                    at = p * XS + r * half
                    u_ref[2 * res + p, r] = both[at : at + half, h * 128 : h * 128 + 128]
        return carry
    lax.fori_loop(0, XR, residue, 0, unroll=UNROLL)


def place_of(o, s):
    e = s - OWN
    if o < 2:
        e = e + o * EXTRA
        m = jnp.where(s < OWN, o, jnp.where(e < 14, 4, 5))
        n = jnp.where(s < OWN, s, jnp.where(e < 14, e, e - 14))
    elif o < 4:
        e = e + (o - 2) * EXTRA
        m = jnp.where(s < OWN, o, 6 + lax.rem(e, 2))
        n = jnp.where(s < OWN, s, e // 2)
    elif o == 4:
        e = s + 12
        m = jnp.where(s < 8, 4, 6 + lax.rem(e, 2))
        n = jnp.where(s < 8, s + 14, e // 2)
    else:
        m, n = 5, s + 6
    return m, lax.rem(n, 2), n // 2


def unit_at(gx, gz, u):
    right = gx >= XR // 2
    m = jnp.where(right, XR - 1 - gx, gx)
    n = 2 * u + gz
    e = jnp.where(m == 4, n, jnp.where(m == 5, n + 14, 2 * n + m - 6))
    upper = e >= EXTRA
    helps = jnp.where(m == 4, n < 14, jnp.where(m == 5, n < 6, e < 2 * EXTRA))
    owner = jnp.where(upper, 1, 0) + jnp.where(m >= 6, 2, 0)
    own_slot = jnp.where(m == 4, n - 14, jnp.where(m == 5, n - 6, e - 12))
    o = jnp.where(m < 4, m, jnp.where(helps, owner, jnp.where(m == 5, 5, 4)))
    s = jnp.where(
        m < 4, n, jnp.where(helps, OWN + e - jnp.where(upper, EXTRA, 0), own_slot)
    )
    unit = o * PER + s
    return jnp.where(right, XR * PER - 1 - unit, unit)


def x_gather(u_refs, out_ref):
    low_half = lax.broadcasted_iota(jnp.int32, (UNIT, 128), 1) < 64
    split = SIDE % PER
    for first, last in ((0, split), (split, PER)):
        def back(i, carry):
            part = i * UNIT // (XS // 2)
            at = pl.multiple_of(i * UNIT - part * (XS // 2), UNIT)
            for h in range(2):
                values = [
                    tuple(
                        u_refs[h][2 * res + p, part, pl.ds(at, UNIT), :]
                        for p in range(2)
                    )
                    for res in range(XR)
                ]
                for g, (re, im) in enumerate(small_dft(values, -1)):
                    if g * PER + first < SIDE:
                        m, side, u = place_of(g, i)
                    elif (XR - g) * PER - last < SIDE:
                        m, side, u = place_of(XR - 1 - g, PER - 1 - i)
                        m = XR - 1 - m
                    else:
                        continue
                    worker = 2 * m + side
                    line = pl.ds(pl.multiple_of(u * UNIT, UNIT), UNIT)
                    if h == 0:
                        out_ref[worker, 0, line, :] = re
                        out_ref[worker, 1, line, :] = im
                    else:
                        out_ref[worker, 2, line, :] = jnp.where(low_half, re, im)
            return carry
        lax.fori_loop(first, last, back, 0)


def z_forward(unit_of, row, rows, v_ref, high_ref, low_ref, out_ref, w_ref):
    low_half = lax.broadcasted_iota(jnp.int32, (rows, 128), 1) < 64

    def group(r, carry):
        real, imag, mixed = (
            [v_ref[r * 4 + j, x, pl.ds(row, rows), :] for j in range(4)] for x in range(3)
        )
        p0r, p2r, p0i, p2i, p1r, p1i = [], [], [], [], [], []
        for source, first, second in ((real, p0r, p2r), (imag, p0i, p2i), (mixed, p1r, p1i)):
            for t in range(2):
                a, b = merge(source[2 * t], source[2 * t + 1], low_half)
                first.append(a)
                second.append(b)
        lines = jnp.concatenate(
            [jnp.concatenate(x, axis=1) for x in (p0r, p1r, p2r, p0i, p1i, p2i)], axis=0
        )
        high, low = parts_of(lines)
        cos, sin = (
            dot3(high, low, high_ref[r, :, at : at + ZS], low_ref[r, :, at : at + ZS], ((1,), (1,)))
            for at in (0, ZS)
        )
        w_ref[r, : 3 * rows, :ZS] = cos[: 3 * rows] + sin[3 * rows :]
        w_ref[r, : 3 * rows, ZS:] = cos[3 * rows :] - sin[: 3 * rows]
        return carry
    lax.fori_loop(0, ZR, group, 0, unroll=UNROLL_FWD)

    def body(i, carry):
        at = pl.multiple_of(i * UNIT, UNIT)
        along = unit_of(row // UNIT + i) * UNIT + lax.broadcasted_iota(jnp.int32, (UNIT, 128), 0)
        along = jnp.where(2 * along < NX, along, along - NX)
        wave_along = along.astype(jnp.float32) * (TWO_PI / NX)
        keep_along = 3 * jnp.abs(along) < NX
        for lane in range(0, ZS, 128):
            spectra = []
            for j in range(3):
                values = [
                    tuple(
                        w_ref[r, pl.ds(j * rows + at, UNIT), pl.ds(p * ZS + lane, 128)]
                        for p in range(2)
                    )
                    for r in range(ZR)
                ]
                spectra.append(small_dft(values, -1))
            for half, groups in enumerate((LOW, HIGH)):
                for place, a in enumerate(groups):
                    start = a * ZS + lane - (NZ if half else 0)
                    mode = start + lax.broadcasted_iota(jnp.int32, (UNIT, 128), 1)
                    wave_across = mode.astype(jnp.float32) * (TWO_PI / NZ)
                    keep = jnp.logical_and(3 * jnp.abs(mode) < NZ, keep_along)
                    (ar, ai), (br, bi), (cr, ci) = (x[a] for x in spectra)
                    terms = [
                        jnp.where(keep, wave_along * ai + wave_across * bi, 0.0),
                        jnp.where(keep, -(wave_along * ar + wave_across * br), 0.0),
                        jnp.where(keep, wave_along * bi + wave_across * ci, 0.0),
                        jnp.where(keep, -(wave_along * br + wave_across * cr), 0.0),
                    ]
                    for x in range(4):
                        out_ref[half, x, pl.ds(row + at, UNIT), pl.ds(place * ZS + lane, 128)] = terms[x]
        return carry
    lax.fori_loop(0, rows // UNIT, body, 0)


def substep_kernel(
    velocity_ref, tables_hbm, fh_hbm, fl_hbm,
    term_ref,
    rows_ref, zh_ref, zl_ref, ih_ref, il_ref, fh_ref, fl_ref,
    zth_ref, ztl_ref, out_ref, in_ref, th_ref, tl_ref, f_ref, back_ref, work_ref, w_ref,
    table_sems, own_sems, swap_send, swap_recv, out_send, out_recv, back_send, back_recv,
    res_send, res_recv,
):
    gx, gz = lax.axis_index("gx"), lax.axis_index("gz")
    count = 2 * XR
    me = 2 * gx + gz
    half = rows_ref.shape[2]
    offsets = [sum(CHUNKS[:c]) for c in range(len(CHUNKS))]

    def device(t):
        return (t // 2, lax.rem(t, 2))

    tables = [
        pltpu.make_async_copy(src, dst, table_sems.at[n])
        for n, (src, dst) in enumerate(
            (
                (tables_hbm.at[pl.ds(0, ZR)], zh_ref),
                (tables_hbm.at[pl.ds(ZR, ZR)], zl_ref),
                (tables_hbm.at[pl.ds(2 * ZR, XR)], ih_ref),
                (tables_hbm.at[pl.ds(2 * ZR + XR, XR)], il_ref),
                (fh_hbm, fh_ref),
                (fl_hbm, fl_ref),
            )
        )
    ]

    def load_own(c):
        return pltpu.make_async_copy(
            velocity_ref.at[:, pl.ds(pl.multiple_of(gz * half + offsets[c], 16), CHUNKS[c]), :],
            rows_ref.at[0, :, pl.ds(offsets[c], CHUNKS[c]), :],
            own_sems.at[c],
        )

    def swap(c):
        return pltpu.make_async_remote_copy(
            src_ref=velocity_ref.at[
                :, pl.ds(pl.multiple_of((1 - gz) * half + offsets[c], 16), CHUNKS[c]), :
            ],
            dst_ref=rows_ref.at[1, :, pl.ds(offsets[c], CHUNKS[c]), :],
            send_sem=swap_send.at[c],
            recv_sem=swap_recv.at[c],
            device_id=(gx, 1 - gz),
            device_id_type=pl.DeviceIdType.MESH,
        )

    for c in range(len(CHUNKS)):
        load_own(c).start()
    for table in tables[:2]:
        table.start()

    barrier = pltpu.get_barrier_semaphore()

    def greet(i, carry):
        pl.semaphore_signal(
            barrier,
            inc=1,
            device_id=device(lax.rem(me + i, count)),
            device_id_type=pl.DeviceIdType.MESH,
        )
        return carry

    lax.fori_loop(1, count, greet, 0)
    pl.semaphore_wait(barrier, count - 1)
    for c in range(len(CHUNKS)):
        swap(c).start()
    for table in tables[2:]:
        table.start()

    def target(i, c):
        return lax.rem(me + jnp.where(me < XR, i, 2 * XR - i), count)

    def ship(src_ref, dst_ref, sends, recvs, c, at, length):
        span = pl.ds(at, length)

        def copy(i):
            t = target(i, c)
            return pltpu.make_async_remote_copy(
                src_ref=src_ref.at[t, :, span, :],
                dst_ref=dst_ref.at[me, :, span, :],
                send_sem=sends.at[c, i],
                recv_sem=recvs.at[c, me],
                device_id=device(t),
                device_id_type=pl.DeviceIdType.MESH,
            )

        def local():
            return pltpu.make_async_copy(
                src_ref.at[me, :, span, :], dst_ref.at[me, :, span, :], recvs.at[c, me]
            )

        return copy, local

    def takes(t, src_ref, dst_ref, sends, recvs, c, at, length):
        if dst_ref is not work_ref or at < SHORT * UNIT:
            return t >= 0
        g = t // 2
        return jnp.logical_and(g != 5, g != XR - 6)

    def goes(t, *args):
        return jnp.logical_and(t != me, takes(t, *args))

    def ship_start(*args):
        copy, local = ship(*args)

        def start(i, carry):
            @pl.when(goes(target(i, args[4]), *args))
            def _():
                copy(i).start()
            return carry

        lax.fori_loop(0, count, start, 0)

        @pl.when(takes(me, *args))
        def _():
            local().start()

    def ship_arrive(src_ref, dst_ref, sends, recvs, c, at, length):
        span = pl.ds(at, length)
        _, local = ship(src_ref, dst_ref, sends, recvs, c, at, length)

        def wait(i, carry):
            t = lax.rem(me + i, count)
            pltpu.make_async_copy(
                src_ref.at[t, :, span, :], dst_ref.at[t, :, span, :], recvs.at[c, t]
            ).wait()
            return carry

        lax.fori_loop(1, count, wait, 0)
        local().wait()

    def ship_leave(*args):
        copy, _ = ship(*args)

        def wait(i, carry):
            @pl.when(goes(target(i, args[4]), *args))
            def _():
                copy(i).wait_send()
            return carry

        lax.fori_loop(0, count, wait, 0)

    def spread_args(c):
        return out_ref, in_ref, out_send, out_recv, c, offsets[c], CHUNKS[c]

    tables[0].wait()
    tables[1].wait()
    for c in range(len(CHUNKS)):
        load_own(c).wait()
        swap(c).wait_recv()
        z_inverse(
            gz == 0, rows_ref, offsets[c], CHUNKS[c],
            zh_ref, zl_ref, out_ref, zth_ref, ztl_ref,
        )
        ship_start(*spread_args(c))

    for c in range(len(CHUNKS)):
        ship_arrive(*spread_args(c))
        x_spread(in_ref, offsets[c], CHUNKS[c], th_ref, tl_ref)
        if c == len(CHUNKS) - 2:
            for table in tables[2:]:
                table.wait()
            x_early(4 * offsets[-1], ih_ref, il_ref, th_ref, tl_ref, f_ref)
    for c in range(len(CHUNKS)):
        ship_leave(*spread_args(c))
    x_products(
        4 * offsets[-1], ih_ref, il_ref, fh_ref, fl_ref, th_ref, tl_ref, f_ref, (out_ref, in_ref)
    )
    x_gather((out_ref, in_ref), back_ref)

    starts = [sum(SPANS[:c]) for c in range(len(SPANS))]

    def back_args(c):
        return back_ref, work_ref, back_send, back_recv, c, starts[c] * UNIT, SPANS[c] * UNIT

    for c in range(BACK_AHEAD):
        ship_start(*back_args(c))

    def result(u, side):
        unit = unit_at(gx, gz, u)
        owner = unit // PER
        slot = unit - owner * PER
        src = rows_ref.at[
            side, :, pl.ds(pl.multiple_of(u * UNIT, UNIT), UNIT), pl.ds(0, term_ref.shape[2])
        ]
        dst = term_ref.at[:, pl.ds(pl.multiple_of(slot * UNIT, UNIT), UNIT), :]
        here = jnp.logical_and(owner == gx, side == gz)

        def remote():
            return pltpu.make_async_remote_copy(
                src_ref=src,
                dst_ref=dst,
                send_sem=res_send.at[side, u],
                recv_sem=res_recv.at[slot],
                device_id=(owner, side),
                device_id_type=pl.DeviceIdType.MESH,
            )

        return here, remote, lambda: pltpu.make_async_copy(src, dst, res_recv.at[slot])

    def forward(c):
        ship_arrive(*back_args(c))
        unit, units = starts[c], SPANS[c]
        z_forward(
            functools.partial(unit_at, gx, gz), unit * UNIT, units * UNIT,
            work_ref, zh_ref, zl_ref, rows_ref, w_ref,
        )

        def send(n, carry):
            for side in range(2):
                here, remote, local = result(unit + n, side)

                @pl.when(here)
                def _():
                    local().start()

                @pl.when(jnp.logical_not(here))
                def _():
                    remote().start()
            return carry

        lax.fori_loop(0, units, send, 0)

    for c in range(len(SPANS)):
        @pl.when(takes(me, *back_args(c)))
        def _():
            forward(c)

        if c + BACK_AHEAD < len(SPANS):
            ship_start(*back_args(c + BACK_AHEAD))

    def sent(u, carry):
        for side in range(2):
            here, remote, _ = result(u, side)

            @pl.when(jnp.logical_not(here))
            def _():
                remote().wait_send()
        return carry

    def got(s, carry):
        unit = gx * PER + s

        @pl.when(jnp.logical_or(unit < NEEDED, unit >= XR * PER - NEEDED))
        def _():
            pltpu.make_async_copy(
                rows_ref.at[0, :, pl.ds(0, UNIT), pl.ds(0, term_ref.shape[2])],
                term_ref.at[:, pl.ds(pl.multiple_of(s * UNIT, UNIT), UNIT), :],
                res_recv.at[s],
            ).wait()
        return carry

    lax.fori_loop(0, PER, got, 0)
    short = jnp.logical_or(gx == 5, gx == XR - 6)
    lax.fori_loop(0, jnp.where(short, SHORT, UNITS), sent, 0)

    for c in range(len(CHUNKS)):
        swap(c).wait_send()
    for c in range(len(SPANS)):
        ship_leave(*back_args(c))


def advance_kernel(
    base_ref, v_ref, old_ref, term_ref, next_hbm, non_hbm, next_ref, non_ref, store_sems
):
    mode_count, extent = v_ref.shape[2:]
    lower = lax.axis_index("gz") == 0
    across = lax.axis_index("gz") * extent + lax.broadcasted_iota(jnp.int32, (1, extent), 1)
    wave_across = jnp.where(2 * across < NZ, across, across - NZ).astype(jnp.float32) * (TWO_PI / NZ)
    empty = jnp.zeros((UNIT, extent - term_ref.shape[2]), jnp.float32)

    def at(c):
        return pl.ds(pl.multiple_of(c * BLOCK, BLOCK), BLOCK)

    def stores(c):
        return (
            pltpu.make_async_copy(
                next_ref.at[:, :, at(c), :], next_hbm.at[:, :, at(c), :], store_sems.at[0, c]
            ),
            pltpu.make_async_copy(
                non_ref.at[:, :, at(c), :], non_hbm.at[:, :, at(c), :], store_sems.at[1, c]
            ),
        )

    def work(c, carry):
        def lines(i, carry):
            row = pl.multiple_of(c * BLOCK + i * UNIT, UNIT)
            start = lax.axis_index("gx") * XS + row
            active = jnp.logical_or(start < NEEDED * UNIT, start >= NX - NEEDED * UNIT)
            along = start + lax.broadcasted_iota(jnp.int32, (UNIT, 1), 0)
            wave_along = jnp.where(2 * along < NX, along, along - NX).astype(jnp.float32) * (TWO_PI / NX)
            damping = jnp.exp(-VISCOSITY * (wave_along * wave_along + wave_across * wave_across))
            shear = base_ref[0] * wave_along
            to = pl.ds(row, UNIT)
            for f in range(2):
                for p in range(2):
                    term = jnp.where(active, term_ref[2 * f + p, to, :], 0.0)
                    term = jnp.where(
                        lower,
                        jnp.concatenate([term, empty], axis=1),
                        jnp.concatenate([empty, term], axis=1),
                    )
                    other = shear * v_ref[f, 1 - p, to, :]
                    result = term + other if p == 0 else term - other
                    non_ref[f, p, to, :] = result
                    next_ref[f, p, to, :] = damping * (
                        v_ref[f, p, to, :]
                        + TIME_STEP * (GAMMA_NEW * result + ZETA_OLD * old_ref[f, p, to, :])
                    )
            return carry

        lax.fori_loop(0, BLOCK // UNIT, lines, 0)
        for store in stores(c):
            store.start()
        return carry

    lax.fori_loop(0, mode_count // BLOCK, work, 0)

    def end(c, carry):
        for store in stores(c):
            store.wait()
        return carry

    lax.fori_loop(0, mode_count // BLOCK, end, 0)


def lines_local(velocity, previous, base_flow):
    velocity, previous = velocity[:, :, 0], previous[:, :, 0]
    mode_count, extent = velocity.shape[2:]
    half = mode_count // 2
    rows = max(CHUNKS)
    f32, bf16 = jnp.float32, jnp.bfloat16
    zh, zl = z_table()
    xh, xl = x_inverse_table()
    fh, fl = x_forward_table()
    active = len(LOW) * ZS
    count = 2 * XR
    dma = pltpu.SemaphoreType.DMA

    term = pl.pallas_call(
        substep_kernel,
        out_shape=jax.ShapeDtypeStruct((4, mode_count, active), f32),
        in_specs=[pl.BlockSpec(memory_space=pl.ANY)] * 4,
        out_specs=pl.BlockSpec(memory_space=pl.ANY),
        scratch_shapes=[
            pltpu.VMEM((2, 4, half, extent), f32),
            pltpu.VMEM(zh.shape, bf16),
            pltpu.VMEM(zl.shape, bf16),
            pltpu.VMEM(xh.shape, bf16),
            pltpu.VMEM(xl.shape, bf16),
            pltpu.VMEM(fh.shape, bf16),
            pltpu.VMEM(fl.shape, bf16),
            pltpu.VMEM((ZR, 4 * rows, ZS), bf16),
            pltpu.VMEM((ZR, 4 * rows, ZS), bf16),
            pltpu.VMEM((count, 2, half, 128), f32),
            pltpu.VMEM((count, 2, half, 128), f32),
            pltpu.VMEM((XR, 2 * XS, 128), bf16),
            pltpu.VMEM((XR, 2 * XS, 128), bf16),
            pltpu.VMEM((XR, XS, 128), f32),
            pltpu.VMEM((count, 3, UNITS * UNIT, 128), f32),
            pltpu.VMEM((count, 3, UNITS * UNIT, 128), f32),
            pltpu.VMEM((ZR, 3 * max(SPANS) * UNIT, 2 * ZS), f32),
            dma((6,)),
            dma((len(CHUNKS),)),
            dma((len(CHUNKS),)),
            dma((len(CHUNKS),)),
            dma((len(CHUNKS), count)),
            dma((len(CHUNKS), count)),
            dma((len(SPANS), count)),
            dma((len(SPANS), count)),
            dma((2, UNITS)),
            dma((PER,)),
        ],
        compiler_params=pltpu.CompilerParams(
            collective_id=1, has_side_effects=True, vmem_limit_bytes=int(SUB_VMEM * MIB)
        ),
        cost_estimate=pl.CostEstimate(
            flops=10**10, bytes_accessed=64 * velocity.size, transcendentals=0
        ),
        name="substep",
    )(velocity.reshape(4, mode_count, extent), np.concatenate([zh, zl, xh, xl]), fh, fl)

    field = pltpu.VMEM(velocity.shape, f32)
    blocks = mode_count // BLOCK
    advanced, nonlinear = pl.pallas_call(
        advance_kernel,
        out_shape=[jax.ShapeDtypeStruct(velocity.shape, f32)] * 2,
        in_specs=[pl.BlockSpec(memory_space=pltpu.SMEM)] + [pl.BlockSpec(memory_space=pltpu.VMEM)] * 3,
        out_specs=[pl.BlockSpec(memory_space=pl.ANY)] * 2,
        scratch_shapes=[
            field,
            field,
            dma((2, blocks)),
        ],
        compiler_params=pltpu.CompilerParams(vmem_limit_bytes=ADV_VMEM * MIB),
        name="advance",
    )(
        base_flow,
        velocity,
        previous,
        term,
    )
    return advanced[:, :, None], nonlinear[:, :, None]


def solution(mesh):
    in_specs = (P(None, None, None, "gx", "gz"), P(None, None, None, "gx", "gz"), P())
    out_specs = (P(None, None, None, "gx", "gz"), P(None, None, None, "gx", "gz"))
    fits = mesh.shape["gx"] == XR and mesh.shape["gz"] == 2
    work = lines_local if fits else local
    return jax.shard_map(work, mesh=mesh, in_specs=in_specs, out_specs=out_specs, check_vma=False)
```
